32 devices in a mesh: dp: 8 (over y, x, core), tensor: 4 (over z).
Axes of the slice: x: 2, y: 2, z: 4, core: 2. Of those that a mesh axis runs over, the one named last changes fastest.
Arguments:
- hidden: bfloat16 [16384, 1024], P(('dp', 'tensor')), may hold values from -6 to 6
- segments: int32 [8, 2048], P('dp'), may hold values from 0 to 15, never falling along the last dimension, each value on 1 to 1024 neighbouring positions
- cotangent: bfloat16 [16384, 1024], P(('dp', 'tensor')), may hold values from -6 to 6
- norm_gain: float32 [1024], replicated, may hold values from 0.5 to 1.5
- ffn_gain: float32 [1024], replicated, may hold values from 0.5 to 1.5
- query_proj: bfloat16 [1024, 512], P('dp', 'tensor'), may hold values from -0.1875 to 0.1875
- key_proj: bfloat16 [1024, 128], P('dp'), may hold values from -0.1875 to 0.1875
- value_proj: bfloat16 [1024, 128], P('dp'), may hold values from -0.1875 to 0.1875
- attn_out_proj: bfloat16 [512, 1024], P('tensor', 'dp'), may hold values from -1 to 1
- gate_inner: bfloat16 [1024, 1536], P('dp', 'tensor'), may hold values from -0.1875 to 0.1875
- input_inner: bfloat16 [1024, 1536], P('dp', 'tensor'), may hold values from -0.1875 to 0.1875
- state_proj: bfloat16 [1024, 256], P('dp'), may hold values from -0.1875 to 0.1875
- step_proj: bfloat16 [1024, 24], P('dp', 'tensor'), may hold values from -0.1875 to 0.1875
- mamba_out: bfloat16 [1536, 1024], P('tensor', 'dp'), may hold values from -0.15625 to 0.15625
- conv_weight: float32 [4, 1792], replicated, may hold values from -4 to 4
- conv_bias: float32 [1792], replicated, may hold values from -4 to 4
- decay_log: float32 [24], replicated, may hold values from -4 to 2.5
- skip_gain: float32 [24], replicated, may hold values from 0.5 to 1.5
- step_bias: float32 [24], replicated, may hold values from -5 to -1
- ffn_gate: bfloat16 [1024, 2048], P('dp', 'tensor'), may hold values from -0.1875 to 0.1875
- ffn_up: bfloat16 [1024, 2048], P('dp', 'tensor'), may hold values from -0.1875 to 0.1875
- ffn_down: bfloat16 [2048, 1024], P('tensor', 'dp'), may hold values from -0.125 to 0.125
Outputs:
- output: bfloat16 [16384, 1024], P(('dp', 'tensor'))
- hidden_grad: float32 [16384, 1024], P(('dp', 'tensor'))
- norm_gain_grad: float32 [1024], replicated
- ffn_gain_grad: float32 [1024], replicated
- query_proj_grad: float32 [1024, 512], P('dp', 'tensor')
- key_proj_grad: float32 [1024, 128], P(('dp', 'tensor'))
- value_proj_grad: float32 [1024, 128], P(('dp', 'tensor'))
- attn_out_proj_grad: float32 [512, 1024], P('tensor', 'dp')
- gate_inner_grad: float32 [1024, 1536], P('dp', 'tensor')
- input_inner_grad: float32 [1024, 1536], P('dp', 'tensor')
- state_proj_grad: float32 [1024, 256], P(('dp', 'tensor'))
- step_proj_grad: float32 [1024, 24], P('dp', 'tensor')
- mamba_out_grad: float32 [1536, 1024], P('tensor', 'dp')
- conv_weight_grad: float32 [4, 1792], replicated
- conv_bias_grad: float32 [1792], replicated
- decay_log_grad: float32 [24], replicated
- skip_gain_grad: float32 [24], replicated
- step_bias_grad: float32 [24], replicated
- ffn_gate_grad: float32 [1024, 2048], P('dp', 'tensor')
- ffn_up_grad: float32 [1024, 2048], P('dp', 'tensor')
- ffn_down_grad: float32 [2048, 1024], P('tensor', 'dp')
The draws below stay inside these ranges and needn't reach their ends.
Inputs may be any that keep to these rules, and one draw needn't show every extreme that they name: `segments`: in each row the numbers never fall; a document holds 1 to half of 2048 positions, and one holds exactly that many.
All inputs are finite; a program needn't handle non-finite values.
Results may differ from the reference program's by a relative error of at most 0.012.
Values may be sent and summed in bfloat16 or wider, within the bound.
No kernel may reach another device: no remote copies, remote signals or barrier semaphores. Data moves between devices by JAX's collectives and lax.ppermute only.
A program may use at most 256 MiB of HBM per device.

```python
import math
import jax
import jax.numpy as jnp
import numpy as np
from jax import lax

D = 1024
QH = 8
KVH = 2
HD = 64
MH = 24
MP = 64
NS = 128
KCONV = 4
FF = 2048
SEQ = 2048
SPAN = 128
BLOCK = 512
CHANNELS = 1792
TOKENS = 16384
N_DP = 8


def draw_decay_log(key, part):
    key = jax.random.fold_in(key, 11)
    slow_key = jax.random.fold_in(key, 1)
    return jax.random.uniform(slow_key, (MH,), jnp.float32, -4.0, 2.5)


def draw_step_bias(key, part):
    key = jax.random.fold_in(key, 23)
    return jax.random.uniform(key, (MH,), jnp.float32, -5.0, -1.0)


def block_scale(rng, dims, cuts, low, high):
    gain = 1.0
    for position, blocks in cuts:
        heights = jax.random.uniform(jax.random.fold_in(jax.random.fold_in(rng, 6), position), (blocks,), jnp.float32, low / len(cuts), high / len(cuts))
        gain = gain * jnp.repeat(jnp.exp(heights), dims[position] // blocks).reshape((-1,) + (1,) * (len(dims) - 1 - position))
    return gain


def profile(number_of, total, most, lean):
    loads = [(1 << 20) // math.isqrt(rank ** lean) + 1 for rank in range(2, number_of + 1)]
    rest, counts = total - most - (number_of - 1), [1] * (number_of - 1)
    while rest > 0:
        free = [i for i in range(number_of - 1) if counts[i] < most]
        whole, remaining = sum([loads[i] for i in free]), rest
        for i in free:
            more = min(most - counts[i], max(1, remaining * loads[i] // whole), rest)
            counts[i] = counts[i] + more
            rest = rest - more
    return np.array([most] + counts)


def ragged_sizes(rng, count, total, limit, skew):
    if count == 2:
        one = jax.random.randint(rng, (), max(1, total - limit), min(limit, total - 1) + 1)
        return jnp.stack([one, total - one])
    lengths = jnp.asarray(profile(count, total, limit, skew), jnp.int32)
    couples = (count - 1) // 2
    source_of, taker = lengths[1:1 + 2 * couples:2], lengths[2:2 + 2 * couples:2]
    slack = jnp.minimum(source_of - 1, limit - taker)
    passed = jax.random.randint(jax.random.fold_in(rng, 1), (couples,), 0, 1 << 20) % (slack + 1)
    lengths = lengths.at[1:1 + 2 * couples:2].set(source_of - passed).at[2:2 + 2 * couples:2].set(taker + passed)
    return lengths[jax.random.permutation(jax.random.fold_in(rng, 2), count)]


def gaussian(stream_key, extent, width, bound, cuts=(), kind=jnp.bfloat16):
    level = block_scale(stream_key, extent, cuts, -0.22, 0.18) if cuts else 1.0
    entries = jax.random.normal(stream_key, extent, jnp.float32) * width * level
    return jnp.minimum(jnp.maximum(entries, -bound), bound).astype(kind)


def setup_inputs(seed: int = 0) -> dict:
    keys = jax.random.split(jax.random.key(seed), 23)
    return {
        "hidden": gaussian(keys[0], (TOKENS, D), 1.0, 6.0, ((0, 32),)),
        "segments": jax.vmap(lambda own: jnp.searchsorted(jnp.cumsum(ragged_sizes(own, max(4, SEQ // 128), SEQ, SEQ // 2, 2)), jnp.arange(SEQ), side="right"))(jax.random.split(keys[1], N_DP)).reshape((N_DP, SEQ)).astype(jnp.int32),
        "cotangent": gaussian(keys[2], (TOKENS, D), 1.0, 6.0, ((0, 32),)),
        "norm_gain": jnp.clip(1.0 + 0.1 * jax.random.normal(keys[3], (D,), jnp.float32), 0.5, 1.5),
        "ffn_gain": jnp.clip(1.0 + 0.1 * jax.random.normal(keys[4], (D,), jnp.float32), 0.5, 1.5),
        "query_proj": gaussian(keys[5], (D, QH * HD), D ** -0.5, 0.1875, ((0, 8), (1, 4))),
        "key_proj": gaussian(keys[6], (D, KVH * HD), D ** -0.5, 0.1875, ((0, 8),)),
        "value_proj": gaussian(keys[7], (D, KVH * HD), D ** -0.5, 0.1875, ((0, 8),)),
        "attn_out_proj": gaussian(keys[8], (QH * HD, D), 32 ** -0.5, 1.0, ((0, 4), (1, 8))),
        "gate_inner": gaussian(keys[9], (D, MH * MP), D ** -0.5, 0.1875, ((0, 8), (1, 4))),
        "input_inner": gaussian(keys[10], (D, MH * MP), D ** -0.5, 0.1875, ((0, 8), (1, 4))),
        "state_proj": gaussian(keys[11], (D, 2 * NS), D ** -0.5, 0.1875, ((0, 8),)),
        "step_proj": gaussian(keys[12], (D, MH), D ** -0.5, 0.1875, ((0, 8), (1, 4))),
        "mamba_out": gaussian(keys[13], (MH * MP, D), (MH * MP) ** -0.5, 0.15625, ((0, 4), (1, 8))),
        "conv_weight": gaussian(keys[14], (KCONV, CHANNELS), 0.5, 4.0, (), jnp.float32),
        "conv_bias": gaussian(keys[15], (CHANNELS,), 0.5, 4.0, (), jnp.float32),
        "decay_log": draw_decay_log(jax.random.fold_in(keys[22], 71), 0),
        "skip_gain": jnp.clip(jax.random.uniform(keys[17], (MH,), jnp.float32, 0.5, 1.5), 0.5, 1.5),
        "step_bias": draw_step_bias(jax.random.fold_in(keys[22], 71), 0),
        "ffn_gate": gaussian(keys[19], (D, FF), D ** -0.5, 0.1875, ((0, 8), (1, 4))),
        "ffn_up": gaussian(keys[20], (D, FF), D ** -0.5, 0.1875, ((0, 8), (1, 4))),
        "ffn_down": gaussian(keys[21], (FF, D), FF ** -0.5, 0.125, ((0, 4), (1, 8))),
    }


epsilon = 1e-05
rope_base = 100000000000.0

@jax.custom_vjp
def low(v):
    return lax.optimization_barrier(v.astype(jnp.bfloat16)).astype(jnp.float32)

@jax.custom_vjp
def low_back(v):
    return v

def low_keep(v):
    return (low(v), None)

def low_pass(kept, grad):
    return (grad,)

def back_keep(v):
    return (v, None)

def back_low(kept, grad):
    return (low(grad),)
low.defvjp(low_keep, low_pass)
low_back.defvjp(back_keep, back_low)

def matmul(left, right):
    return jnp.dot(left, right, precision=lax.Precision.HIGHEST)

def rms_scale(values, gain_vec):
    return values * lax.rsqrt(lax.optimization_barrier(jnp.mean(values * values, axis=-1, keepdims=True)) + epsilon) * gain_vec

def rotary(values):
    length, head_count, head_size = values.shape
    half_size = head_size // 2
    frequency = rope_base ** (-2.0 * jnp.arange(half_size, dtype=jnp.float32) / head_size)
    angles = jnp.arange(length, dtype=jnp.float32)[:, None] * frequency[None, :]
    cosine = jnp.cos(angles)[:, None, :]
    sine_part = jnp.sin(angles)[:, None, :]
    first_half = values[..., :half_size]
    second_half = values[..., half_size:]
    return jnp.concatenate([first_half * cosine - second_half * sine_part, second_half * cosine + first_half * sine_part], axis=-1)

def attend(query, key_heads, values, segment):
    length, head_count, head_size = query.shape
    group_size = head_count // key_heads.shape[1]
    keys_all = jnp.repeat(key_heads, group_size, axis=1)
    values_all = jnp.repeat(values, group_size, axis=1)
    block_rows = min(BLOCK, length)
    block_count = length // block_rows
    begin_rows = (jnp.arange(block_count) * block_rows).astype(jnp.int32)
    columns = jnp.arange(length)

    def one_block(element):
        rows_query, begin_at = element
        row_segment = lax.dynamic_slice_in_dim(segment, begin_at, block_rows)
        row_position = begin_at + jnp.arange(block_rows)
        allowed = (row_segment[:, None] == segment[None, :]) & (row_position[:, None] >= columns[None, :])
        scores = jnp.einsum('qhd,khd->hqk', rows_query, keys_all, precision=lax.Precision.HIGHEST) * head_size ** (-0.5)
        scores = low_back(scores)
        scores = jnp.where(allowed[None], scores, -1e+30)
        attn_probs = low(jax.nn.softmax(scores, axis=-1))
        return jnp.einsum('hqk,khd->qhd', attn_probs, values_all, precision=lax.Precision.HIGHEST)
    result = lax.map(jax.checkpoint(one_block), (query.reshape(block_count, block_rows, head_count, head_size), begin_rows))
    return result.reshape(length, head_count, head_size)

def causal_conv(raw_input, kernel, conv_shift, segment):
    length = raw_input.shape[0]
    kernel_taps = kernel.shape[0]
    summed = conv_shift[None, :] + kernel[kernel_taps - 1][None, :] * raw_input
    for offset in range(1, kernel_taps):
        shifted = jnp.pad(raw_input, ((offset, 0), (0, 0)))[:length]
        seg_shift = jnp.pad(segment, (offset, 0), constant_values=-1)[:length]
        keep_mask = (seg_shift == segment).astype(jnp.float32)[:, None]
        summed = summed + kernel[kernel_taps - 1 - offset][None, :] * shifted * keep_mask
    return summed

def state_scan(x_heads, input_mat, output_mat, dt_step, log_decay, segment):
    length, head_count, head_size = x_heads.shape
    state_size = input_mat.shape[1]
    block_rows = min(SPAN, length)
    block_count = length // block_rows
    previous = jnp.concatenate([jnp.full((1,), -1, jnp.int32), segment[:-1].astype(jnp.int32)])
    elements = (x_heads.reshape(block_count, block_rows, head_count, head_size), input_mat.reshape(block_count, block_rows, state_size), output_mat.reshape(block_count, block_rows, state_size), dt_step.reshape(block_count, block_rows, head_count), log_decay.reshape(block_count, block_rows, head_count), segment.astype(jnp.int32).reshape(block_count, block_rows), previous.reshape(block_count, block_rows)[:, 0])
    positions = jnp.arange(block_rows)
    causal = positions[:, None] >= positions[None, :]

    def advance(carried, element):
        x_block, b_block, c_block, dt_block, decay_block, seg_block, before = element
        cumulative = jnp.cumsum(decay_block, axis=0)
        allowed = causal & (seg_block[:, None] == seg_block[None, :])
        log_gap = cumulative[:, None, :] - cumulative[None, :, :]
        decays = jnp.exp(jnp.where(allowed[:, :, None], log_gap, 0.0)) * allowed[:, :, None]
        affinity = jnp.dot(c_block, b_block.T, precision=lax.Precision.HIGHEST)
        mixing = affinity[:, :, None] * decays * dt_block[None, :, :]
        within = jnp.einsum('tsh,shp->thp', mixing, x_block, precision=lax.Precision.HIGHEST)
        carry_in = (seg_block == before).astype(jnp.float32)
        reached = jnp.einsum('tn,hnp->thp', c_block, carried, precision=lax.Precision.HIGHEST)
        carried_part = reached * (carry_in[:, None] * jnp.exp(cumulative))[:, :, None]
        last_seg = (seg_block == seg_block[-1]).astype(jnp.float32)
        final_weight = last_seg[:, None] * jnp.exp(cumulative[-1][None, :] - cumulative) * dt_block
        next_state = carried * (carry_in[-1] * jnp.exp(cumulative[-1]))[:, None, None] + jnp.einsum('sh,sn,shp->hnp', final_weight, b_block, x_block, precision=lax.Precision.HIGHEST)
        return (next_state, within + carried_part)
    initial = jnp.zeros((head_count, state_size, head_size), jnp.float32)
    final_state, outputs = lax.scan(jax.checkpoint(advance), initial, elements)
    return outputs.reshape(length, head_count, head_size)

def mixer_core(normed, query_proj, key_proj, value_proj, attn_out_proj, gate_inner, input_inner, state_proj, step_proj, mamba_out, conv_weight, conv_bias, decay_log, skip_gain, step_bias, segment):
    length = normed.shape[0]
    query = low_back(low(rotary(matmul(normed, query_proj).reshape(length, -1, HD))))
    key_heads = low(rotary(matmul(normed, key_proj).reshape(length, -1, HD)))
    values = low(matmul(normed, value_proj).reshape(length, -1, HD))
    attended = attend(query, key_heads, values, segment)
    attended = low_back(low(attended.reshape(length, -1)))
    head_count = decay_log.shape[0]
    inner_width = head_count * MP
    z_gate = low_back(matmul(normed, gate_inner))
    x_raw = low_back(matmul(normed, input_inner))
    bc_raw = matmul(normed, state_proj)
    dt_raw = low_back(matmul(normed, step_proj))
    mixed = jax.nn.silu(causal_conv(jnp.concatenate([x_raw, bc_raw], axis=1), conv_weight, conv_bias, segment))
    x_heads = low(mixed[:, :inner_width]).reshape(length, head_count, MP)
    input_mat = low(mixed[:, inner_width:inner_width + NS])
    output_mat = low(mixed[:, inner_width + NS:])
    dt_step = jax.nn.softplus(dt_raw + step_bias[None, :])
    log_decay = dt_step * (-jnp.exp(decay_log))[None, :]
    scanned = state_scan(x_heads, input_mat, output_mat, dt_step, log_decay, segment)
    full_y = scanned + skip_gain[None, :, None] * x_heads
    gated = low_back(low(full_y.reshape(length, inner_width) * jax.nn.silu(z_gate)))
    return matmul(attended, attn_out_proj) + matmul(gated, mamba_out)

def ffn_core(normed2, ffn_gate, ffn_up, ffn_down):
    gate_lin = low_back(matmul(normed2, ffn_gate))
    up_lin = low_back(matmul(normed2, ffn_up))
    activation = low_back(low(jax.nn.silu(gate_lin) * up_lin))
    return matmul(activation, ffn_down)

def layer(seq_row, segment, norm_gain, ffn_gain, query_proj, key_proj, value_proj, attn_out_proj, gate_inner, input_inner, state_proj, step_proj, mamba_out, conv_weight, conv_bias, decay_log, skip_gain, step_bias, ffn_gate, ffn_up, ffn_down):
    normed = low(rms_scale(seq_row, norm_gain))
    mixer = low_back(mixer_core(normed, query_proj, key_proj, value_proj, attn_out_proj, gate_inner, input_inner, state_proj, step_proj, mamba_out, conv_weight, conv_bias, decay_log, skip_gain, step_bias, segment))
    residual = seq_row + mixer
    normed2 = low(rms_scale(residual, ffn_gain))
    return residual + low_back(ffn_core(normed2, ffn_gate, ffn_up, ffn_down))

def reference(hidden, segments, cotangent, norm_gain, ffn_gain, query_proj, key_proj, value_proj, attn_out_proj, gate_inner, input_inner, state_proj, step_proj, mamba_out, conv_weight, conv_bias, decay_log, skip_gain, step_bias, ffn_gate, ffn_up, ffn_down):
    params = tuple((element.astype(jnp.float32) for element in (norm_gain, ffn_gain, query_proj, key_proj, value_proj, attn_out_proj, gate_inner, input_inner, state_proj, step_proj, mamba_out, conv_weight, conv_bias, decay_log, skip_gain, step_bias, ffn_gate, ffn_up, ffn_down)))
    seq_rows = hidden.astype(jnp.float32).reshape(N_DP, SEQ, D)
    cot_rows = cotangent.astype(jnp.float32).reshape(N_DP, SEQ, D)

    def per_sequence(totals, element):
        seq_row, segment, cot_row = element

        def apply_layer(row_in, *weights):
            return layer(row_in, segment, *weights)
        result, pullback = jax.vjp(apply_layer, seq_row, *params)
        gradients = pullback(cot_row)
        totals = tuple((summed + extra for summed, extra in zip(totals, gradients[1:])))
        return (totals, (result.astype(jnp.bfloat16), gradients[0]))
    initial = tuple((jnp.zeros_like(element) for element in params))
    totals, (outputs, row_grads) = lax.scan(per_sequence, initial, (seq_rows, segments, cot_rows))
    return (outputs.reshape(TOKENS, D), row_grads.reshape(TOKENS, D), totals[0], totals[1], totals[2], totals[3], totals[4], totals[5], totals[6], totals[7], totals[8], totals[9], totals[10], totals[11], totals[12], totals[13], totals[14], totals[15], totals[16], totals[17], totals[18])
```

```python
import functools

import jax
import jax.numpy as jnp
from jax import lax
from jax.experimental import pallas as pl
from jax.experimental.pallas import tpu as pltpu
from jax.sharding import PartitionSpec as P

QH = 8
KVH = 2
HD = 64
MH = 24
MP = 64
NS = 128
KCONV = 4
GROUP = QH // KVH
INNER = MH * MP
SPAN = 128
HALO = 16
QB = 128
KB = 256
NEG = -1e30

epsilon = 1e-05
rope_base = 100000000000.0
f32 = jnp.float32
bf16 = jnp.bfloat16

NN = (((1,), (0,)), ((), ()))
NT = (((1,), (1,)), ((), ()))
TN = (((0,), (0,)), ((), ()))


def dot(a, b, dims=NN):
    return lax.dot_general(a, b, dims, preferred_element_type=f32)


def split2(v, axis=1):
    hi = v.astype(bf16)
    lo = (v - hi.astype(f32)).astype(bf16)
    return jnp.concatenate([hi, lo], axis=axis)


def params(mb):
    return pltpu.CompilerParams(vmem_limit_bytes=mb * 1024 * 1024)


def sds(shape, dtype):
    return jax.ShapeDtypeStruct(shape, dtype)


def whole(shape):
    return pl.BlockSpec(shape, lambda *_: (0,) * len(shape))


def attn_keep(segk_ref, segq_ref, off, i, back):
    pos_k = lax.broadcasted_iota(jnp.int32, (KB, QB), 0) + off
    pos_q = lax.broadcasted_iota(jnp.int32, (KB, QB), 1) + (back + i * QB)
    same = segk_ref[pl.ds(off, KB), :] == segq_ref[:, i * QB : (i + 1) * QB]
    return same & (pos_k <= pos_q)


def head_columns(place_ref, base, pair):
    return pl.ds(pl.multiple_of(place_ref[base + pair] * (2 * HD), 2 * HD), 2 * HD)


def stack_heads(ref, i, columns):
    rows = slice(i * QB, (i + 1) * QB)
    heads = []
    for at in columns:
        pair = ref[rows, at]
        heads += [pair[:, :HD], pair[:, HD:]]
    return jnp.concatenate(heads, axis=0)


def attn_fwd_kernel(first_ref, q_ref, k_ref, vt_ref, segq_ref, segk_ref, o_ref, lse_ref):
    rows = q_ref.shape[0]
    back = k_ref.shape[1] - rows
    wide = GROUP * QB
    for i in range(rows // QB):
        last = (back + (i + 1) * QB + KB - 1) // KB
        for g in range(KVH):
            columns = [head_columns(first_ref, rows // QB, g * GROUP // 2 + n) for n in range(GROUP // 2)]
            queries = stack_heads(q_ref, i, columns)

            def body(j, carry):
                top, total, acc = carry
                off = pl.multiple_of(j * KB, KB)
                scores = dot(k_ref[g, pl.ds(off, KB), :], queries, NT)
                keep = attn_keep(segk_ref, segq_ref, off, i, back)
                keep = jnp.concatenate([keep] * GROUP, axis=1)
                scores = jnp.where(keep, scores, NEG)
                new_top = jnp.maximum(top, jnp.max(scores, axis=0, keepdims=True))
                scale = jnp.exp(top - new_top)
                probs = jnp.exp(scores - new_top)
                total = total * scale + jnp.sum(probs, axis=0, keepdims=True)
                vt = vt_ref[g * HD : (g + 1) * HD, pl.ds(off, KB)]
                acc = acc * scale + dot(vt, probs.astype(bf16))
                return new_top, total, acc

            start = (jnp.full((1, wide), NEG, f32), jnp.zeros((1, wide), f32), jnp.zeros((HD, wide), f32))
            top, total, acc = lax.fori_loop(first_ref[i], last, body, start)
            lse_ref[i * KVH + g : i * KVH + g + 1, :] = top + jnp.log(total)
            acc = acc / total
            for h in range(0, GROUP, 2):
                pair = jnp.concatenate(
                    [acc[:, h * QB : (h + 1) * QB], acc[:, (h + 1) * QB : (h + 2) * QB]], axis=0
                ).T
                o_ref[i * QB : (i + 1) * QB, columns[h // 2]] = pair.astype(bf16)


def attn_bwd_kernel(first_ref, q_ref, k_ref, v_ref, do_ref, o_ref, lse_ref, segq_ref, segk_ref,
                    dq_ref, dk_ref, dv_ref):
    rows = q_ref.shape[0]
    back = k_ref.shape[1] - rows
    wide = GROUP * QB
    dk_ref[...] = jnp.zeros_like(dk_ref)
    dv_ref[...] = jnp.zeros_like(dv_ref)
    for i in range(rows // QB):
        last = (back + (i + 1) * QB + KB - 1) // KB
        for g in range(KVH):
            columns = [head_columns(first_ref, rows // QB, g * GROUP // 2 + n) for n in range(GROUP // 2)]
            queries = stack_heads(q_ref, i, columns)
            grads = stack_heads(do_ref, i, columns)
            outs = stack_heads(o_ref, i, columns)
            prod = grads.astype(f32) * outs.astype(f32)
            ones = jnp.ones((8, 2 * HD), bf16)
            delta = dot(ones, split2(prod), NT)[0:1, :]
            lse = lse_ref[i * KVH + g : i * KVH + g + 1, :]

            def body(j, acc):
                off = pl.multiple_of(j * KB, KB)
                keys = k_ref[g, pl.ds(off, KB), :]
                vals = v_ref[g, pl.ds(off, KB), :]
                keep = attn_keep(segk_ref, segq_ref, off, i, back)
                keep = jnp.concatenate([keep] * GROUP, axis=1)
                scores = jnp.where(keep, dot(keys, queries, NT), NEG)
                probs = jnp.exp(scores - lse)
                dprobs = dot(vals, grads, NT)
                dscores = (probs * (dprobs - delta)).astype(bf16)
                dv_ref[g, pl.ds(off, KB), :] += dot(probs.astype(bf16), grads)
                dk_ref[g, pl.ds(off, KB), :] += dot(dscores, queries)
                return acc + dot(keys, dscores, TN)

            acc = lax.fori_loop(first_ref[i], last, body, jnp.zeros((HD, wide), f32))
            acc = acc * (HD ** -0.5)
            for h in range(0, GROUP, 2):
                pair = jnp.concatenate(
                    [acc[:, h * QB : (h + 1) * QB], acc[:, (h + 1) * QB : (h + 2) * QB]], axis=0
                ).T
                dq_ref[i * QB : (i + 1) * QB, columns[h // 2]] = pair.astype(bf16)


SMEM = pl.BlockSpec(memory_space=pltpu.SMEM)


def vmem_specs(n):
    return [pl.BlockSpec(memory_space=pltpu.VMEM)] * n


def attn_fwd(first, q, k, vt, segq, segk):
    rows = q.shape[0]
    return pl.pallas_call(
        attn_fwd_kernel,
        out_shape=(sds(q.shape, bf16), sds((rows // QB * KVH, GROUP * QB), f32)),
        in_specs=[SMEM] + vmem_specs(5),
        out_specs=tuple(vmem_specs(2)),
        compiler_params=params(40),
        cost_estimate=pl.CostEstimate(flops=4_000_000_000, bytes_accessed=4_000_000, transcendentals=4_000_000),
        name="attn_fwd",
    )(first, q, k, vt, segq, segk)


def attn_bwd(first, q, k, v, do, o, lse, segq, segk):
    return pl.pallas_call(
        attn_bwd_kernel,
        out_shape=(sds(q.shape, bf16), sds(k.shape, f32), sds(k.shape, f32)),
        in_specs=[SMEM] + vmem_specs(8),
        out_specs=tuple(vmem_specs(3)),
        compiler_params=params(40),
        cost_estimate=pl.CostEstimate(flops=10_000_000_000, bytes_accessed=8_000_000, transcendentals=4_000_000),
        name="attn_bwd",
    )(first, q, k, v, do, o, lse, segq, segk)


LANE = 128
COLS = (INNER + 2 * NS) // LANE


def expander():
    head = jnp.arange(LANE)[:, None]
    channel = jnp.arange(INNER)[None, :] // MP
    return (head == channel).astype(bf16)


def tri_masks():
    t = lax.broadcasted_iota(jnp.int32, (SPAN, SPAN), 0)
    s = lax.broadcasted_iota(jnp.int32, (SPAN, SPAN), 1)
    return t, s


def widen(v, spread2):
    return dot(split2(v), spread2)


def conv_block(u_ref, tap_ref, meta, base, col):
    lanes = slice(col * LANE, (col + 1) * LANE)
    window = u_ref[pl.ds(base + HALO - 8, SPAN + 8), lanes]
    taps = [window[8:, :]]
    for j in range(1, KCONV):
        taps.append(window[8 - j : 8 - j + SPAN, :] * meta[:, j : j + 1])
    total = tap_ref[KCONV : KCONV + 1, lanes] + tap_ref[KCONV - 1 : KCONV, lanes] * taps[0]
    for j in range(1, KCONV):
        total = total + tap_ref[KCONV - 1 - j : KCONV - j, lanes] * taps[j]
    return taps, total


def mamba_pre_kernel(u_ref, tap_ref, meta_ref, dtr_ref, head_ref, spread_ref,
                     mix_ref, dt_ref, cum_ref, cumt_ref, ec_ref, fw_ref, g_ref, fin_ref):
    c = pl.program_id(0)
    base = pl.multiple_of(c * SPAN, SPAN)

    @pl.when(c == 0)
    def _():
        fin_ref[...] = jnp.zeros_like(fin_ref)

    meta = meta_ref[...]
    for col in range(COLS):
        total = conv_block(u_ref, tap_ref, meta, base, col)[1]
        mix_ref[:, col * LANE : (col + 1) * LANE] = (total * jax.nn.sigmoid(total)).astype(bf16)
    raw = dtr_ref[...] + head_ref[0:1, :]
    dt = jnp.maximum(raw, 0.0) + jnp.log1p(jnp.exp(-jnp.abs(raw)))
    decay = dt * head_ref[1:2, :]
    t, s = tri_masks()
    lower = (t >= s).astype(f32)
    cum = lax.dot_general(lower, decay, NN, precision=lax.Precision.HIGHEST, preferred_element_type=f32)
    end = cum[SPAN - 1 : SPAN, :]
    ec = meta[:, 4:5] * jnp.exp(cum)
    fw = meta[:, 5:6] * jnp.exp(end - cum)
    gain = ec[SPAN - 1 : SPAN, :]
    dt_ref[...] = dt
    cum_ref[...] = cum
    cumt_ref[...] = cum.T[: cumt_ref.shape[0], :]
    ec_ref[...] = ec
    fw_ref[...] = fw
    gain8 = jnp.broadcast_to(gain, (8, LANE))
    g_ref[...] = gain8
    spread2 = spread_ref[...]
    weight = widen(fw * dt, spread2)
    x = mix_ref[:, :INNER].astype(f32)
    b = mix_ref[:, INNER : INNER + NS]
    state = fin_ref[...] * widen(gain8, spread2)[0:1, :]
    fin_ref[...] = state + dot(b, (x * weight).astype(bf16), TN)


def chunk_spec(width):
    return pl.BlockSpec((SPAN, width), lambda c: (c, 0))


def mamba_pre(u, taps, meta, dt_raw, heads, spread2):
    rows = meta.shape[0]
    n = rows // SPAN
    width = INNER + 2 * NS
    hl = 32
    return pl.pallas_call(
        mamba_pre_kernel,
        grid=(n,),
        in_specs=[whole(u.shape), whole(taps.shape), chunk_spec(8), chunk_spec(LANE), whole(heads.shape),
                  whole(spread2.shape)],
        out_specs=(chunk_spec(width), chunk_spec(LANE), chunk_spec(LANE), pl.BlockSpec((hl, SPAN), lambda c: (0, c)),
                   chunk_spec(LANE), chunk_spec(LANE), pl.BlockSpec((8, LANE), lambda c: (c, 0)), whole((NS, INNER))),
        out_shape=(sds((rows, width), bf16), sds((rows, LANE), f32), sds((rows, LANE), f32), sds((hl, rows), f32),
                   sds((rows, LANE), f32), sds((rows, LANE), f32), sds((8 * n, LANE), f32), sds((NS, INNER), f32)),
        compiler_params=params(40),
        cost_estimate=pl.CostEstimate(flops=1_000_000_000, bytes_accessed=9_000_000, transcendentals=2_000_000),
        name="mamba_pre",
    )(u, taps, meta, dt_raw, heads, spread2)


def pair_halves(v):
    lane = lax.broadcasted_iota(jnp.int32, v.shape, 1)
    zero = jnp.zeros_like(v)
    return jnp.concatenate([jnp.where(lane < MP, v, zero), jnp.where(lane < MP, zero, v)], axis=0)


def mamba_fwd_kernel(init_ref, mix_ref, dt_ref, cum_ref, cumt_ref, ec_ref, fw_ref, g_ref, segc_ref, segr_ref,
                     z_ref, skip_ref, spread_ref, gated_ref, full_ref, states_ref, state_ref):
    c = pl.program_id(0)

    @pl.when(c == 0)
    def _():
        state_ref[...] = init_ref[...]

    state = state_ref[...].astype(bf16)
    states_ref[0] = state
    spread2 = spread_ref[...]
    b = mix_ref[:, INNER : INNER + NS]
    cm = mix_ref[:, INNER + NS :]
    t, s = tri_masks()
    allowed = (segc_ref[...] == segr_ref[...]) & (t >= s)
    off = jnp.where(allowed, 0.0, NEG)
    affinity = dot(cm, b, NT)
    cum = cum_ref[...]
    dt = dt_ref[...]
    dt_wide = widen(dt, spread2)
    ec_wide = widen(ec_ref[...], spread2)
    carried = dot(cm, state) * ec_wide
    for p in range(MH // 2):
        lanes = slice(p * LANE, (p + 1) * LANE)
        x = mix_ref[:, lanes].astype(f32)
        pieces = []
        for h in (2 * p, 2 * p + 1):
            gap = cum[:, h : h + 1] - cumt_ref[h : h + 1, :] + off
            pieces.append((affinity * jnp.exp(gap)).astype(bf16))
        scaled = (x * dt_wide[:, lanes]).astype(bf16)
        y = dot(jnp.concatenate(pieces, axis=1), pair_halves(scaled)) + carried[:, lanes]
        y = y + skip_ref[0:1, lanes] * x
        z = z_ref[:, lanes]
        full_ref[:, lanes] = y.astype(bf16)
        gated_ref[:, lanes] = (y * (z * jax.nn.sigmoid(z))).astype(bf16)
    weight = widen(fw_ref[...] * dt, spread2)
    x = mix_ref[:, :INNER].astype(f32)
    gain = widen(g_ref[...], spread2)[0:1, :]
    state_ref[...] = state_ref[...] * gain + dot(b, (x * weight).astype(bf16), TN)


def mamba_fwd(init, mix, dt, cum, cumt, ec, fw, g, segc, segr, z, skip, spread2):
    rows = mix.shape[0]
    n = rows // SPAN
    return pl.pallas_call(
        mamba_fwd_kernel,
        grid=(n,),
        in_specs=[whole(init.shape), chunk_spec(mix.shape[1]), chunk_spec(LANE), chunk_spec(LANE),
                  pl.BlockSpec((cumt.shape[0], SPAN), lambda c: (0, c)), chunk_spec(LANE), chunk_spec(LANE),
                  pl.BlockSpec((8, LANE), lambda c: (c, 0)), chunk_spec(1), pl.BlockSpec((1, SPAN), lambda c: (0, c)),
                  chunk_spec(INNER), whole(skip.shape), whole(spread2.shape)],
        out_specs=(chunk_spec(INNER), chunk_spec(INNER), pl.BlockSpec((1, NS, INNER), lambda c: (c, 0, 0))),
        out_shape=(sds((rows, INNER), bf16), sds((rows, INNER), bf16), sds((n, NS, INNER), bf16)),
        scratch_shapes=[pltpu.VMEM((NS, INNER), f32)],
        compiler_params=params(40),
        cost_estimate=pl.CostEstimate(flops=3_000_000_000, bytes_accessed=12_000_000, transcendentals=3_000_000),
        name="mamba_fwd",
    )(init, mix, dt, cum, cumt, ec, fw, g, segc, segr, z, skip, spread2)


def mamba_bpre_kernel(dg_ref, z_ref, full_ref, cm_ref, ec_ref, g_ref, spread_ref, dy_ref, dz_ref, back_ref):
    c = pl.program_id(0)

    @pl.when(c == 0)
    def _():
        back_ref[...] = jnp.zeros_like(back_ref)

    spread2 = spread_ref[...]
    z = z_ref[...]
    sig = jax.nn.sigmoid(z)
    dg = dg_ref[...].astype(f32)
    dy = dg * (z * sig)
    dy_ref[...] = dy.astype(bf16)
    dz_ref[...] = (dg * full_ref[...].astype(f32) * (sig * (1.0 + z * (1.0 - sig)))).astype(bf16)
    weighted = (dy * widen(ec_ref[...], spread2)).astype(bf16)
    gain = widen(g_ref[...], spread2)[0:1, :]
    back_ref[...] = back_ref[...] * gain + dot(cm_ref[...], weighted, TN)


def mamba_bpre(dg, z, full, mix, ec, g, spread2):
    rows = dg.shape[0]
    n = rows // SPAN
    rev = lambda width, col=0: pl.BlockSpec((SPAN, width), lambda c: (n - 1 - c, col))
    return pl.pallas_call(
        mamba_bpre_kernel,
        grid=(n,),
        in_specs=[rev(INNER), rev(INNER), rev(INNER), rev(NS, (INNER + NS) // NS), rev(LANE),
                  pl.BlockSpec((8, LANE), lambda c: (n - 1 - c, 0)), whole(spread2.shape)],
        out_specs=(rev(INNER), rev(INNER), whole((NS, INNER))),
        out_shape=(sds((rows, INNER), bf16), sds((rows, INNER), bf16), sds((NS, INNER), f32)),
        compiler_params=params(40),
        cost_estimate=pl.CostEstimate(flops=500_000_000, bytes_accessed=11_000_000, transcendentals=1_000_000),
        name="mamba_bpre",
    )(dg, z, full, mix, ec, g, spread2)


def mamba_bwd_kernel(init_ref, mix_ref, dt_ref, cum_ref, cumt_ref, ec_ref, fw_ref, g_ref, segc_ref, segr_ref,
                     dy_ref, states_ref, u_ref, tap_ref, meta_ref, skip_ref, head_ref, spread_ref, gather_ref,
                     dpre_ref, ddt_ref, conv_ref, small_ref, dstate_ref, acc_ref, rows_ref, dx_ref, dbc_ref):
    step = pl.program_id(0)
    c = pl.num_programs(0) - 1 - step
    base = pl.multiple_of(c * SPAN, SPAN)

    @pl.when(step == 0)
    def _():
        dstate_ref[...] = init_ref[...]
        conv_ref[...] = jnp.zeros_like(conv_ref)
        small_ref[...] = jnp.zeros_like(small_ref)
        rows_ref[...] = jnp.zeros_like(rows_ref)

    spread2 = spread_ref[...]
    gather2 = gather_ref[...]
    b = mix_ref[:, INNER : INNER + NS]
    cm = mix_ref[:, INNER + NS :]
    cum = cum_ref[...]
    dt = dt_ref[...]
    dt_wide = widen(dt, spread2)
    s, t = tri_masks()
    allowed = (segc_ref[...] == segr_ref[...]) & (t >= s)
    off = jnp.where(allowed, 0.0, NEG)
    affinity = dot(b, cm, NT)
    acc_ref[...] = jnp.zeros_like(acc_ref)
    for p in range(MH // 2):
        lanes = slice(p * LANE, (p + 1) * LANE)
        x = mix_ref[:, lanes].astype(f32)
        scaled = (x * dt_wide[:, lanes]).astype(bf16)
        dy = dy_ref[:, lanes]
        dmix = dot(pair_halves(scaled), dy, NT)
        pieces = []
        total = None
        for q, h in enumerate((2 * p, 2 * p + 1)):
            gap = cumt_ref[h : h + 1, :] - cum[:, h : h + 1] + off
            decays = jnp.exp(gap)
            mixing = (affinity * decays).astype(bf16)
            pieces.append(mixing)
            dm = dmix[q * SPAN : (q + 1) * SPAN, :]
            rows_ref[h : h + 1, :] = jnp.sum(dm * mixing.astype(f32), axis=0, keepdims=True)
            part = dm * decays
            total = part if total is None else total + part
        acc_ref[...] += total
        dx_ref[:, lanes] = dot(jnp.concatenate(pieces, axis=1), pair_halves(dy))
    dscaled = dx_ref[...]
    x = mix_ref[:, :INNER].astype(f32)
    scaled = (x * dt_wide).astype(bf16).astype(f32)
    dy = dy_ref[...].astype(f32)
    dstate = dstate_ref[...]
    dstate_low = dstate.astype(bf16)
    state = states_ref[0]
    ec_wide = widen(ec_ref[...], spread2)
    fw_wide = widen(fw_ref[...], spread2)
    from_state = fw_wide * dot(b, dstate_low)
    carried = ec_wide * dot(cm, state)
    weighted_dy = (dy * ec_wide).astype(bf16)
    cols_sum = dot(split2(scaled * dscaled), gather2)
    carr_sum = dot(split2(dy * carried), gather2)
    fdf_sum = dot(split2(scaled * from_state), gather2)
    dxd = dscaled + from_state
    ddt_direct = dot(split2(x * dxd), gather2)
    skip_part = dot(split2(dy * x), gather2)
    gain = widen(g_ref[...], spread2)[0:1, :]
    state_dot = jnp.sum(dstate * state.astype(f32), axis=0, keepdims=True) * gain
    state_dot = dot(split2(jnp.broadcast_to(state_dot, (8, INNER))), gather2)[0:1, :]
    tt, ss = tri_masks()
    suffix = (ss >= tt).astype(bf16)
    prefix = (ss < tt).astype(bf16)
    suffix2 = jnp.concatenate([suffix, suffix], axis=1)
    dlog = dot(suffix2, split2(carr_sum - cols_sum, axis=0))
    dlog = dlog + dot(suffix2, split2(rows_ref[...]), NT)
    dlog = dlog + dot(jnp.concatenate([prefix, prefix], axis=1), split2(fdf_sum, axis=0)) + state_dot
    decay_rate = head_ref[1:2, :]
    ddt = (ddt_direct + dlog * decay_rate) * (1.0 - jnp.exp(-dt))
    ddt_ref[...] = ddt.astype(bf16)
    small_ref[0:1, :] += jnp.sum(dlog * dt, axis=0, keepdims=True) * decay_rate
    small_ref[1:2, :] += jnp.sum(skip_part, axis=0, keepdims=True)
    small_ref[2:3, :] += jnp.sum(ddt, axis=0, keepdims=True)
    dx_ref[...] = dxd * dt_wide + skip_ref[0:1, :] * dy
    daff = acc_ref[...]
    daff_low = daff.astype(bf16)
    fx = (scaled * fw_wide).astype(bf16)
    dbc_ref[:, :NS] = dot(daff_low, cm) + dot(fx, dstate_low, NT)
    dbc_ref[:, NS:] = dot(daff_low, b, TN) + dot(weighted_dy, state, NT)
    dstate_ref[...] = dstate * gain + dot(cm, weighted_dy, TN)
    meta = meta_ref[...]
    for col in range(COLS):
        lanes = slice(col * LANE, (col + 1) * LANE)
        taps, total = conv_block(u_ref, tap_ref, meta, base, col)
        sig = jax.nn.sigmoid(total)
        if col * LANE < INNER:
            dmixed = dx_ref[:, lanes]
        else:
            dmixed = dbc_ref[:, col * LANE - INNER : (col + 1) * LANE - INNER]
        dpre = dmixed * (sig * (1.0 + total * (1.0 - sig)))
        dpre_ref[:, lanes] = dpre
        for j in range(KCONV):
            conv_ref[KCONV - 1 - j : KCONV - j, lanes] += jnp.sum(dpre * taps[j], axis=0, keepdims=True)
        conv_ref[KCONV : KCONV + 1, lanes] += jnp.sum(dpre, axis=0, keepdims=True)


def mamba_bwd(init, mix, dt, cum, cumt, ec, fw, g, segc, segr, dy, states, u, taps, meta, skip, heads, spread2, gather2):
    rows = mix.shape[0]
    n = rows // SPAN
    width = mix.shape[1]
    rev = lambda w: pl.BlockSpec((SPAN, w), lambda c: (n - 1 - c, 0))
    return pl.pallas_call(
        mamba_bwd_kernel,
        grid=(n,),
        in_specs=[whole(init.shape), rev(width), rev(LANE), rev(LANE),
                  pl.BlockSpec((cumt.shape[0], SPAN), lambda c: (0, n - 1 - c)), rev(LANE), rev(LANE),
                  pl.BlockSpec((8, LANE), lambda c: (n - 1 - c, 0)), rev(1),
                  pl.BlockSpec((1, SPAN), lambda c: (0, n - 1 - c)), rev(INNER),
                  pl.BlockSpec((1, NS, INNER), lambda c: (n - 1 - c, 0, 0)), whole(u.shape), whole(taps.shape),
                  rev(8), whole(skip.shape), whole(heads.shape), whole(spread2.shape), whole(gather2.shape)],
        out_specs=(rev(width), rev(LANE), whole((8, width)), whole((8, LANE))),
        out_shape=(sds((rows, width), f32), sds((rows, LANE), bf16), sds((8, width), f32), sds((8, LANE), f32)),
        scratch_shapes=[pltpu.VMEM((NS, INNER), f32), pltpu.VMEM((SPAN, SPAN), f32), pltpu.VMEM((LANE, SPAN), f32),
                        pltpu.VMEM((SPAN, INNER), f32), pltpu.VMEM((SPAN, 2 * NS), f32)],
        compiler_params=params(56),
        cost_estimate=pl.CostEstimate(flops=6_000_000_000, bytes_accessed=16_000_000, transcendentals=4_000_000),
        name="mamba_bwd",
    )(init, mix, dt, cum, cumt, ec, fw, g, segc, segr, dy, states, u, taps, meta, skip, heads, spread2, gather2)


class Ring:
    def __init__(self, mesh):
        self.nd = mesh.shape["dp"]
        self.nt = mesh.shape["tensor"]
        k = self.nd.bit_length() - 1
        self.bits = [1 << i for i in range(k)]
        self.masks = [0]
        for bit in self.bits[:0:-1] if k else []:
            pass
        order = [1] + [1 << i for i in range(k - 1, 0, -1)] if k else []
        self.order = order
        masks = [0]
        for bit in reversed(order):
            masks = masks + [m ^ bit for m in masks]
        self.masks = masks

    def dp(self, value, bit):
        return lax.ppermute(value, "dp", [(i, i ^ bit) for i in range(self.nd)])

    def shift(self, value, s):
        n = self.nt
        return lax.ppermute(value, "tensor", [(i, (i + s) % n) for i in range(n)])

    def line(self, value, s):
        n = self.nt
        return lax.ppermute(value, "tensor", [(i, i + s) for i in range(n) if 0 <= i + s < n])

    def gather_dp(self, value):
        rows, cols = value.shape
        if self.nd == 1:
            return value
        near, last = self.order[1:], self.order[0]
        half = cols // 2
        sides = []
        for piece, order in ((value[:, :half], near[::-1]), (value[:, half:], near)):
            held, masks = piece, [0]
            for bit in order:
                held = jnp.concatenate([held, self.dp(held, bit)], axis=0)
                masks = masks + [m ^ bit for m in masks]
            sides.append([held[masks.index(m) * rows : (masks.index(m) + 1) * rows] for m in self.masks[: self.nd // 2]])
        low = jnp.concatenate([jnp.concatenate(side, axis=0) for side in sides], axis=1)
        return jnp.concatenate([low, self.dp(low, last)], axis=0)

    def gather_tensor(self, value):
        return [value] + [self.shift(value, s) for s in range(1, self.nt)]

    def scatter_dp(self, make, cols):
        total = self.nd
        last, near = self.order[0], self.order[1:]
        upper = make(1, 2)
        got = self.dp(upper, last)
        kept = (make(0, 2).astype(f32) + got.astype(f32)).astype(bf16)
        rows = kept.shape[0] // (total // 2)
        half = cols // 2
        blocks = total // 2
        outs = []
        for piece, order in ((kept[:, :half], near), (kept[:, half:], near[::-1])):
            held = [piece[i * rows : (i + 1) * rows] for i in range(blocks)]
            masks = list(self.masks[:blocks])
            for bit in order:
                mine = [i for i, m in enumerate(masks) if not m & bit]
                theirs = [i for i, m in enumerate(masks) if m & bit]
                sent = jnp.concatenate([held[i] for i in theirs], axis=0)
                came = self.dp(sent, bit)
                held = [
                    (held[i].astype(f32) + came[n * rows : (n + 1) * rows].astype(f32)).astype(bf16)
                    for n, i in enumerate(mine)
                ]
                masks = [masks[i] for i in mine]
            outs.append(held[0])
        return jnp.concatenate(outs, axis=1)

    def scatter_tensor(self, parts):
        total = parts[0].astype(f32)
        for s in range(1, self.nt):
            total = total + self.shift(parts[s], self.nt - s).astype(f32)
        return total

    def line_heads(self, value, s):
        return jnp.roll(self.line(value, s), s * (value.shape[1] // self.nt), axis=1)

    def all_sum(self, value):
        for bit in self.bits:
            value = value + self.dp(value, bit)
        return value + sum(self.shift(value, s) for s in range(1, self.nt))


def rms_back(d_normed, values, scale, gain):
    weighted = d_normed * gain
    inner = jnp.mean(weighted * values, axis=-1, keepdims=True)
    gain_grad = jnp.sum(d_normed * values * scale, axis=0)
    return scale * weighted - values * (scale * scale * scale * inner), gain_grad


def rope_tables(rows, start):
    half = HD // 2
    frequency = rope_base ** (-2.0 * jnp.arange(half, dtype=f32) / HD)
    angles = (start + jnp.arange(rows)).astype(f32)[:, None] * frequency[None, :]
    return jnp.cos(angles)[:, None, :], jnp.sin(angles)[:, None, :]


def rotate(values, cosine, sine):
    heads = values.reshape(values.shape[0], -1, HD)
    a, b = heads[..., : HD // 2], heads[..., HD // 2 :]
    return jnp.concatenate([a * cosine - b * sine, b * cosine + a * sine], axis=-1).reshape(values.shape)


def per_device(
    mesh,
    hidden,
    segments,
    cotangent,
    norm_gain,
    ffn_gain,
    query_proj,
    key_proj,
    value_proj,
    attn_out_proj,
    gate_inner,
    input_inner,
    state_proj,
    step_proj,
    mamba_out,
    conv_weight,
    conv_bias,
    decay_log,
    skip_gain,
    step_bias,
    ffn_gate,
    ffn_up,
    ffn_down,
):
    ring = Ring(mesh)
    nd, nt = ring.nd, ring.nt
    di, ti = lax.axis_index("dp"), lax.axis_index("tensor")
    rows, width = hidden.shape
    block = width // nd
    seq = segments.shape[1]
    hops = -(-(seq // 2 - 1) // rows)
    back = hops * rows
    segment = segments[0]

    def permute_width(values, forward=True):
        axis = values.ndim - 1
        pieces = []
        for r in range(nd):
            if forward:
                at = di ^ ring.masks[r]
            else:
                index = jnp.asarray([ring.masks.index(m) for m in range(nd)])
                at = index[di ^ r]
            pieces.append(lax.dynamic_slice_in_dim(values, at * block, block, axis))
        return jnp.concatenate(pieces, axis=axis)

    def relative(values, axis):
        step = values.shape[axis] // nt
        pieces = [
            lax.dynamic_slice_in_dim(values, lax.rem(ti + nt - s, nt) * step, step, axis) for s in range(nt)
        ]
        return jnp.concatenate(pieces, axis=axis)

    step_cols = step_proj.shape[1]
    step_pad = jnp.pad(step_proj, ((0, 0), (0, LANE - step_cols)))

    def gather(packs, widths):
        parts = ring.gather_tensor(packs)
        pieces = []
        at = 0
        for w in widths:
            pieces += [part[:, at : at + w] for part in parts]
            at += w
        full = ring.gather_dp(jnp.concatenate(pieces, axis=1))
        outs, at = [], 0
        for w in widths:
            outs.append(full[:, at : at + w * nt])
            at += w * nt
        return outs

    w_shared = ring.gather_dp(jnp.concatenate([key_proj, value_proj, state_proj], axis=1))
    w_q, w_step4, w_x = gather(
        jnp.concatenate([query_proj, step_pad, input_inner], axis=1),
        (query_proj.shape[1], LANE, input_inner.shape[1]),
    )
    w_z, w_ao, w_mo = gather(
        jnp.concatenate([gate_inner, attn_out_proj.T, mamba_out.T], axis=1),
        (gate_inner.shape[1], attn_out_proj.shape[0], mamba_out.shape[0]),
    )
    w_fg, w_fu = gather(jnp.concatenate([ffn_gate, ffn_up], axis=1), (ffn_gate.shape[1], ffn_up.shape[1]))
    (w_fd,) = gather(ffn_down.T, (ffn_down.shape[0],))
    w_step = jnp.concatenate([w_step4[:, s * LANE : s * LANE + step_cols] for s in range(nt)], axis=1)
    w_step = jnp.pad(w_step, ((0, 0), (0, LANE - MH)))
    w_kv, w_bc = w_shared[:, : 2 * KVH * HD], w_shared[:, 2 * KVH * HD :]

    hid = permute_width(hidden).astype(f32)
    cot = permute_width(cotangent)
    gain1 = permute_width(norm_gain)[None, :]
    gain2 = permute_width(ffn_gain)[None, :]
    scale1 = lax.rsqrt(jnp.mean(hid * hid, axis=-1, keepdims=True) + epsilon)
    normed = (hid * scale1 * gain1).astype(bf16)

    halo = ring.line(normed[rows - HALO :], 1)
    normed_ext = jnp.concatenate([halo, normed], axis=0)

    start = ti * rows
    cosine, sine = rope_tables(rows, start)
    padded = jnp.concatenate([jnp.full((back,), -1, jnp.int32), segment])
    seg_keys = lax.dynamic_slice_in_dim(padded, start, back + rows)
    seg_own = seg_keys[back:]
    seg_col, seg_row = seg_own[:, None], seg_own[None, :]
    chunks = rows // SPAN
    grouped = seg_own.reshape(chunks, SPAN)
    before = jnp.concatenate([seg_keys[back - 1 : back], grouped[:-1, -1]])
    carry_in = (grouped == before[:, None]).astype(f32).reshape(rows)
    in_last = (grouped == grouped[:, -1:]).astype(f32).reshape(rows)
    keeps = [(seg_keys[back - j : back - j + rows] == seg_own).astype(f32) for j in range(KCONV)]
    zero = jnp.zeros((rows,), f32)
    meta = jnp.stack(keeps + [carry_in, in_last, zero, zero], axis=1)
    first_tokens = seg_own.reshape(rows // QB, QB)[:, 0]
    doc_start = jnp.sum((segment[None, :] < first_tokens[:, None]).astype(jnp.int32), axis=1)
    first_block = jnp.maximum(doc_start - (start - back), 0) // KB
    per_place = QH // nt // 2
    place = jnp.stack(
        [lax.rem(ti + nt - a // per_place, nt) * per_place + a % per_place for a in range(QH // 2)]
    ).astype(jnp.int32)
    first_block = jnp.concatenate([first_block.astype(jnp.int32), place])

    kv = dot(normed, w_kv)
    key = rotate(kv[:, : KVH * HD], cosine, sine).astype(bf16)
    value = kv[:, KVH * HD :].astype(bf16)
    kv_own = jnp.concatenate([key, value], axis=1)
    kv_all = jnp.concatenate([ring.line(kv_own, s) for s in range(hops, 0, -1)] + [kv_own], axis=0)
    keys3 = kv_all[:, : KVH * HD].reshape(-1, KVH, HD).transpose(1, 0, 2)
    vals3 = kv_all[:, KVH * HD :].reshape(-1, KVH, HD).transpose(1, 0, 2)
    vals_t = kv_all[:, KVH * HD :].T
    query = rotate(dot(normed, w_q), cosine, sine).astype(bf16)
    query8 = query * jnp.asarray(HD ** -0.5, bf16)

    bc_raw = dot(normed_ext, w_bc)
    x_raw = dot(normed_ext, w_x)
    u = jnp.concatenate([x_raw, bc_raw], axis=1)
    dt_raw = dot(normed, w_step)
    conv_rel = jnp.concatenate([relative(conv_weight[:, :INNER], 1), conv_weight[:, INNER:]], axis=1)
    bias_rel = jnp.concatenate([relative(conv_bias[:INNER], 0), conv_bias[INNER:]], axis=0)
    taps = jnp.concatenate([conv_rel, bias_rel[None, :], jnp.zeros((3, INNER + 2 * NS), f32)], axis=0)
    rate = -jnp.exp(relative(decay_log, 0))
    heads = jnp.zeros((8, LANE), f32)
    heads = heads.at[0, :MH].set(relative(step_bias, 0)).at[1, :MH].set(rate)
    skip = jnp.broadcast_to(jnp.repeat(relative(skip_gain, 0), MP)[None, :], (8, INNER))
    spread = expander()
    spread2 = jnp.concatenate([spread, spread], axis=0)
    gather2 = jnp.concatenate([spread.T, spread.T], axis=0)

    mix, dt, cum, cumt, ec, fw, g, final = mamba_pre(u, taps, meta, dt_raw, heads, spread2)
    decay_all = jnp.prod(g.reshape(chunks, 8, LANE)[:, 0, :], axis=0)[:MH]
    decay_wide = jnp.repeat(decay_all, MP)[None, :]
    final_low = final.astype(bf16)
    state_in = None
    for s in range(hops, 0, -1):
        came = ring.line_heads(final_low, s)
        if s > 1:
            decays_came = ring.line_heads(decay_wide, 1)
            state_in = came.astype(f32) * decays_came
        else:
            state_in = came.astype(f32) if state_in is None else state_in + came.astype(f32)

    attended, lse = attn_fwd(first_block, query8, keys3, vals_t, seg_row, seg_keys[:, None])
    z_gate = dot(normed, w_z)
    gated, full, states = mamba_fwd(
        state_in, mix, dt, cum, cumt, ec, fw, g, seg_col, seg_row, z_gate, skip, spread2
    )
    mixer = dot(attended, w_ao, NT) + dot(gated, w_mo, NT)
    residual = hid + mixer
    scale2 = lax.rsqrt(jnp.mean(residual * residual, axis=-1, keepdims=True) + epsilon)
    normed2 = (residual * scale2 * gain2).astype(bf16)

    gate_lin = dot(normed2, w_fg)
    up_lin = dot(normed2, w_fu)
    sig = jax.nn.sigmoid(gate_lin)
    silu = gate_lin * sig
    activation = (silu * up_lin).astype(bf16)
    output = (residual + dot(activation, w_fd, NT)).astype(bf16)

    d_act = dot(cot, w_fd).astype(bf16).astype(f32)
    d_gate = (d_act * up_lin * (sig * (1.0 + gate_lin * (1.0 - sig)))).astype(bf16)
    d_up = (d_act * silu).astype(bf16)
    d_normed2 = dot(d_gate, w_fg, NT) + dot(d_up, w_fu, NT)
    d_res_norm, ffn_gain_grad = rms_back(d_normed2, residual, scale2, gain2)
    d_residual = cot.astype(f32) + d_res_norm
    d_mixer = d_residual.astype(bf16)

    def scatter(pairs):
        cols = sum(right.shape[1] for _, right in pairs)

        def make(lo, hi):
            half = width // 2
            if hi - lo == 2:
                return jnp.concatenate([dot(l[:, :half], r, TN) for l, r in pairs], axis=1)
            return jnp.concatenate([dot(l[:, half:], r, TN).astype(bf16) for l, r in pairs], axis=1)

        return ring.scatter_dp(make, cols)

    def scatter_both(pairs, widths=None):
        summed = scatter(pairs)
        parts = []
        for s in range(nt):
            at, pieces = 0, []
            for _, right in pairs:
                w = right.shape[1] // nt
                pieces.append(summed[:, at + s * w : at + (s + 1) * w])
                at += right.shape[1]
            parts.append(jnp.concatenate(pieces, axis=1))
        own = ring.scatter_tensor(parts)
        outs, at = [], 0
        for _, right in pairs:
            w = right.shape[1] // nt
            outs.append(own[:, at : at + w])
            at += w
        return outs

    (g_fd,) = scatter_both([(cot, activation)])
    g_fg, g_fu = scatter_both([(normed2, d_gate), (normed2, d_up)])

    d_gated = dot(d_mixer, w_mo).astype(bf16)
    d_attended = dot(d_mixer, w_ao).astype(bf16)
    dy, d_z, back_state = mamba_bpre(d_gated, z_gate, full, mix, ec, g, spread2)
    back_low = back_state.astype(bf16)
    d_state = None
    for s in range(hops, 0, -1):
        came = ring.line_heads(back_low, -s)
        if s > 1:
            decays_came = ring.line_heads(decay_wide, -1)
            d_state = came.astype(f32) * decays_came
        else:
            d_state = came.astype(f32) if d_state is None else d_state + came.astype(f32)
    g_ao, g_mo = scatter_both([(d_mixer, attended), (d_mixer, gated)])

    d_query, dk3, dv3 = attn_bwd(
        first_block, query8, keys3, vals3, d_attended, attended, lse, seg_row, seg_keys[:, None]
    )
    dkv = jnp.concatenate([dk3.transpose(1, 0, 2).reshape(-1, KVH * HD), dv3.transpose(1, 0, 2).reshape(-1, KVH * HD)], axis=1)
    dkv_own = dkv[back:]
    for s in range(1, hops + 1):
        at = back - s * rows
        dkv_own = dkv_own + ring.line(dkv[at : at + rows].astype(bf16), -s).astype(f32)
    d_k = rotate(dkv_own[:, : KVH * HD], cosine, -sine).astype(bf16)
    d_v = dkv_own[:, KVH * HD :].astype(bf16)
    d_q = rotate(d_query.astype(f32), cosine, -sine).astype(bf16)

    d_pre, d_step, conv_grads, small = mamba_bwd(
        d_state, mix, dt, cum, cumt, ec, fw, g, seg_col, seg_row, dy, states, u, taps, meta, skip, heads, spread2, gather2
    )
    after = jnp.concatenate([ring.line_heads(d_pre[:8, :INNER], -1), ring.line(d_pre[:8, INNER:], -1)], axis=1)
    d_ext = jnp.concatenate([d_pre, after], axis=0)
    seg_pad = jnp.concatenate([segment, jnp.full((KCONV,), -2, jnp.int32)])
    d_u = taps[KCONV - 1 : KCONV] * d_pre
    for j in range(1, KCONV):
        same = (lax.dynamic_slice_in_dim(seg_pad, start + j, rows) == seg_own).astype(f32)[:, None]
        d_u = d_u + taps[KCONV - 1 - j : KCONV - j] * d_ext[j : j + rows] * same
    d_u = d_u.astype(bf16)
    d_x, d_bc = d_u[:, :INNER], d_u[:, INNER:]

    d_shared = jnp.concatenate([d_k, d_v, d_bc], axis=1)
    w_shared_in = w_shared
    d_normed = (
        dot(d_q, w_q, NT) + dot(d_z, w_z, NT) + dot(d_x, w_x, NT) + dot(d_shared, w_shared_in, NT) + dot(d_step, w_step, NT)
    )
    d_hid_norm, norm_gain_grad = rms_back(d_normed, hid, scale1, gain1)
    hidden_grad = permute_width(d_residual + d_hid_norm, False)

    d_step4 = jnp.concatenate(
        [jnp.pad(d_step[:, s * step_cols : (s + 1) * step_cols], ((0, 0), (0, LANE - step_cols))) for s in range(nt)], axis=1
    )
    g_q, g_z = scatter_both([(normed, d_q), (normed, d_z)])
    g_x, g_step = scatter_both([(normed, d_x), (normed, d_step4)])
    shared = scatter([(normed, d_shared)])
    piece = block // nt
    shared_parts = [
        lax.dynamic_slice_in_dim(shared, lax.rem(ti + nt - s, nt) * piece, piece, 0) for s in range(nt)
    ]
    g_shared = ring.scatter_tensor(shared_parts)

    conv_flat = jnp.concatenate([relative(conv_grads[: KCONV + 1, :INNER], 1), conv_grads[: KCONV + 1, INNER:]], axis=1)
    small_flat = relative(small[:3, :MH], 1)
    vector = jnp.concatenate(
        [permute_width(norm_gain_grad, False), permute_width(ffn_gain_grad, False), conv_flat.reshape(-1), small_flat.reshape(-1)]
    )
    size = vector.shape[0]
    padded_size = -(-size // 1024) * 1024
    vector = ring.all_sum(jnp.pad(vector, (0, padded_size - size)).reshape(-1, LANE)).reshape(-1)
    at = 2 * width
    conv_sum = vector[at : at + conv_flat.size].reshape(conv_flat.shape)
    at += conv_flat.size
    small_sum = vector[at : at + 3 * MH].reshape(3, MH)
    return (
        output_back(permute_width, output),
        hidden_grad,
        vector[:width],
        vector[width : 2 * width],
        g_q,
        g_shared[:, : KVH * HD],
        g_shared[:, KVH * HD : 2 * KVH * HD],
        g_ao.T,
        g_z,
        g_x,
        g_shared[:, 2 * KVH * HD :],
        g_step[:, :step_cols],
        g_mo.T,
        conv_sum[:KCONV],
        conv_sum[KCONV],
        small_sum[0],
        small_sum[1],
        small_sum[2],
        g_fg,
        g_fu,
        g_fd.T,
    )


def output_back(permute, output):
    return permute(output, False)


def solution(mesh):
    in_specs = (
        P(("dp", "tensor"), None),
        P("dp", None),
        P(("dp", "tensor"), None),
        P(),
        P(),
        P("dp", "tensor"),
        P("dp", None),
        P("dp", None),
        P("tensor", "dp"),
        P("dp", "tensor"),
        P("dp", "tensor"),
        P("dp", None),
        P("dp", "tensor"),
        P("tensor", "dp"),
        P(),
        P(),
        P(),
        P(),
        P(),
        P("dp", "tensor"),
        P("dp", "tensor"),
        P("tensor", "dp"),
    )
    out_specs = (
        P(("dp", "tensor"), None),
        P(("dp", "tensor"), None),
        P(),
        P(),
        P("dp", "tensor"),
        P(("dp", "tensor"), None),
        P(("dp", "tensor"), None),
        P("tensor", "dp"),
        P("dp", "tensor"),
        P("dp", "tensor"),
        P(("dp", "tensor"), None),
        P("dp", "tensor"),
        P("tensor", "dp"),
        P(),
        P(),
        P(),
        P(),
        P(),
        P("dp", "tensor"),
        P("dp", "tensor"),
        P("tensor", "dp"),
    )
    return jax.shard_map(
        functools.partial(per_device, mesh), mesh=mesh, in_specs=in_specs, out_specs=out_specs, check_vma=False
    )
```

```python
import functools

import jax
import jax.numpy as jnp
import numpy as np
from jax import lax
from jax.experimental import pallas as pl
from jax.experimental.pallas import tpu as pltpu
from jax.sharding import PartitionSpec as P

QH = 8
KVH = 2
HD = 64
MH = 24
MP = 64
NS = 128
KCONV = 4
GROUP = QH // KVH
INNER = MH * MP
SPAN = 128
HALO = 16
LANE = 128
QB = 128
KB = 256
NEG = -1e30
FFN_AFTER = 1
COST = pl.CostEstimate(flops=2_000_000_000, bytes_accessed=4_000_000, transcendentals=0)

epsilon = 1e-05
rope_base = 100000000000.0
f32 = jnp.float32
bf16 = jnp.bfloat16

NN = (((1,), (0,)), ((), ()))
NT = (((1,), (1,)), ((), ()))
TN = (((0,), (0,)), ((), ()))


def dot(a, b, dims=NN):
    return lax.dot_general(a, b, dims, preferred_element_type=f32)


def split2(v, axis=1):
    hi = v.astype(bf16)
    lo = (v - hi.astype(f32)).astype(bf16)
    return jnp.concatenate([hi, lo], axis=axis)


def params(mb):
    return pltpu.CompilerParams(vmem_limit_bytes=mb * 1024 * 1024)


def sds(shape, dtype):
    return jax.ShapeDtypeStruct(shape, dtype)


def whole(shape):
    return pl.BlockSpec(shape, lambda *_: (0,) * len(shape), pipeline_mode=pl.Buffered(1))


def wholes(arrays):
    return [whole(a.shape) for a in arrays]


def attn_keep(segk_ref, segq_ref, off, i, back):
    pos_k = lax.broadcasted_iota(jnp.int32, (KB, QB), 0) + off
    pos_q = lax.broadcasted_iota(jnp.int32, (KB, QB), 1) + (back + i * QB)
    same = segk_ref[pl.ds(off, KB), :] == segq_ref[:, i * QB : (i + 1) * QB]
    return same & (pos_k <= pos_q)


def head_columns(g):
    return [slice(c * HD, (c + 2) * HD) for c in range(g * GROUP, (g + 1) * GROUP, 2)]


def stack_heads(ref, i, columns):
    rows = slice(i * QB, (i + 1) * QB)
    heads = []
    for at in columns:
        pair = ref[rows, at]
        heads += [pair[:, :HD], pair[:, HD:]]
    return jnp.concatenate(heads, axis=0)


def turn(v, cosine, sine):
    lane = lax.broadcasted_iota(jnp.int32, v.shape, 1)
    swapped = jnp.where(lane % HD < HD // 2, pltpu.roll(v, LANE - HD // 2, 1), pltpu.roll(v, HD // 2, 1))
    return v * cosine + swapped * sine


def load_pairs(pair_ref, kv_refs, at):
    rows = kv_refs[0].shape[0]
    for n, ref in enumerate(kv_refs):
        both = ref[:, at : at + KVH * HD]
        for g in range(KVH):
            pair_ref[g, n * rows : (n + 1) * rows, :] = both[:, g * HD : (g + 1) * HD]


def attn_fwd_kernel(first_ref, q_ref, segq_ref, segk_ref, *refs):
    kv_refs, (o_ref, lse_ref, k_ref, vt_ref) = refs[:-4], refs[-4:]
    rows = q_ref.shape[0]
    back = k_ref.shape[1] - rows
    wide = GROUP * QB
    load_pairs(k_ref, kv_refs, 0)
    for n, ref in enumerate(kv_refs):
        vt_ref[:, n * rows : (n + 1) * rows] = ref[:, KVH * HD :].astype(f32).T.astype(bf16)
    for i in range(rows // QB):
        last = (back + (i + 1) * QB + KB - 1) // KB
        for g in range(KVH):
            columns = head_columns(g)
            queries = stack_heads(q_ref, i, columns)

            def body(j, carry):
                top, total, acc = carry
                off = pl.multiple_of(j * KB, KB)
                scores = dot(k_ref[g, pl.ds(off, KB), :], queries, NT)
                keep = attn_keep(segk_ref, segq_ref, off, i, back)
                keep = jnp.concatenate([keep] * GROUP, axis=1)
                scores = jnp.where(keep, scores, NEG)
                new_top = jnp.maximum(top, jnp.max(scores, axis=0, keepdims=True))
                scale = jnp.exp(top - new_top)
                probs = jnp.exp(scores - new_top)
                total = total * scale + jnp.sum(probs, axis=0, keepdims=True)
                vt = vt_ref[g * HD : (g + 1) * HD, pl.ds(off, KB)]
                acc = acc * scale + dot(vt, probs.astype(bf16))
                return new_top, total, acc

            start = (jnp.full((1, wide), NEG, f32), jnp.zeros((1, wide), f32), jnp.zeros((HD, wide), f32))
            top, total, acc = lax.fori_loop(first_ref[i], last, body, start)
            lse_ref[i * KVH + g : i * KVH + g + 1, :] = top + jnp.log(total)
            acc = acc / total
            for h in range(0, GROUP, 2):
                pair = jnp.concatenate(
                    [acc[:, h * QB : (h + 1) * QB], acc[:, (h + 1) * QB : (h + 2) * QB]], axis=0
                ).T
                o_ref[i * QB : (i + 1) * QB, columns[h // 2]] = pair.astype(bf16)


def attn_bwd_kernel(first_ref, q_ref, do_ref, o_ref, lse_ref, segq_ref, segk_ref, cos_ref, sin_ref, *refs):
    n_kv = (len(refs) - 5) // 2
    kv_refs, dq_ref, dkv_refs = refs[:n_kv], refs[n_kv], refs[n_kv + 1 : 2 * n_kv + 1]
    k_ref, v_ref, dk_ref, dv_ref = refs[2 * n_kv + 1 :]
    rows = q_ref.shape[0]
    back = k_ref.shape[1] - rows
    wide = GROUP * QB
    load_pairs(k_ref, kv_refs, 0)
    load_pairs(v_ref, kv_refs, KVH * HD)
    dk_ref[...] = jnp.zeros_like(dk_ref)
    dv_ref[...] = jnp.zeros_like(dv_ref)
    for i in range(rows // QB):
        last = (back + (i + 1) * QB + KB - 1) // KB
        here = slice(i * QB, (i + 1) * QB)
        for g in range(KVH):
            columns = head_columns(g)
            queries = stack_heads(q_ref, i, columns)
            grads = stack_heads(do_ref, i, columns)
            outs = stack_heads(o_ref, i, columns)
            prod = grads.astype(f32) * outs.astype(f32)
            ones = jnp.ones((8, 2 * HD), bf16)
            delta = dot(ones, split2(prod), NT)[0:1, :]
            lse = lse_ref[i * KVH + g : i * KVH + g + 1, :]

            def body(j, acc):
                off = pl.multiple_of(j * KB, KB)
                keys = k_ref[g, pl.ds(off, KB), :]
                vals = v_ref[g, pl.ds(off, KB), :]
                keep = attn_keep(segk_ref, segq_ref, off, i, back)
                keep = jnp.concatenate([keep] * GROUP, axis=1)
                scores = jnp.where(keep, dot(keys, queries, NT), NEG)
                probs = jnp.exp(scores - lse)
                dprobs = dot(vals, grads, NT)
                dscores = (probs * (dprobs - delta)).astype(bf16)
                dv_ref[g, pl.ds(off, KB), :] += dot(probs.astype(bf16), grads)
                dk_ref[g, pl.ds(off, KB), :] += dot(dscores, queries)
                return acc + dot(keys, dscores, TN)

            acc = lax.fori_loop(first_ref[i], last, body, jnp.zeros((HD, wide), f32))
            acc = acc * (HD ** -0.5)
            for h in range(0, GROUP, 2):
                pair = jnp.concatenate(
                    [acc[:, h * QB : (h + 1) * QB], acc[:, (h + 1) * QB : (h + 2) * QB]], axis=0
                ).T
                pair = turn(pair.astype(bf16).astype(f32), cos_ref[here, :], -sin_ref[here, :])
                dq_ref[here, columns[h // 2]] = pair.astype(bf16)
    for n, out in enumerate(dkv_refs):
        span = slice(n * rows, (n + 1) * rows)
        for at, ref in ((0, dk_ref), (KVH * HD, dv_ref)):
            both = jnp.concatenate([ref[g, span, :] for g in range(KVH)], axis=1)
            out[:, at : at + KVH * HD] = both.astype(out.dtype)


SMEM = pl.BlockSpec(memory_space=pltpu.SMEM)


def attn_fwd(first, q, segq, segk, kvs):
    rows = q.shape[0]
    total = rows * len(kvs)
    arrays = (q, segq, segk, *kvs)
    outs = (sds(q.shape, bf16), sds((rows // QB * KVH, GROUP * QB), f32))
    return pl.pallas_call(
        attn_fwd_kernel,
        grid=(1,),
        out_shape=outs,
        in_specs=[SMEM] + wholes(arrays),
        out_specs=tuple(wholes(outs)),
        scratch_shapes=[pltpu.VMEM((KVH, total, HD), bf16), pltpu.VMEM((KVH * HD, total), bf16)],
        compiler_params=params(40),
        cost_estimate=COST,
        name="attn_fwd",
    )(first, *arrays)


def attn_bwd(first, q, do, o, lse, segq, segk, cosine, sine, kvs):
    total = q.shape[0] * len(kvs)
    arrays = (q, do, o, lse, segq, segk, cosine, sine, *kvs)
    outs = (sds(q.shape, bf16), *[sds(a.shape, bf16) for a in kvs[:-1]], sds(kvs[-1].shape, f32))
    return pl.pallas_call(
        attn_bwd_kernel,
        grid=(1,),
        out_shape=outs,
        in_specs=[SMEM] + wholes(arrays),
        out_specs=tuple(wholes(outs)),
        scratch_shapes=[pltpu.VMEM((KVH, total, HD), bf16)] * 2 + [pltpu.VMEM((KVH, total, HD), f32)] * 2,
        compiler_params=params(40),
        cost_estimate=COST,
        name="attn_bwd",
    )(first, *arrays)


COLS = (INNER + 2 * NS) // LANE


def tri_masks():
    t = lax.broadcasted_iota(jnp.int32, (SPAN, SPAN), 0)
    s = lax.broadcasted_iota(jnp.int32, (SPAN, SPAN), 1)
    return t, s


def widen(v, spread2):
    return dot(split2(v), spread2)


def store_carry(step, carry_ref, state_ref, keep_ref):
    @pl.when(step == pl.num_programs(0) - 1)
    def _():
        carry_ref[:NS, :] = state_ref[...].astype(bf16)
        keep = keep_ref[...]
        high = keep.astype(bf16)
        carry_ref[NS:, :] = jnp.concatenate([high, (keep - high.astype(f32)).astype(bf16)], axis=0)


def load_carry(near_ref, far_refs):
    state = near_ref[:NS, :].astype(f32)
    for far_ref in far_refs:
        kept = near_ref[NS : NS + 1, :].astype(f32) + near_ref[NS + 8 : NS + 9, :].astype(f32)
        state = state + far_ref[:NS, :].astype(f32) * kept
    return state


def conv_block(u_ref, tap_ref, meta, base, col):
    lanes = slice(col * LANE, (col + 1) * LANE)
    window = u_ref[pl.ds(base + HALO - 8, SPAN + 8), lanes]
    taps = [window[8:, :]]
    for j in range(1, KCONV):
        taps.append(window[8 - j : 8 - j + SPAN, :] * meta[:, j : j + 1])
    total = tap_ref[KCONV : KCONV + 1, lanes] + tap_ref[KCONV - 1 : KCONV, lanes] * taps[0]
    for j in range(1, KCONV):
        total = total + tap_ref[KCONV - 1 - j : KCONV - j, lanes] * taps[j]
    return taps, total


def mamba_pre_kernel(u_ref, tap_ref, meta_ref, dtr_ref, head_ref, spread_ref,
                     mix_ref, dt_ref, cum_ref, cumt_ref, ec_ref, fw_ref, g_ref, carry_ref, fin_ref, keep_ref):
    c = pl.program_id(0)
    base = pl.multiple_of(c * SPAN, SPAN)

    @pl.when(c == 0)
    def _():
        fin_ref[...] = jnp.zeros_like(fin_ref)
        keep_ref[...] = jnp.ones_like(keep_ref)

    meta = meta_ref[...]
    for col in range(COLS):
        total = conv_block(u_ref, tap_ref, meta, base, col)[1]
        mix_ref[:, col * LANE : (col + 1) * LANE] = (total * jax.nn.sigmoid(total)).astype(bf16)
    raw = dtr_ref[...] + head_ref[0:1, :]
    dt = jnp.maximum(raw, 0.0) + jnp.log1p(jnp.exp(-jnp.abs(raw)))
    decay = dt * head_ref[1:2, :]
    t, s = tri_masks()
    lower = (t >= s).astype(f32)
    cum = lax.dot_general(lower, decay, NN, precision=lax.Precision.HIGHEST, preferred_element_type=f32)
    end = cum[SPAN - 1 : SPAN, :]
    ec = meta[:, 4:5] * jnp.exp(cum)
    fw = meta[:, 5:6] * jnp.exp(end - cum)
    gain = ec[SPAN - 1 : SPAN, :]
    dt_ref[...] = dt
    cum_ref[...] = cum
    cumt_ref[...] = cum.T[: cumt_ref.shape[0], :]
    ec_ref[...] = ec
    fw_ref[...] = fw
    gain8 = jnp.broadcast_to(gain, (8, LANE))
    g_ref[...] = gain8
    spread2 = spread_ref[...]
    weight = widen(fw * dt, spread2)
    x = mix_ref[:, :INNER].astype(f32)
    b = mix_ref[:, INNER : INNER + NS]
    gain_wide = widen(gain8, spread2)
    fin_ref[...] = fin_ref[...] * gain_wide[0:1, :] + dot(b, (x * weight).astype(bf16), TN)
    keep_ref[...] = keep_ref[...] * gain_wide
    store_carry(c, carry_ref, fin_ref, keep_ref)


def chunk_spec(width):
    return pl.BlockSpec((SPAN, width), lambda c: (c, 0))


def mamba_pre(u, taps, meta, dt_raw, heads, spread2):
    rows = meta.shape[0]
    n = rows // SPAN
    width = INNER + 2 * NS
    hl = 32
    return pl.pallas_call(
        mamba_pre_kernel,
        grid=(n,),
        in_specs=[whole(u.shape), whole(taps.shape), chunk_spec(8), chunk_spec(LANE), whole(heads.shape),
                  whole(spread2.shape)],
        out_specs=(chunk_spec(width), chunk_spec(LANE), chunk_spec(LANE), pl.BlockSpec((hl, SPAN), lambda c: (0, c)),
                   chunk_spec(LANE), chunk_spec(LANE), pl.BlockSpec((8, LANE), lambda c: (c, 0)), whole((NS + 16, INNER))),
        out_shape=(sds((rows, width), bf16), sds((rows, LANE), f32), sds((rows, LANE), f32), sds((hl, rows), f32),
                   sds((rows, LANE), f32), sds((rows, LANE), f32), sds((8 * n, LANE), f32),
                   sds((NS + 16, INNER), bf16)),
        scratch_shapes=[pltpu.VMEM((NS, INNER), f32), pltpu.VMEM((8, INNER), f32)],
        compiler_params=params(40),
        cost_estimate=COST,
        name="mamba_pre",
    )(u, taps, meta, dt_raw, heads, spread2)


def pair_halves(v):
    lane = lax.broadcasted_iota(jnp.int32, v.shape, 1)
    zero = jnp.zeros_like(v)
    return jnp.concatenate([jnp.where(lane < MP, v, zero), jnp.where(lane < MP, zero, v)], axis=0)


def mamba_fwd_kernel(mix_ref, dt_ref, cum_ref, cumt_ref, ec_ref, fw_ref, g_ref, segc_ref, segr_ref,
                     z_ref, skip_ref, spread_ref, *refs):
    carries, (gated_ref, full_ref, states_ref, state_ref) = refs[:-4], refs[-4:]
    c = pl.program_id(0)

    @pl.when(c == 0)
    def _():
        state_ref[...] = load_carry(carries[0], carries[1:])

    state = state_ref[...].astype(bf16)
    states_ref[0] = state
    spread2 = spread_ref[...]
    b = mix_ref[:, INNER : INNER + NS]
    cm = mix_ref[:, INNER + NS :]
    t, s = tri_masks()
    allowed = (segc_ref[...] == segr_ref[...]) & (t >= s)
    off = jnp.where(allowed, 0.0, NEG)
    affinity = dot(cm, b, NT)
    cum = cum_ref[...]
    dt = dt_ref[...]
    dt_wide = widen(dt, spread2)
    ec_wide = widen(ec_ref[...], spread2)
    carried = dot(cm, state) * ec_wide
    for p in range(MH // 2):
        lanes = slice(p * LANE, (p + 1) * LANE)
        x = mix_ref[:, lanes].astype(f32)
        pieces = []
        for h in (2 * p, 2 * p + 1):
            gap = cum[:, h : h + 1] - cumt_ref[h : h + 1, :] + off
            pieces.append((affinity * jnp.exp(gap)).astype(bf16))
        scaled = (x * dt_wide[:, lanes]).astype(bf16)
        y = dot(jnp.concatenate(pieces, axis=1), pair_halves(scaled)) + carried[:, lanes]
        y = y + skip_ref[0:1, lanes] * x
        z = z_ref[:, lanes]
        full_ref[:, lanes] = y.astype(bf16)
        gated_ref[:, lanes] = (y * (z * jax.nn.sigmoid(z))).astype(bf16)
    weight = widen(fw_ref[...] * dt, spread2)
    x = mix_ref[:, :INNER].astype(f32)
    gain = widen(g_ref[...], spread2)[0:1, :]
    state_ref[...] = state_ref[...] * gain + dot(b, (x * weight).astype(bf16), TN)


def mamba_fwd(mix, dt, cum, cumt, ec, fw, g, segc, segr, z, skip, spread2, carries):
    rows = mix.shape[0]
    n = rows // SPAN
    return pl.pallas_call(
        mamba_fwd_kernel,
        grid=(n,),
        in_specs=[chunk_spec(mix.shape[1]), chunk_spec(LANE), chunk_spec(LANE),
                  pl.BlockSpec((cumt.shape[0], SPAN), lambda c: (0, c)), chunk_spec(LANE), chunk_spec(LANE),
                  pl.BlockSpec((8, LANE), lambda c: (c, 0)), chunk_spec(1), pl.BlockSpec((1, SPAN), lambda c: (0, c)),
                  chunk_spec(INNER), whole(skip.shape), whole(spread2.shape), *wholes(carries)],
        out_specs=(chunk_spec(INNER), chunk_spec(INNER), pl.BlockSpec((1, NS, INNER), lambda c: (c, 0, 0))),
        out_shape=(sds((rows, INNER), bf16), sds((rows, INNER), bf16), sds((n, NS, INNER), bf16)),
        scratch_shapes=[pltpu.VMEM((NS, INNER), f32)],
        compiler_params=params(40),
        cost_estimate=COST,
        name="mamba_fwd",
    )(mix, dt, cum, cumt, ec, fw, g, segc, segr, z, skip, spread2, *carries)


def mamba_bpre_kernel(dg_ref, z_ref, full_ref, cm_ref, ec_ref, g_ref, spread_ref, dy_ref, dz_ref, carry_ref, back_ref, keep_ref):
    c = pl.program_id(0)

    @pl.when(c == 0)
    def _():
        back_ref[...] = jnp.zeros_like(back_ref)
        keep_ref[...] = jnp.ones_like(keep_ref)

    spread2 = spread_ref[...]
    z = z_ref[...]
    sig = jax.nn.sigmoid(z)
    dg = dg_ref[...].astype(f32)
    dy = dg * (z * sig)
    dy_ref[...] = dy.astype(bf16)
    dz_ref[...] = (dg * full_ref[...].astype(f32) * (sig * (1.0 + z * (1.0 - sig)))).astype(bf16)
    weighted = (dy * widen(ec_ref[...], spread2)).astype(bf16)
    gain_wide = widen(g_ref[...], spread2)
    back_ref[...] = back_ref[...] * gain_wide[0:1, :] + dot(cm_ref[...], weighted, TN)
    keep_ref[...] = keep_ref[...] * gain_wide
    store_carry(c, carry_ref, back_ref, keep_ref)


def mamba_bpre(dg, z, full, mix, ec, g, spread2):
    rows = dg.shape[0]
    n = rows // SPAN
    rev = lambda width, col=0: pl.BlockSpec((SPAN, width), lambda c: (n - 1 - c, col))
    return pl.pallas_call(
        mamba_bpre_kernel,
        grid=(n,),
        in_specs=[rev(INNER), rev(INNER), rev(INNER), rev(NS, (INNER + NS) // NS), rev(LANE),
                  pl.BlockSpec((8, LANE), lambda c: (n - 1 - c, 0)), whole(spread2.shape)],
        out_specs=(rev(INNER), rev(INNER), whole((NS + 16, INNER))),
        out_shape=(sds((rows, INNER), bf16), sds((rows, INNER), bf16), sds((NS + 16, INNER), bf16)),
        scratch_shapes=[pltpu.VMEM((NS, INNER), f32), pltpu.VMEM((8, INNER), f32)],
        compiler_params=params(40),
        cost_estimate=COST,
        name="mamba_bpre",
    )(dg, z, full, mix, ec, g, spread2)


def mamba_bwd_kernel(mix_ref, dt_ref, cum_ref, cumt_ref, ec_ref, fw_ref, g_ref, segc_ref, segr_ref,
                     dy_ref, states_ref, u_ref, tap_ref, meta_ref, skip_ref, head_ref, spread_ref, gather_ref, *refs):
    carries = refs[:-9]
    dpre_ref, ddt_ref, conv_ref, small_ref, dstate_ref, acc_ref, rows_ref, dx_ref, dbc_ref = refs[-9:]
    step = pl.program_id(0)
    c = pl.num_programs(0) - 1 - step
    base = pl.multiple_of(c * SPAN, SPAN)

    @pl.when(step == 0)
    def _():
        dstate_ref[...] = load_carry(carries[0], carries[1:])
        conv_ref[...] = jnp.zeros_like(conv_ref)
        small_ref[...] = jnp.zeros_like(small_ref)
        rows_ref[...] = jnp.zeros_like(rows_ref)

    spread2 = spread_ref[...]
    gather2 = gather_ref[...]
    b = mix_ref[:, INNER : INNER + NS]
    cm = mix_ref[:, INNER + NS :]
    cum = cum_ref[...]
    dt = dt_ref[...]
    dt_wide = widen(dt, spread2)
    s, t = tri_masks()
    allowed = (segc_ref[...] == segr_ref[...]) & (t >= s)
    off = jnp.where(allowed, 0.0, NEG)
    affinity = dot(b, cm, NT)
    acc_ref[...] = jnp.zeros_like(acc_ref)
    for p in range(MH // 2):
        lanes = slice(p * LANE, (p + 1) * LANE)
        x = mix_ref[:, lanes].astype(f32)
        scaled = (x * dt_wide[:, lanes]).astype(bf16)
        dy = dy_ref[:, lanes]
        dmix = dot(pair_halves(scaled), dy, NT)
        pieces = []
        total = None
        for q, h in enumerate((2 * p, 2 * p + 1)):
            gap = cumt_ref[h : h + 1, :] - cum[:, h : h + 1] + off
            decays = jnp.exp(gap)
            mixing = (affinity * decays).astype(bf16)
            pieces.append(mixing)
            dm = dmix[q * SPAN : (q + 1) * SPAN, :]
            rows_ref[h : h + 1, :] = jnp.sum(dm * mixing.astype(f32), axis=0, keepdims=True)
            part = dm * decays
            total = part if total is None else total + part
        acc_ref[...] += total
        dx_ref[:, lanes] = dot(jnp.concatenate(pieces, axis=1), pair_halves(dy))
    dscaled = dx_ref[...]
    x = mix_ref[:, :INNER].astype(f32)
    scaled = (x * dt_wide).astype(bf16).astype(f32)
    dy = dy_ref[...].astype(f32)
    dstate = dstate_ref[...]
    dstate_low = dstate.astype(bf16)
    state = states_ref[0]
    ec_wide = widen(ec_ref[...], spread2)
    fw_wide = widen(fw_ref[...], spread2)
    from_state = fw_wide * dot(b, dstate_low)
    carried = ec_wide * dot(cm, state)
    weighted_dy = (dy * ec_wide).astype(bf16)
    cols_sum = dot(split2(scaled * dscaled), gather2)
    carr_sum = dot(split2(dy * carried), gather2)
    fdf_sum = dot(split2(scaled * from_state), gather2)
    dxd = dscaled + from_state
    ddt_direct = dot(split2(x * dxd), gather2)
    skip_part = dot(split2(dy * x), gather2)
    gain = widen(g_ref[...], spread2)[0:1, :]
    state_dot = jnp.sum(dstate * state.astype(f32), axis=0, keepdims=True) * gain
    state_dot = dot(split2(jnp.broadcast_to(state_dot, (8, INNER))), gather2)[0:1, :]
    tt, ss = tri_masks()
    suffix = (ss >= tt).astype(bf16)
    prefix = (ss < tt).astype(bf16)
    suffix2 = jnp.concatenate([suffix, suffix], axis=1)
    dlog = dot(suffix2, split2(carr_sum - cols_sum, axis=0))
    dlog = dlog + dot(suffix2, split2(rows_ref[...]), NT)
    dlog = dlog + dot(jnp.concatenate([prefix, prefix], axis=1), split2(fdf_sum, axis=0)) + state_dot
    decay_rate = head_ref[1:2, :]
    ddt = (ddt_direct + dlog * decay_rate) * (1.0 - jnp.exp(-dt))
    ddt_ref[...] = ddt.astype(bf16)
    small_ref[0:1, :] += jnp.sum(dlog * dt, axis=0, keepdims=True) * decay_rate
    small_ref[1:2, :] += jnp.sum(skip_part, axis=0, keepdims=True)
    small_ref[2:3, :] += jnp.sum(ddt, axis=0, keepdims=True)
    dx_ref[...] = dxd * dt_wide + skip_ref[0:1, :] * dy
    daff = acc_ref[...]
    daff_low = daff.astype(bf16)
    fx = (scaled * fw_wide).astype(bf16)
    dbc_ref[:, :NS] = dot(daff_low, cm) + dot(fx, dstate_low, NT)
    dbc_ref[:, NS:] = dot(daff_low, b, TN) + dot(weighted_dy, state, NT)
    dstate_ref[...] = dstate * gain + dot(cm, weighted_dy, TN)
    meta = meta_ref[...]
    for col in range(COLS):
        lanes = slice(col * LANE, (col + 1) * LANE)
        taps, total = conv_block(u_ref, tap_ref, meta, base, col)
        sig = jax.nn.sigmoid(total)
        if col * LANE < INNER:
            dmixed = dx_ref[:, lanes]
        else:
            dmixed = dbc_ref[:, col * LANE - INNER : (col + 1) * LANE - INNER]
        dpre = dmixed * (sig * (1.0 + total * (1.0 - sig)))
        dpre_ref[:, lanes] = dpre
        for j in range(KCONV):
            conv_ref[KCONV - 1 - j : KCONV - j, lanes] += jnp.sum(dpre * taps[j], axis=0, keepdims=True)
        conv_ref[KCONV : KCONV + 1, lanes] += jnp.sum(dpre, axis=0, keepdims=True)


def mamba_bwd(mix, dt, cum, cumt, ec, fw, g, segc, segr, dy, states, u, taps, meta, skip, heads, spread2, gather2,
              carries):
    rows = mix.shape[0]
    n = rows // SPAN
    width = mix.shape[1]
    rev = lambda w: pl.BlockSpec((SPAN, w), lambda c: (n - 1 - c, 0))
    return pl.pallas_call(
        mamba_bwd_kernel,
        grid=(n,),
        in_specs=[rev(width), rev(LANE), rev(LANE),
                  pl.BlockSpec((cumt.shape[0], SPAN), lambda c: (0, n - 1 - c)), rev(LANE), rev(LANE),
                  pl.BlockSpec((8, LANE), lambda c: (n - 1 - c, 0)), rev(1),
                  pl.BlockSpec((1, SPAN), lambda c: (0, n - 1 - c)), rev(INNER),
                  pl.BlockSpec((1, NS, INNER), lambda c: (n - 1 - c, 0, 0)), whole(u.shape), whole(taps.shape),
                  rev(8), whole(skip.shape), whole(heads.shape), whole(spread2.shape), whole(gather2.shape),
                  *wholes(carries)],
        out_specs=(rev(width), rev(LANE), whole((8, width)), whole((8, LANE))),
        out_shape=(sds((rows, width), f32), sds((rows, LANE), bf16), sds((8, width), f32), sds((8, LANE), f32)),
        scratch_shapes=[pltpu.VMEM((NS, INNER), f32), pltpu.VMEM((SPAN, SPAN), f32), pltpu.VMEM((LANE, SPAN), f32),
                        pltpu.VMEM((SPAN, INNER), f32), pltpu.VMEM((SPAN, 2 * NS), f32)],
        compiler_params=params(56),
        cost_estimate=COST,
        name="mamba_bwd",
    )(mix, dt, cum, cumt, ec, fw, g, segc, segr, dy, states, u, taps, meta, skip, heads, spread2, gather2, *carries)


NB = 8
LOW = (0, 2, 4, 6)
ORDERS = ((2, 4), (4, 2))
SETS = ((0, 1), (2, 3))
SET_MASKS = ((0, 2, 4, 6), (0, 4, 2, 6))


class Ring:
    def __init__(self, mesh):
        self.nd = mesh.shape["dp"]
        self.nt = mesh.shape["tensor"]
        self.unit = self.nd // NB
        base = range(0, self.nd, self.unit)
        self.groups = [[b + i for i in range(self.unit)] for b in base]

    def dp(self, value, mask):
        step = mask * self.unit
        return lax.ppermute(value, "dp", [(i, i ^ step) for i in range(self.nd)])

    def shift(self, value, s):
        n = self.nt
        return lax.ppermute(value, "tensor", [(i, (i + s) % n) for i in range(n)])

    def line(self, value, s):
        n = self.nt
        return lax.ppermute(value, "tensor", [(i, i + s) for i in range(n) if 0 <= i + s < n])

    def block(self, value):
        if self.unit == 1:
            return value
        return lax.all_gather(value, "dp", axis=0, tiled=True, axis_index_groups=self.groups)

    def unblock(self, value):
        if self.unit == 1:
            return value
        return lax.psum_scatter(value, "dp", scatter_dimension=0, tiled=True, axis_index_groups=self.groups)

    def gather(self, pack, hold=lambda stage, values: values):
        own = self.block(pack)
        (own,) = hold(0, [own])
        parts = [own] + [self.shift(own, s) for s in range(1, self.nt)]
        pairs = hold(1, [join([parts[s] for s in members]) for members in SETS])
        nears = [self.dp(pair, one) for pair, (one, _) in zip(pairs, ORDERS)]
        firsts = [
            join([parts[s] for s in members] + [near]) for members, near in zip(SETS, nears)
        ]
        firsts = hold(2, firsts)
        sides = [[first, self.dp(first, two)] for first, (_, two) in zip(firsts, ORDERS)]
        sides = [hold(3, side) for side in sides]
        return [[lows, [self.dp(low, 1) for low in lows]] for lows in sides]

    def scatter(self, sent, kept):
        came = self.dp(sent, 1)
        parts = []
        for n, (second, first) in enumerate(ORDERS):
            here = slice(2 * n, 2 * n + 2)
            out = add(kept[here, 2:], came[here, 2:])
            mine = add(kept[here, :2], came[here, :2])
            got = self.dp(out, first)
            out = add(mine[:, 1:], got[:, 1:])
            mine = add(mine[:, :1], got[:, :1])
            got = self.dp(out, second)
            parts += [add(mine[i, 0], got[i, 0]) for i in range(2)]
        return parts

    def total(self, parts):
        total = parts[0].astype(f32)
        for s in range(1, self.nt):
            total = total + self.shift(parts[s], self.nt - s).astype(f32)
        return total

    def collect(self, parts):
        return self.unblock(self.total(parts))

    def all_sum(self, value):
        bit = 1
        while bit < self.nd:
            value = value + lax.ppermute(value, "dp", [(i, i ^ bit) for i in range(self.nd)])
            bit *= 2
        return value + sum(self.shift(value, s) for s in range(1, self.nt))


def after(values, *others):
    return lax.optimization_barrier((tuple(values), others))[0]


def add(a, b):
    return (a.astype(f32) + b.astype(f32)).astype(bf16)


def join_kernel(*refs):
    out = refs[-1]
    if len(out.shape) == 3:
        for i, ref in enumerate(refs[:-1]):
            out[i] = ref[...]
    else:
        for i, ref in enumerate(refs[:2]):
            out[0, i] = ref[...]
        out[1] = refs[2][...]


def join(pieces):
    rows, cols = pieces[0].shape
    shape = (2, rows, cols) if len(pieces) == 2 else (2, 2, rows, cols)
    return pl.pallas_call(
        join_kernel,
        grid=(1,),
        out_shape=sds(shape, bf16),
        in_specs=wholes(pieces),
        out_specs=whole(shape),
        compiler_params=params(40),
        cost_estimate=COST,
        name="join",
    )(*pieces)


def block_rows(index_ref, at, rows):
    return pl.ds(pl.multiple_of(index_ref[at] * rows, rows), rows)


def part_columns(index_ref, s, width):
    return pl.ds(pl.multiple_of(index_ref[8 + s] * width, width), width)


def assemble_kernel(widths, index_ref, *refs):
    buffers, outs = refs[:8], refs[8:]
    rows = buffers[0].shape[2]
    for n in range(2):
        for half in range(2):
            for k in range(4):
                buffer = buffers[4 * n + 2 * half + k // 2]
                m = LOW.index(SET_MASKS[n][k])
                here = block_rows(index_ref, 4 * half + m, rows)
                for i in range(2):
                    at = 0
                    for width, out in zip(widths, outs):
                        piece = buffer[k % 2, i, :, at : at + width]
                        at += width
                        if out.shape[1] == width:
                            out[here, :] = piece if n + i == 0 else out[here, :] + piece
                        else:
                            out[here, part_columns(index_ref, 2 * n + i, width)] = piece


def assemble(index, sides, widths, totals):
    buffers = [buffer for side in sides for lows in side for buffer in lows]
    model = NB * buffers[0].shape[2]
    outs = tuple(sds((model, total), bf16) for total in totals)
    return pl.pallas_call(
        functools.partial(assemble_kernel, widths),
        grid=(1,),
        out_shape=outs,
        in_specs=[SMEM] + wholes(buffers),
        out_specs=tuple(wholes(outs)),
        compiler_params=params(48),
        cost_estimate=COST,
        name="assemble",
    )(index, *buffers)


def project_kernel(widths, index_ref, *refs):
    buffers, (normed_ref, halo_ref, cos_ref, sin_ref) = refs[:8], refs[8:12]
    weights, (u_ref, q_ref, kv_ref, dt_ref) = refs[12:16], refs[16:]
    assemble_kernel(widths, index_ref, *buffers, *weights)
    w_q, w_step, w_x, w_shared = weights
    kv_width = KVH * HD
    half = normed_ref.shape[0] // 2
    for r in range(2):
        here = slice(r * half, (r + 1) * half)
        normed = normed_ref[here, :]
        cosine, sine = cos_ref[here, :], sin_ref[here, :]
        kv = dot(normed, w_shared[:, : 2 * kv_width])
        kv_ref[here, :kv_width] = turn(kv[:, :kv_width], cosine, sine).astype(bf16)
        kv_ref[here, kv_width:] = kv[:, kv_width:].astype(bf16)
        q = dot(normed, w_q[...])
        for c in range(0, q.shape[1], LANE):
            tile = turn(q[:, c : c + LANE], cosine, sine).astype(bf16)
            q_ref[here, c : c + LANE] = tile * jnp.asarray(HD ** -0.5, bf16)
        dt_ref[here, :] = dot(normed, w_step[...])
        below = slice(HALO + r * half, HALO + (r + 1) * half)
        u_ref[below, INNER:] = dot(normed, w_shared[:, 2 * kv_width :])
        for c in range(0, INNER, 512):
            u_ref[below, c : c + 512] = dot(normed, w_x[:, c : c + 512])
    u_ref[:HALO, INNER:] = dot(halo_ref[...], w_shared[:, 2 * kv_width :])
    for c in range(0, INNER, 512):
        u_ref[:HALO, c : c + 512] = dot(halo_ref[...], w_x[:, c : c + 512])


def project(index, sides, widths, totals, normed, halo, cosine, sine):
    buffers = [buffer for side in sides for lows in side for buffer in lows]
    rows, model = normed.shape
    arrays = (*buffers, normed, halo, cosine, sine)
    outs = tuple(sds((model, total), bf16) for total in totals)
    outs += (sds((HALO + rows, INNER + 2 * NS), f32), sds((rows, QH * HD), bf16), sds((rows, 2 * KVH * HD), bf16),
             sds((rows, LANE), f32))
    return pl.pallas_call(
        functools.partial(project_kernel, widths),
        grid=(1,),
        out_shape=outs,
        in_specs=[SMEM] + wholes(arrays),
        out_specs=tuple(wholes(outs)),
        compiler_params=params(56),
        cost_estimate=COST,
        name="project",
    )(index, *arrays)


def transpose_into(out_ref, values):
    for c in range(0, values.shape[1], LANE):
        out_ref[c : c + LANE, :] = values[:, c : c + LANE].astype(f32).T.astype(bf16)


def norm_kernel(h_ref, c_ref, gain_ref, n_ref, nt_ref, ct_ref, scale_ref):
    values = h_ref[...].astype(f32)
    scale = lax.rsqrt(jnp.mean(values * values, axis=-1, keepdims=True) + epsilon)
    scale_ref[...] = scale
    n_ref[...] = (values * scale * gain_ref[...]).astype(bf16)
    transpose_into(nt_ref, n_ref[...])
    transpose_into(ct_ref, c_ref[...])


def pack_kernel(flips, *refs):
    out, at = refs[-1], 0
    for flip, ref in zip(flips, refs[:-1]):
        if flip:
            count = ref.shape[0]
            for r in range(0, count, LANE):
                out[:, at + r : at + r + LANE] = ref[r : r + LANE, :].astype(f32).T.astype(bf16)
        else:
            count = ref.shape[1]
            out[:, at : at + count] = ref[...]
        at += count


def pack(arrays, flips):
    rows = arrays[0].shape[0]
    columns = sum(a.shape[0] if flip else a.shape[1] for a, flip in zip(arrays, flips))
    return simple_call(functools.partial(pack_kernel, flips), "pack", tuple(arrays), sds((rows, columns), bf16))


def middle_kernel(att_ref, gated_ref, wa_ref, wm_ref, h_ref, gain_ref, res_ref, n_ref, nt_ref, scale_ref):
    model = h_ref.shape[1]
    for c in range(0, model, 256):
        cols = slice(c, c + 256)
        mixer = dot(att_ref[...], wa_ref[cols, :], NT) + dot(gated_ref[...], wm_ref[cols, :], NT)
        res_ref[:, cols] = h_ref[:, cols].astype(f32) + mixer
    values = res_ref[...]
    scale = lax.rsqrt(jnp.mean(values * values, axis=-1, keepdims=True) + epsilon)
    scale_ref[...] = scale
    n_ref[...] = (values * scale * gain_ref[...]).astype(bf16)
    transpose_into(nt_ref, n_ref[...])


def after_ffn_kernel(dn_ref, res_ref, scale_ref, gain_ref, c_ref, wa_ref, wm_ref,
                     dres_ref, dmt_ref, dg_ref, da_ref, gain_grad_ref):
    dn, values, scale = dn_ref[...], res_ref[...], scale_ref[...]
    weighted = dn * gain_ref[...]
    inner = jnp.mean(weighted * values, axis=-1, keepdims=True)
    gain_grad_ref[...] = jnp.broadcast_to(jnp.sum(dn * values * scale, axis=0, keepdims=True), gain_grad_ref.shape)
    dres = c_ref[...].astype(f32) + scale * weighted - values * (scale * scale * scale * inner)
    dres_ref[...] = dres
    low = dres.astype(bf16)
    transpose_into(dmt_ref, low)
    da_ref[...] = dot(low, wa_ref[...]).astype(bf16)
    for c in range(0, wm_ref.shape[1], 512):
        dg_ref[:, c : c + 512] = dot(low, wm_ref[:, c : c + 512]).astype(bf16)


def conv_back_kernel(dpre_ref, after_ref, tap_ref, keep_ref, dkv_ref, dx_ref, dshared_ref):
    rows = dpre_ref.shape[0]
    kv = dkv_ref.shape[1]
    dshared_ref[:, :kv] = dkv_ref[...]
    for c in range(0, rows, SPAN):
        keep = keep_ref[c : c + SPAN, :]
        for col in range(COLS):
            lanes = slice(col * LANE, (col + 1) * LANE)
            if c + SPAN < rows:
                window = dpre_ref[c : c + SPAN + 8, lanes]
            else:
                window = jnp.concatenate([dpre_ref[c : c + SPAN, lanes], after_ref[:, lanes]], axis=0)
            total = tap_ref[KCONV - 1 : KCONV, lanes] * window[:SPAN, :]
            for j in range(1, KCONV):
                total = total + tap_ref[KCONV - 1 - j : KCONV - j, lanes] * window[j : j + SPAN, :] * keep[:, j : j + 1]
            if col * LANE < INNER:
                dx_ref[c : c + SPAN, lanes] = total.astype(bf16)
            else:
                at = kv + col * LANE - INNER
                dshared_ref[c : c + SPAN, at : at + LANE] = total.astype(bf16)


def kv_back_kernel(cos_ref, sin_ref, own_ref, *refs):
    out_ref = refs[-1]
    total = own_ref[...]
    for ref in refs[:-1]:
        total = total + ref[...].astype(f32)
    kv_width = KVH * HD
    out_ref[:, :kv_width] = turn(total[:, :kv_width], cos_ref[...], -sin_ref[...]).astype(bf16)
    out_ref[:, kv_width:] = total[:, kv_width:].astype(bf16)


def simple_call(kernel, name, arrays, outs, flops=0):
    single = not isinstance(outs, tuple)
    shapes = (outs,) if single else outs
    size = sum(a.size * a.dtype.itemsize for a in arrays) + sum(a.size * a.dtype.itemsize for a in shapes)
    return pl.pallas_call(
        kernel,
        grid=(1,),
        out_shape=outs,
        in_specs=wholes(arrays),
        out_specs=whole(outs.shape) if single else tuple(wholes(outs)),
        compiler_params=params(56),
        cost_estimate=COST,
        name=name,
    )(*arrays)


def left_rows(index_ref, left_ref, half, side):
    rows = left_ref.shape[0] // NB
    order = [LOW.index(m) for m in SET_MASKS[side]]
    return jnp.concatenate([left_ref[block_rows(index_ref, 4 * half + m, rows), :] for m in order], axis=0)


def grad_kernel(plan, n_left, n_right, index_ref, *refs):
    lefts = refs[:n_left]
    rights = refs[n_left : n_left + n_right]
    sent_ref, kept_ref = refs[n_left + n_right :]
    for s in range(4):
        for half, out in ((1, sent_ref), (0, kept_ref)):
            cache = {}
            at = 0
            for left, right, width, kind in plan:
                if kind == "fixed":
                    value = rights[right][:, s * width : (s + 1) * width]
                elif kind == "all":
                    value = rights[right][...]
                else:
                    value = rights[right][:, part_columns(index_ref, s, width)]
                if left not in cache:
                    cache[left] = left_rows(index_ref, lefts[left], half, s // 2)
                result = dot(cache[left], value)
                out[s, :, :, at : at + width] = result.reshape(4, -1, width).astype(bf16)
                at += width


def weight_grads(index, lefts, rights, plan):
    rows = lefts[0].shape[0] // NB
    columns = sum(width for _, _, width, _ in plan)
    outs = (sds((4, 4, rows, columns), bf16),) * 2
    return pl.pallas_call(
        functools.partial(grad_kernel, plan, len(lefts), len(rights)),
        grid=(1,),
        out_shape=outs,
        in_specs=[SMEM] + wholes(lefts) + wholes(rights),
        out_specs=tuple(wholes(outs)),
        compiler_params=params(56),
        cost_estimate=COST,
        name="weight_grads",
    )(index, *lefts, *rights)


def ffn_kernel(index_ref, w_ref, n_ref, nt_ref, c_ref, ct_ref, res_ref, grad_ref, out_ref, dn_ref, acc_ref):
    s = pl.program_id(0)
    model = n_ref.shape[1]
    units = w_ref.shape[3] // 3

    def weight(k):
        return w_ref[:, 0, :, k * units : (k + 1) * units].reshape(model, units)

    @pl.when(s == 0)
    def _():
        acc_ref[...] = res_ref[...]
        dn_ref[...] = jnp.zeros_like(dn_ref)

    gate = dot(n_ref[...], weight(0))
    up = dot(n_ref[...], weight(1))
    dact = dot(c_ref[...], weight(2)).astype(bf16).astype(f32)
    sig = jax.nn.sigmoid(gate)
    silu = gate * sig
    act = (silu * up).astype(bf16)
    dgate = (dact * up * (sig * (1.0 + gate * (1.0 - sig)))).astype(bf16)
    dup = (dact * silu).astype(bf16)
    acc_ref[...] += dot(act, weight(2), NT)
    dn_ref[...] += dot(dgate, weight(0), NT) + dot(dup, weight(1), NT)
    grad_ref[:, :units] = dot(nt_ref[...], dgate).astype(bf16)
    grad_ref[:, units : 2 * units] = dot(nt_ref[...], dup).astype(bf16)
    grad_ref[:, 2 * units :] = dot(ct_ref[...], act).astype(bf16)

    @pl.when(s == pl.num_programs(0) - 1)
    def _():
        out_ref[...] = acc_ref[...].astype(bf16)


def ffn(index, weights, normed, normed_t, cot, cot_t, residual):
    nd, nt, rows, columns = weights.shape
    tokens, model = normed.shape
    arrays = (normed, normed_t, cot, cot_t, residual)
    return pl.pallas_call(
        ffn_kernel,
        grid_spec=pltpu.PrefetchScalarGridSpec(
            num_scalar_prefetch=1,
            grid=(nt,),
            in_specs=[pl.BlockSpec((nd, 1, rows, columns), lambda s, index: (0, index[8 + s], 0, 0))] + wholes(arrays),
            out_specs=(
                pl.BlockSpec((model, columns), lambda s, index: (0, s)),
                whole((tokens, model)),
                whole((tokens, model)),
            ),
            scratch_shapes=[pltpu.VMEM((tokens, model), f32)],
        ),
        out_shape=(sds((model, nt * columns), bf16), sds((tokens, model), bf16), sds((tokens, model), f32)),
        compiler_params=params(60),
        cost_estimate=COST,
        name="ffn",
    )(index, weights, *arrays)


def rms_back(d_normed, values, scale, gain):
    weighted = d_normed * gain
    inner = jnp.mean(weighted * values, axis=-1, keepdims=True)
    gain_grad = jnp.sum(d_normed * values * scale, axis=0)
    return scale * weighted - values * (scale * scale * scale * inner), gain_grad


def rope_tables(rows, start):
    half = HD // 2
    frequency = rope_base ** (-2.0 * jnp.arange(half, dtype=f32) / HD)
    angles = (start + jnp.arange(rows)).astype(f32)[:, None] * frequency[None, :]
    cosine, sine = jnp.cos(angles), jnp.sin(angles)
    return jnp.concatenate([cosine] * 4, axis=1), jnp.concatenate([-sine, sine] * 2, axis=1)


def per_device(
    mesh,
    hidden,
    segments,
    cotangent,
    norm_gain,
    ffn_gain,
    query_proj,
    key_proj,
    value_proj,
    attn_out_proj,
    gate_inner,
    input_inner,
    state_proj,
    step_proj,
    mamba_out,
    conv_weight,
    conv_bias,
    decay_log,
    skip_gain,
    step_bias,
    ffn_gate,
    ffn_up,
    ffn_down,
):
    ring = Ring(mesh)
    nt = ring.nt
    di, ti = lax.axis_index("dp"), lax.axis_index("tensor")
    rows, width = hidden.shape
    seq = segments.shape[1]
    hops = -(-(seq // 2 - 1) // rows)
    back = hops * rows
    segment = segments[0]
    kv_width = KVH * HD
    step_cols = step_proj.shape[1]

    block = di // ring.unit
    index = jnp.stack(
        [block ^ m for m in LOW] + [block ^ m ^ 1 for m in LOW] + [lax.rem(ti + nt - s, nt) for s in range(nt)]
    ).astype(jnp.int32)

    start = ti * rows
    normed, normed_t, cot_t, scale1 = simple_call(
        norm_kernel,
        "norm_in",
        (hidden, cotangent, norm_gain[None, :]),
        (sds((rows, width), bf16), sds((width, rows), bf16), sds((width, rows), bf16), sds((rows, 1), f32)),
    )
    halo = ring.line(normed[rows - HALO :], 1)
    cosine, sine = rope_tables(rows, start)

    step_wide = jnp.zeros((step_proj.shape[0], LANE), bf16)
    step_wide = lax.dynamic_update_slice(step_wide, step_proj, (0, ti * step_cols))
    shared = jnp.concatenate([key_proj, value_proj, state_proj], axis=1)
    quarter = shared.shape[1] // nt
    shared_part = lax.dynamic_slice_in_dim(shared, ti * quarter, quarter, 1)
    widths1 = (query_proj.shape[1], LANE, input_inner.shape[1], quarter)
    widths2 = (gate_inner.shape[1], attn_out_proj.shape[0], mamba_out.shape[0])
    stages = {}

    def note(stage, values):
        stages[stage] = stages.get(stage, []) + list(values)
        return values

    def follow(stage, values):
        return after(values, *([stages[2]] if stage == 0 else [sides1] if stage == 1 else []))

    pack1 = pack((query_proj, step_wide, input_inner, shared_part), (False,) * 4)
    sides1 = ring.gather(pack1, note)
    pack2 = pack((gate_inner, attn_out_proj, mamba_out), (False, True, True))
    sides2 = ring.gather(pack2, follow)
    ffn_pack = pack((ffn_gate, ffn_up, ffn_down), (False, False, True))
    (ffn_pack,) = after([ffn_pack], *stages[FFN_AFTER]) if FFN_AFTER else [ffn_pack]
    w_ffn = lax.all_gather(ffn_pack, ("dp", "tensor"), axis=0, tiled=True)
    w_ffn = w_ffn.reshape(ring.nd, nt, *ffn_pack.shape)
    w_q, w_step, w_x, w_shared, u, query8, kv_own, dt_raw = project(
        index, sides1, widths1, (widths1[0] * nt, LANE, widths1[2] * nt, quarter * nt), normed, halo, cosine, sine
    )
    w_z, w_ao, w_mo = assemble(index, sides2, widths2, tuple(w * nt for w in widths2))

    padded = jnp.concatenate([jnp.full((back,), -1, jnp.int32), segment])
    seg_keys = lax.dynamic_slice_in_dim(padded, start, back + rows)
    seg_own = seg_keys[back:]
    seg_col, seg_row = seg_own[:, None], seg_own[None, :]
    chunks = rows // SPAN
    grouped = seg_own.reshape(chunks, SPAN)
    before = jnp.concatenate([seg_keys[back - 1 : back], grouped[:-1, -1]])
    carry_in = (grouped == before[:, None]).astype(f32).reshape(rows)
    in_last = (grouped == grouped[:, -1:]).astype(f32).reshape(rows)
    keeps = [(seg_keys[back - j : back - j + rows] == seg_own).astype(f32) for j in range(KCONV)]
    zero = jnp.zeros((rows,), f32)
    meta = jnp.stack(keeps + [carry_in, in_last, zero, zero], axis=1)
    first_tokens = seg_own.reshape(rows // QB, QB)[:, 0]
    doc_start = jnp.sum((segment[None, :] < first_tokens[:, None]).astype(jnp.int32), axis=1)
    first_block = (jnp.maximum(doc_start - (start - back), 0) // KB).astype(jnp.int32)

    seg_after = jnp.concatenate([segment, jnp.full((KCONV,), -2, jnp.int32)])
    keeps_after = [(lax.dynamic_slice_in_dim(seg_after, start + j, rows) == seg_own).astype(f32) for j in range(KCONV)]
    keeps_after = jnp.stack(keeps_after + [zero] * 4, axis=1)
    kvs = [ring.line(kv_own, s) for s in range(hops, 0, -1)] + [kv_own]

    taps = jnp.concatenate([conv_weight, conv_bias[None, :], jnp.zeros((3, INNER + 2 * NS), f32)], axis=0)
    rate = -jnp.exp(decay_log)
    heads = jnp.pad(jnp.stack([step_bias, rate]), ((0, 6), (0, LANE - MH)))
    skip = jnp.broadcast_to(jnp.repeat(skip_gain, MP)[None, :], (8, INNER))
    spread = np.arange(LANE)[:, None] == np.arange(INNER)[None, :] // MP
    spread2 = jnp.asarray(np.concatenate([spread, spread], axis=0), bf16)
    gather2 = jnp.asarray(np.concatenate([spread.T, spread.T], axis=0), bf16)

    mix, dt, cum, cumt, ec, fw, g, final = mamba_pre(u, taps, meta, dt_raw, heads, spread2)
    carries = [ring.line(final, s) for s in range(1, hops + 1)]
    attended, lse = attn_fwd(first_block, query8, seg_row, seg_keys[:, None], kvs)
    z_gate = dot(normed, w_z)
    gated, full, states = mamba_fwd(
        mix, dt, cum, cumt, ec, fw, g, seg_col, seg_row, z_gate, skip, spread2, carries
    )
    residual, normed2, normed2_t, scale2 = simple_call(
        middle_kernel,
        "middle",
        (attended, gated, w_ao, w_mo, hidden, ffn_gain[None, :]),
        (sds((rows, width), f32), sds((rows, width), bf16), sds((width, rows), bf16), sds((rows, 1), f32)),
        2 * rows * width * (INNER + QH * HD),
    )

    ffn_grads, output, d_normed2 = ffn(index, w_ffn, normed2, normed2_t, cotangent, cot_t, residual)
    ffn_grads = lax.psum_scatter(ffn_grads, "dp", scatter_dimension=0, tiled=True)
    units = ffn_gate.shape[1]
    g_ffn = ring.total([ffn_grads[:, s * 3 * units : (s + 1) * 3 * units] for s in range(nt)])
    d_residual, d_mixer_t, d_gated, d_attended, ffn_gain_grad = simple_call(
        after_ffn_kernel,
        "after_ffn",
        (d_normed2, residual, scale2, ffn_gain[None, :], cotangent, w_ao, w_mo),
        (sds((rows, width), f32), sds((width, rows), bf16), sds((rows, INNER), bf16), sds((rows, QH * HD), bf16),
         sds((8, width), f32)),
        2 * rows * width * (INNER + QH * HD),
    )
    ffn_gain_grad = ffn_gain_grad[0]

    dy, d_z, back_state = mamba_bpre(d_gated, z_gate, full, mix, ec, g, spread2)
    d_carries = [ring.line(back_state, -s) for s in range(1, hops + 1)]
    d_q, *d_kvs = attn_bwd(
        first_block, query8, d_attended, attended, lse, seg_row, seg_keys[:, None], cosine, sine, kvs
    )
    came = [ring.line(d_kvs[hops - s], -s) for s in range(1, hops + 1)]
    d_kv = simple_call(kv_back_kernel, "kv_back", (cosine, sine, d_kvs[-1], *came), sds(kv_own.shape, bf16))

    plan2 = (
        (0, 0, widths2[1], "part"),
        (0, 1, widths2[2], "part"),
        (1, 2, widths2[0], "part"),
        (1, 3, widths1[0], "part"),
    )
    grads2 = ring.collect(
        ring.scatter(*weight_grads(index, (d_mixer_t, normed_t), (attended, gated, d_z, d_q), plan2))
    )

    d_pre, d_step, conv_grads, small = mamba_bwd(
        mix, dt, cum, cumt, ec, fw, g, seg_col, seg_row, dy, states, u, taps, meta, skip, heads, spread2, gather2, d_carries
    )
    d_after = ring.line(d_pre[:8], -1)
    d_x, d_shared = simple_call(
        conv_back_kernel,
        "conv_back",
        (d_pre, d_after, taps, keeps_after, d_kv),
        (sds((rows, INNER), bf16), sds((rows, quarter * nt), bf16)),
    )

    d_x, d_shared = after([d_x, d_shared], ffn_grads)
    plan1 = ((0, 0, widths1[2], "part"), (0, 1, LANE, "all"), (0, 2, quarter, "fixed"))
    parts = ring.scatter(*weight_grads(index, (normed_t,), (d_x, d_step, d_shared), plan1))
    common = widths1[2] + LANE
    shared_sum = jnp.concatenate([part[:, common:] for part in parts], axis=1)
    shared_sum = ring.unblock(shared_sum)
    piece = shared_sum.shape[0] // nt
    parts = [part[:, :common] for part in parts]
    rows_of = []
    for s in range(nt):
        mine = lax.dynamic_slice_in_dim(shared_sum, lax.rem(ti + nt - s, nt) * piece, piece, 0)
        rows_of.append(jnp.concatenate([mine[:, i * quarter : (i + 1) * quarter] for i in range(nt)], axis=0))
    if ring.unit == 1:
        total = ring.total([jnp.concatenate(both, axis=1) for both in zip(parts, rows_of)])
        grads1, g_shared = total[:, :common], total[:, common:]
    else:
        grads1, g_shared = ring.collect(parts), ring.total(rows_of)
    g_shared = jnp.concatenate([g_shared[i * piece : (i + 1) * piece] for i in range(nt)], axis=1)

    d_normed = (
        dot(d_q, w_q, NT) + dot(d_z, w_z, NT) + dot(d_x, w_x, NT) + dot(d_shared, w_shared, NT) + dot(d_step, w_step, NT)
    )
    d_hid_norm, norm_gain_grad = rms_back(d_normed, hidden.astype(f32), scale1, norm_gain[None, :])
    hidden_grad = d_residual + d_hid_norm

    pieces = [norm_gain_grad, ffn_gain_grad, conv_grads[: KCONV + 1].reshape(-1), small[:3, :MH].reshape(-1)]
    vector = jnp.concatenate(pieces)
    size = vector.shape[0]
    vector = jnp.pad(vector, (0, -size % 1024)).reshape(-1, LANE)
    vector = ring.all_sum(vector).reshape(-1)
    at = 2 * width
    conv_sum = vector[at : at + (KCONV + 1) * (INNER + 2 * NS)].reshape(KCONV + 1, INNER + 2 * NS)
    small_sum = vector[size - 3 * MH : size].reshape(3, MH)

    def cut(value, *sizes):
        outs, at = [], 0
        for size in sizes:
            outs.append(value[:, at : at + size])
            at += size
        return outs

    g_fg, g_fu, g_fd = cut(g_ffn, units, units, units)
    g_ao, g_mo, g_z, g_q = cut(grads2, widths2[1], widths2[2], widths2[0], widths1[0])
    g_x, g_step_wide = cut(grads1, widths1[2], LANE)
    g_step = lax.dynamic_slice_in_dim(g_step_wide, ti * step_cols, step_cols, 1)
    return (
        output,
        hidden_grad,
        vector[:width],
        vector[width : 2 * width],
        g_q,
        g_shared[:, :kv_width],
        g_shared[:, kv_width : 2 * kv_width],
        g_ao.T,
        g_z,
        g_x,
        g_shared[:, 2 * kv_width :],
        g_step,
        g_mo.T,
        conv_sum[:KCONV],
        conv_sum[KCONV],
        small_sum[0],
        small_sum[1],
        small_sum[2],
        g_fg,
        g_fu,
        g_fd.T,
    )


def solution(mesh):
    in_specs = (
        P(("dp", "tensor"), None),
        P("dp", None),
        P(("dp", "tensor"), None),
        P(),
        P(),
        P("dp", "tensor"),
        P("dp", None),
        P("dp", None),
        P("tensor", "dp"),
        P("dp", "tensor"),
        P("dp", "tensor"),
        P("dp", None),
        P("dp", "tensor"),
        P("tensor", "dp"),
        P(),
        P(),
        P(),
        P(),
        P(),
        P("dp", "tensor"),
        P("dp", "tensor"),
        P("tensor", "dp"),
    )
    out_specs = (
        P(("dp", "tensor"), None),
        P(("dp", "tensor"), None),
        P(),
        P(),
        P("dp", "tensor"),
        P(("dp", "tensor"), None),
        P(("dp", "tensor"), None),
        P("tensor", "dp"),
        P("dp", "tensor"),
        P("dp", "tensor"),
        P(("dp", "tensor"), None),
        P("dp", "tensor"),
        P("tensor", "dp"),
        P(),
        P(),
        P(),
        P(),
        P(),
        P("dp", "tensor"),
        P("dp", "tensor"),
        P("tensor", "dp"),
    )
    return jax.shard_map(
        functools.partial(per_device, mesh), mesh=mesh, in_specs=in_specs, out_specs=out_specs, check_vma=False
    )
```

```python
import functools

import jax
import jax.numpy as jnp
import numpy as np
from jax import lax
from jax.experimental import pallas as pl
from jax.experimental.pallas import tpu as pltpu
from jax.sharding import PartitionSpec as P

QH = 8
KVH = 2
HD = 64
MH = 24
MP = 64
NS = 128
KCONV = 4
GROUP = QH // KVH
INNER = MH * MP
SPAN = 128
HALO = 16
LANE = 128
QB = 128
KB = 256
NEG = -1e30
FFN_AFTER = 1
COST = pl.CostEstimate(flops=2_000_000_000, bytes_accessed=4_000_000, transcendentals=0)

epsilon = 1e-05
rope_base = 100000000000.0
f32 = jnp.float32
bf16 = jnp.bfloat16

NN = (((1,), (0,)), ((), ()))
NT = (((1,), (1,)), ((), ()))
TN = (((0,), (0,)), ((), ()))


def dot(a, b, dims=NN):
    return lax.dot_general(a, b, dims, preferred_element_type=f32)


def split2(v, axis=1):
    hi = v.astype(bf16)
    lo = (v - hi.astype(f32)).astype(bf16)
    return jnp.concatenate([hi, lo], axis=axis)


def params(mb):
    return pltpu.CompilerParams(vmem_limit_bytes=mb * 1024 * 1024)


def sds(shape, dtype):
    return jax.ShapeDtypeStruct(shape, dtype)


def whole(shape):
    return pl.BlockSpec(shape, lambda *_: (0,) * len(shape), pipeline_mode=pl.Buffered(1))


def wholes(arrays):
    return [whole(a.shape) for a in arrays]


def attn_keep(segk_ref, segq_ref, off, i, back):
    pos_k = lax.broadcasted_iota(jnp.int32, (KB, QB), 0) + off
    pos_q = lax.broadcasted_iota(jnp.int32, (KB, QB), 1) + (back + i * QB)
    same = segk_ref[pl.ds(off, KB), :] == segq_ref[:, i * QB : (i + 1) * QB]
    return same & (pos_k <= pos_q)


def head_columns(g):
    return [slice(c * HD, (c + 2) * HD) for c in range(g * GROUP, (g + 1) * GROUP, 2)]


def stack_heads(ref, i, columns):
    rows = slice(i * QB, (i + 1) * QB)
    heads = []
    for at in columns:
        pair = ref[rows, at]
        heads += [pair[:, :HD], pair[:, HD:]]
    return jnp.concatenate(heads, axis=0)


def turn(v, cosine, sine):
    lane = lax.broadcasted_iota(jnp.int32, v.shape, 1)
    swapped = jnp.where(lane % HD < HD // 2, pltpu.roll(v, LANE - HD // 2, 1), pltpu.roll(v, HD // 2, 1))
    return v * cosine + swapped * sine


def load_pairs(pair_ref, kv_refs, at):
    rows = kv_refs[0].shape[0]
    for n, ref in enumerate(kv_refs):
        both = ref[:, at : at + KVH * HD]
        for g in range(KVH):
            pair_ref[g, n * rows : (n + 1) * rows, :] = both[:, g * HD : (g + 1) * HD]


def attn_fwd_kernel(first_ref, q_ref, segq_ref, segk_ref, *refs):
    kv_refs, (o_ref, lse_ref, k_ref, vt_ref) = refs[:-4], refs[-4:]
    rows = q_ref.shape[0]
    back = k_ref.shape[1] - rows
    wide = GROUP * QB
    load_pairs(k_ref, kv_refs, 0)
    for n, ref in enumerate(kv_refs):
        vt_ref[:, n * rows : (n + 1) * rows] = ref[:, KVH * HD :].astype(f32).T.astype(bf16)
    for i in range(rows // QB):
        last = (back + (i + 1) * QB + KB - 1) // KB
        for g in range(KVH):
            columns = head_columns(g)
            queries = stack_heads(q_ref, i, columns)

            def body(j, carry):
                top, total, acc = carry
                off = pl.multiple_of(j * KB, KB)
                scores = dot(k_ref[g, pl.ds(off, KB), :], queries, NT)
                keep = attn_keep(segk_ref, segq_ref, off, i, back)
                keep = jnp.concatenate([keep] * GROUP, axis=1)
                scores = jnp.where(keep, scores, NEG)
                new_top = jnp.maximum(top, jnp.max(scores, axis=0, keepdims=True))
                scale = jnp.exp(top - new_top)
                probs = jnp.exp(scores - new_top)
                total = total * scale + jnp.sum(probs, axis=0, keepdims=True)
                vt = vt_ref[g * HD : (g + 1) * HD, pl.ds(off, KB)]
                acc = acc * scale + dot(vt, probs.astype(bf16))
                return new_top, total, acc

            start = (jnp.full((1, wide), NEG, f32), jnp.zeros((1, wide), f32), jnp.zeros((HD, wide), f32))
            top, total, acc = lax.fori_loop(first_ref[i], last, body, start)
            lse_ref[i * KVH + g : i * KVH + g + 1, :] = top + jnp.log(total)
            acc = acc / total
            for h in range(0, GROUP, 2):
                pair = jnp.concatenate(
                    [acc[:, h * QB : (h + 1) * QB], acc[:, (h + 1) * QB : (h + 2) * QB]], axis=0
                ).T
                o_ref[i * QB : (i + 1) * QB, columns[h // 2]] = pair.astype(bf16)


def attn_bwd_kernel(first_ref, q_ref, do_ref, o_ref, lse_ref, segq_ref, segk_ref, cos_ref, sin_ref, *refs):
    n_kv = (len(refs) - 5) // 2
    kv_refs, dq_ref, dkv_refs = refs[:n_kv], refs[n_kv], refs[n_kv + 1 : 2 * n_kv + 1]
    k_ref, v_ref, dk_ref, dv_ref = refs[2 * n_kv + 1 :]
    rows = q_ref.shape[0]
    back = k_ref.shape[1] - rows
    wide = GROUP * QB
    load_pairs(k_ref, kv_refs, 0)
    load_pairs(v_ref, kv_refs, KVH * HD)
    dk_ref[...] = jnp.zeros_like(dk_ref)
    dv_ref[...] = jnp.zeros_like(dv_ref)
    for i in range(rows // QB):
        last = (back + (i + 1) * QB + KB - 1) // KB
        here = slice(i * QB, (i + 1) * QB)
        for g in range(KVH):
            columns = head_columns(g)
            queries = stack_heads(q_ref, i, columns)
            grads = stack_heads(do_ref, i, columns)
            outs = stack_heads(o_ref, i, columns)
            prod = grads.astype(f32) * outs.astype(f32)
            ones = jnp.ones((8, 2 * HD), bf16)
            delta = dot(ones, split2(prod), NT)[0:1, :]
            lse = lse_ref[i * KVH + g : i * KVH + g + 1, :]

            def body(j, acc):
                off = pl.multiple_of(j * KB, KB)
                keys = k_ref[g, pl.ds(off, KB), :]
                vals = v_ref[g, pl.ds(off, KB), :]
                keep = attn_keep(segk_ref, segq_ref, off, i, back)
                keep = jnp.concatenate([keep] * GROUP, axis=1)
                scores = jnp.where(keep, dot(keys, queries, NT), NEG)
                probs = jnp.exp(scores - lse)
                dprobs = dot(vals, grads, NT)
                dscores = (probs * (dprobs - delta)).astype(bf16)
                dv_ref[g, pl.ds(off, KB), :] += dot(probs.astype(bf16), grads)
                dk_ref[g, pl.ds(off, KB), :] += dot(dscores, queries)
                return acc + dot(keys, dscores, TN)

            acc = lax.fori_loop(first_ref[i], last, body, jnp.zeros((HD, wide), f32))
            acc = acc * (HD ** -0.5)
            for h in range(0, GROUP, 2):
                pair = jnp.concatenate(
                    [acc[:, h * QB : (h + 1) * QB], acc[:, (h + 1) * QB : (h + 2) * QB]], axis=0
                ).T
                pair = turn(pair.astype(bf16).astype(f32), cos_ref[here, :], -sin_ref[here, :])
                dq_ref[here, columns[h // 2]] = pair.astype(bf16)
    for n, out in enumerate(dkv_refs):
        span = slice(n * rows, (n + 1) * rows)
        for at, ref in ((0, dk_ref), (KVH * HD, dv_ref)):
            both = jnp.concatenate([ref[g, span, :] for g in range(KVH)], axis=1)
            out[:, at : at + KVH * HD] = both.astype(out.dtype)


SMEM = pl.BlockSpec(memory_space=pltpu.SMEM)


def attn_fwd(first, q, segq, segk, kvs):
    rows = q.shape[0]
    total = rows * len(kvs)
    arrays = (q, segq, segk, *kvs)
    outs = (sds(q.shape, bf16), sds((rows // QB * KVH, GROUP * QB), f32))
    return pl.pallas_call(
        attn_fwd_kernel,
        grid=(1,),
        out_shape=outs,
        in_specs=[SMEM] + wholes(arrays),
        out_specs=tuple(wholes(outs)),
        scratch_shapes=[pltpu.VMEM((KVH, total, HD), bf16), pltpu.VMEM((KVH * HD, total), bf16)],
        compiler_params=params(40),
        cost_estimate=COST,
        name="attn_fwd",
    )(first, *arrays)


def attn_bwd(first, q, do, o, lse, segq, segk, cosine, sine, kvs):
    total = q.shape[0] * len(kvs)
    arrays = (q, do, o, lse, segq, segk, cosine, sine, *kvs)
    outs = (sds(q.shape, bf16), *[sds(a.shape, bf16) for a in kvs[:-1]], sds(kvs[-1].shape, f32))
    return pl.pallas_call(
        attn_bwd_kernel,
        grid=(1,),
        out_shape=outs,
        in_specs=[SMEM] + wholes(arrays),
        out_specs=tuple(wholes(outs)),
        scratch_shapes=[pltpu.VMEM((KVH, total, HD), bf16)] * 2 + [pltpu.VMEM((KVH, total, HD), f32)] * 2,
        compiler_params=params(40),
        cost_estimate=COST,
        name="attn_bwd",
    )(first, *arrays)


COLS = (INNER + 2 * NS) // LANE


def tri_masks():
    t = lax.broadcasted_iota(jnp.int32, (SPAN, SPAN), 0)
    s = lax.broadcasted_iota(jnp.int32, (SPAN, SPAN), 1)
    return t, s


def widen(v, spread2):
    return dot(split2(v), spread2)


def store_carry(step, carry_ref, state_ref, keep_ref):
    @pl.when(step == pl.num_programs(0) - 1)
    def _():
        carry_ref[:NS, :] = state_ref[...].astype(bf16)
        keep = keep_ref[...]
        high = keep.astype(bf16)
        carry_ref[NS:, :] = jnp.concatenate([high, (keep - high.astype(f32)).astype(bf16)], axis=0)


def load_carry(near_ref, far_refs):
    state = near_ref[:NS, :].astype(f32)
    for far_ref in far_refs:
        kept = near_ref[NS : NS + 1, :].astype(f32) + near_ref[NS + 8 : NS + 9, :].astype(f32)
        state = state + far_ref[:NS, :].astype(f32) * kept
    return state


def conv_block(u_ref, tap_ref, meta, base, col):
    lanes = slice(col * LANE, (col + 1) * LANE)
    window = u_ref[pl.ds(base + HALO - 8, SPAN + 8), lanes]
    taps = [window[8:, :]]
    for j in range(1, KCONV):
        taps.append(window[8 - j : 8 - j + SPAN, :] * meta[:, j : j + 1])
    total = tap_ref[KCONV : KCONV + 1, lanes] + tap_ref[KCONV - 1 : KCONV, lanes] * taps[0]
    for j in range(1, KCONV):
        total = total + tap_ref[KCONV - 1 - j : KCONV - j, lanes] * taps[j]
    return taps, total


def mamba_pre_kernel(u_ref, tap_ref, meta_ref, dtr_ref, head_ref, spread_ref,
                     mix_ref, dt_ref, cum_ref, cumt_ref, ec_ref, fw_ref, g_ref, carry_ref, fin_ref, keep_ref):
    c = pl.program_id(0)
    base = pl.multiple_of(c * SPAN, SPAN)

    @pl.when(c == 0)
    def _():
        fin_ref[...] = jnp.zeros_like(fin_ref)
        keep_ref[...] = jnp.ones_like(keep_ref)

    meta = meta_ref[...]
    for col in range(COLS):
        total = conv_block(u_ref, tap_ref, meta, base, col)[1]
        mix_ref[:, col * LANE : (col + 1) * LANE] = (total * jax.nn.sigmoid(total)).astype(bf16)
    raw = dtr_ref[...] + head_ref[0:1, :]
    dt = jnp.maximum(raw, 0.0) + jnp.log1p(jnp.exp(-jnp.abs(raw)))
    decay = dt * head_ref[1:2, :]
    t, s = tri_masks()
    lower = (t >= s).astype(f32)
    cum = lax.dot_general(lower, decay, NN, precision=lax.Precision.HIGHEST, preferred_element_type=f32)
    end = cum[SPAN - 1 : SPAN, :]
    ec = meta[:, 4:5] * jnp.exp(cum)
    fw = meta[:, 5:6] * jnp.exp(end - cum)
    gain = ec[SPAN - 1 : SPAN, :]
    dt_ref[...] = dt
    cum_ref[...] = cum
    cumt_ref[...] = cum.T[: cumt_ref.shape[0], :]
    ec_ref[...] = ec
    fw_ref[...] = fw
    gain8 = jnp.broadcast_to(gain, (8, LANE))
    g_ref[...] = gain8
    spread2 = spread_ref[...]
    weight = widen(fw * dt, spread2)
    x = mix_ref[:, :INNER].astype(f32)
    b = mix_ref[:, INNER : INNER + NS]
    gain_wide = widen(gain8, spread2)
    fin_ref[...] = fin_ref[...] * gain_wide[0:1, :] + dot(b, (x * weight).astype(bf16), TN)
    keep_ref[...] = keep_ref[...] * gain_wide
    store_carry(c, carry_ref, fin_ref, keep_ref)


def chunk_spec(width):
    return pl.BlockSpec((SPAN, width), lambda c: (c, 0))


def mamba_pre(u, taps, meta, dt_raw, heads, spread2):
    rows = meta.shape[0]
    n = rows // SPAN
    width = INNER + 2 * NS
    hl = 32
    return pl.pallas_call(
        mamba_pre_kernel,
        grid=(n,),
        in_specs=[whole(u.shape), whole(taps.shape), chunk_spec(8), chunk_spec(LANE), whole(heads.shape),
                  whole(spread2.shape)],
        out_specs=(chunk_spec(width), chunk_spec(LANE), chunk_spec(LANE), pl.BlockSpec((hl, SPAN), lambda c: (0, c)),
                   chunk_spec(LANE), chunk_spec(LANE), pl.BlockSpec((8, LANE), lambda c: (c, 0)), whole((NS + 16, INNER))),
        out_shape=(sds((rows, width), bf16), sds((rows, LANE), f32), sds((rows, LANE), f32), sds((hl, rows), f32),
                   sds((rows, LANE), f32), sds((rows, LANE), f32), sds((8 * n, LANE), f32),
                   sds((NS + 16, INNER), bf16)),
        scratch_shapes=[pltpu.VMEM((NS, INNER), f32), pltpu.VMEM((8, INNER), f32)],
        compiler_params=params(40),
        cost_estimate=COST,
        name="mamba_pre",
    )(u, taps, meta, dt_raw, heads, spread2)


def pair_halves(v):
    lane = lax.broadcasted_iota(jnp.int32, v.shape, 1)
    zero = jnp.zeros_like(v)
    return jnp.concatenate([jnp.where(lane < MP, v, zero), jnp.where(lane < MP, zero, v)], axis=0)


def mamba_fwd_kernel(mix_ref, dt_ref, cum_ref, cumt_ref, ec_ref, fw_ref, g_ref, segc_ref, segr_ref,
                     z_ref, skip_ref, spread_ref, *refs):
    carries, (gated_ref, full_ref, states_ref, state_ref) = refs[:-4], refs[-4:]
    c = pl.program_id(0)

    @pl.when(c == 0)
    def _():
        state_ref[...] = load_carry(carries[0], carries[1:])

    state = state_ref[...].astype(bf16)
    states_ref[0] = state
    spread2 = spread_ref[...]
    b = mix_ref[:, INNER : INNER + NS]
    cm = mix_ref[:, INNER + NS :]
    t, s = tri_masks()
    allowed = (segc_ref[...] == segr_ref[...]) & (t >= s)
    off = jnp.where(allowed, 0.0, NEG)
    affinity = dot(cm, b, NT)
    cum = cum_ref[...]
    dt = dt_ref[...]
    dt_wide = widen(dt, spread2)
    ec_wide = widen(ec_ref[...], spread2)
    carried = dot(cm, state) * ec_wide
    for p in range(MH // 2):
        lanes = slice(p * LANE, (p + 1) * LANE)
        x = mix_ref[:, lanes].astype(f32)
        pieces = []
        for h in (2 * p, 2 * p + 1):
            gap = cum[:, h : h + 1] - cumt_ref[h : h + 1, :] + off
            pieces.append((affinity * jnp.exp(gap)).astype(bf16))
        scaled = (x * dt_wide[:, lanes]).astype(bf16)
        y = dot(jnp.concatenate(pieces, axis=1), pair_halves(scaled)) + carried[:, lanes]
        y = y + skip_ref[0:1, lanes] * x
        z = z_ref[:, lanes]
        full_ref[:, lanes] = y.astype(bf16)
        gated_ref[:, lanes] = (y * (z * jax.nn.sigmoid(z))).astype(bf16)
    weight = widen(fw_ref[...] * dt, spread2)
    x = mix_ref[:, :INNER].astype(f32)
    gain = widen(g_ref[...], spread2)[0:1, :]
    state_ref[...] = state_ref[...] * gain + dot(b, (x * weight).astype(bf16), TN)


def mamba_fwd(mix, dt, cum, cumt, ec, fw, g, segc, segr, z, skip, spread2, carries):
    rows = mix.shape[0]
    n = rows // SPAN
    return pl.pallas_call(
        mamba_fwd_kernel,
        grid=(n,),
        in_specs=[chunk_spec(mix.shape[1]), chunk_spec(LANE), chunk_spec(LANE),
                  pl.BlockSpec((cumt.shape[0], SPAN), lambda c: (0, c)), chunk_spec(LANE), chunk_spec(LANE),
                  pl.BlockSpec((8, LANE), lambda c: (c, 0)), chunk_spec(1), pl.BlockSpec((1, SPAN), lambda c: (0, c)),
                  chunk_spec(INNER), whole(skip.shape), whole(spread2.shape), *wholes(carries)],
        out_specs=(chunk_spec(INNER), chunk_spec(INNER), pl.BlockSpec((1, NS, INNER), lambda c: (c, 0, 0))),
        out_shape=(sds((rows, INNER), bf16), sds((rows, INNER), bf16), sds((n, NS, INNER), bf16)),
        scratch_shapes=[pltpu.VMEM((NS, INNER), f32)],
        compiler_params=params(40),
        cost_estimate=COST,
        name="mamba_fwd",
    )(mix, dt, cum, cumt, ec, fw, g, segc, segr, z, skip, spread2, *carries)


def mamba_bpre_kernel(dg_ref, z_ref, full_ref, cm_ref, ec_ref, g_ref, spread_ref, dy_ref, dz_ref, carry_ref, back_ref, keep_ref):
    c = pl.program_id(0)

    @pl.when(c == 0)
    def _():
        back_ref[...] = jnp.zeros_like(back_ref)
        keep_ref[...] = jnp.ones_like(keep_ref)

    spread2 = spread_ref[...]
    z = z_ref[...]
    sig = jax.nn.sigmoid(z)
    dg = dg_ref[...].astype(f32)
    dy = dg * (z * sig)
    dy_ref[...] = dy.astype(bf16)
    dz_ref[...] = (dg * full_ref[...].astype(f32) * (sig * (1.0 + z * (1.0 - sig)))).astype(bf16)
    weighted = (dy * widen(ec_ref[...], spread2)).astype(bf16)
    gain_wide = widen(g_ref[...], spread2)
    back_ref[...] = back_ref[...] * gain_wide[0:1, :] + dot(cm_ref[...], weighted, TN)
    keep_ref[...] = keep_ref[...] * gain_wide
    store_carry(c, carry_ref, back_ref, keep_ref)


def mamba_bpre(dg, z, full, mix, ec, g, spread2):
    rows = dg.shape[0]
    n = rows // SPAN
    rev = lambda width, col=0: pl.BlockSpec((SPAN, width), lambda c: (n - 1 - c, col))
    return pl.pallas_call(
        mamba_bpre_kernel,
        grid=(n,),
        in_specs=[rev(INNER), rev(INNER), rev(INNER), rev(NS, (INNER + NS) // NS), rev(LANE),
                  pl.BlockSpec((8, LANE), lambda c: (n - 1 - c, 0)), whole(spread2.shape)],
        out_specs=(rev(INNER), rev(INNER), whole((NS + 16, INNER))),
        out_shape=(sds((rows, INNER), bf16), sds((rows, INNER), bf16), sds((NS + 16, INNER), bf16)),
        scratch_shapes=[pltpu.VMEM((NS, INNER), f32), pltpu.VMEM((8, INNER), f32)],
        compiler_params=params(40),
        cost_estimate=COST,
        name="mamba_bpre",
    )(dg, z, full, mix, ec, g, spread2)


def mamba_bwd_kernel(mix_ref, dt_ref, cum_ref, cumt_ref, ec_ref, fw_ref, g_ref, segc_ref, segr_ref,
                     dy_ref, states_ref, u_ref, tap_ref, meta_ref, skip_ref, head_ref, spread_ref, gather_ref, *refs):
    carries = refs[:-9]
    dpre_ref, ddt_ref, conv_ref, small_ref, dstate_ref, acc_ref, rows_ref, dx_ref, dbc_ref = refs[-9:]
    step = pl.program_id(0)
    c = pl.num_programs(0) - 1 - step
    base = pl.multiple_of(c * SPAN, SPAN)

    @pl.when(step == 0)
    def _():
        dstate_ref[...] = load_carry(carries[0], carries[1:])
        conv_ref[...] = jnp.zeros_like(conv_ref)
        small_ref[...] = jnp.zeros_like(small_ref)
        rows_ref[...] = jnp.zeros_like(rows_ref)

    spread2 = spread_ref[...]
    gather2 = gather_ref[...]
    b = mix_ref[:, INNER : INNER + NS]
    cm = mix_ref[:, INNER + NS :]
    cum = cum_ref[...]
    dt = dt_ref[...]
    dt_wide = widen(dt, spread2)
    s, t = tri_masks()
    allowed = (segc_ref[...] == segr_ref[...]) & (t >= s)
    off = jnp.where(allowed, 0.0, NEG)
    affinity = dot(b, cm, NT)
    acc_ref[...] = jnp.zeros_like(acc_ref)
    for p in range(MH // 2):
        lanes = slice(p * LANE, (p + 1) * LANE)
        x = mix_ref[:, lanes].astype(f32)
        scaled = (x * dt_wide[:, lanes]).astype(bf16)
        dy = dy_ref[:, lanes]
        dmix = dot(pair_halves(scaled), dy, NT)
        pieces = []
        total = None
        for q, h in enumerate((2 * p, 2 * p + 1)):
            gap = cumt_ref[h : h + 1, :] - cum[:, h : h + 1] + off
            decays = jnp.exp(gap)
            mixing = (affinity * decays).astype(bf16)
            pieces.append(mixing)
            dm = dmix[q * SPAN : (q + 1) * SPAN, :]
            rows_ref[h : h + 1, :] = jnp.sum(dm * mixing.astype(f32), axis=0, keepdims=True)
            part = dm * decays
            total = part if total is None else total + part
        acc_ref[...] += total
        dx_ref[:, lanes] = dot(jnp.concatenate(pieces, axis=1), pair_halves(dy))
    dscaled = dx_ref[...]
    x = mix_ref[:, :INNER].astype(f32)
    scaled = (x * dt_wide).astype(bf16).astype(f32)
    dy = dy_ref[...].astype(f32)
    dstate = dstate_ref[...]
    dstate_low = dstate.astype(bf16)
    state = states_ref[0]
    ec_wide = widen(ec_ref[...], spread2)
    fw_wide = widen(fw_ref[...], spread2)
    from_state = fw_wide * dot(b, dstate_low)
    carried = ec_wide * dot(cm, state)
    weighted_dy = (dy * ec_wide).astype(bf16)
    cols_sum = dot(split2(scaled * dscaled), gather2)
    carr_sum = dot(split2(dy * carried), gather2)
    fdf_sum = dot(split2(scaled * from_state), gather2)
    dxd = dscaled + from_state
    ddt_direct = dot(split2(x * dxd), gather2)
    skip_part = dot(split2(dy * x), gather2)
    gain = widen(g_ref[...], spread2)[0:1, :]
    state_dot = jnp.sum(dstate * state.astype(f32), axis=0, keepdims=True) * gain
    state_dot = dot(split2(jnp.broadcast_to(state_dot, (8, INNER))), gather2)[0:1, :]
    tt, ss = tri_masks()
    suffix = (ss >= tt).astype(bf16)
    prefix = (ss < tt).astype(bf16)
    suffix2 = jnp.concatenate([suffix, suffix], axis=1)
    dlog = dot(suffix2, split2(carr_sum - cols_sum, axis=0))
    dlog = dlog + dot(suffix2, split2(rows_ref[...]), NT)
    dlog = dlog + dot(jnp.concatenate([prefix, prefix], axis=1), split2(fdf_sum, axis=0)) + state_dot
    decay_rate = head_ref[1:2, :]
    ddt = (ddt_direct + dlog * decay_rate) * (1.0 - jnp.exp(-dt))
    ddt_ref[...] = ddt.astype(bf16)
    small_ref[0:1, :] += jnp.sum(dlog * dt, axis=0, keepdims=True) * decay_rate
    small_ref[1:2, :] += jnp.sum(skip_part, axis=0, keepdims=True)
    small_ref[2:3, :] += jnp.sum(ddt, axis=0, keepdims=True)
    dx_ref[...] = dxd * dt_wide + skip_ref[0:1, :] * dy
    daff = acc_ref[...]
    daff_low = daff.astype(bf16)
    fx = (scaled * fw_wide).astype(bf16)
    dbc_ref[:, :NS] = dot(daff_low, cm) + dot(fx, dstate_low, NT)
    dbc_ref[:, NS:] = dot(daff_low, b, TN) + dot(weighted_dy, state, NT)
    dstate_ref[...] = dstate * gain + dot(cm, weighted_dy, TN)
    meta = meta_ref[...]
    for col in range(COLS):
        lanes = slice(col * LANE, (col + 1) * LANE)
        taps, total = conv_block(u_ref, tap_ref, meta, base, col)
        sig = jax.nn.sigmoid(total)
        if col * LANE < INNER:
            dmixed = dx_ref[:, lanes]
        else:
            dmixed = dbc_ref[:, col * LANE - INNER : (col + 1) * LANE - INNER]
        dpre = dmixed * (sig * (1.0 + total * (1.0 - sig)))
        dpre_ref[:, lanes] = dpre
        for j in range(KCONV):
            conv_ref[KCONV - 1 - j : KCONV - j, lanes] += jnp.sum(dpre * taps[j], axis=0, keepdims=True)
        conv_ref[KCONV : KCONV + 1, lanes] += jnp.sum(dpre, axis=0, keepdims=True)


def mamba_bwd(mix, dt, cum, cumt, ec, fw, g, segc, segr, dy, states, u, taps, meta, skip, heads, spread2, gather2,
              carries):
    rows = mix.shape[0]
    n = rows // SPAN
    width = mix.shape[1]
    rev = lambda w: pl.BlockSpec((SPAN, w), lambda c: (n - 1 - c, 0))
    return pl.pallas_call(
        mamba_bwd_kernel,
        grid=(n,),
        in_specs=[rev(width), rev(LANE), rev(LANE),
                  pl.BlockSpec((cumt.shape[0], SPAN), lambda c: (0, n - 1 - c)), rev(LANE), rev(LANE),
                  pl.BlockSpec((8, LANE), lambda c: (n - 1 - c, 0)), rev(1),
                  pl.BlockSpec((1, SPAN), lambda c: (0, n - 1 - c)), rev(INNER),
                  pl.BlockSpec((1, NS, INNER), lambda c: (n - 1 - c, 0, 0)), whole(u.shape), whole(taps.shape),
                  rev(8), whole(skip.shape), whole(heads.shape), whole(spread2.shape), whole(gather2.shape),
                  *wholes(carries)],
        out_specs=(rev(width), rev(LANE), whole((8, width)), whole((8, LANE))),
        out_shape=(sds((rows, width), f32), sds((rows, LANE), bf16), sds((8, width), f32), sds((8, LANE), f32)),
        scratch_shapes=[pltpu.VMEM((NS, INNER), f32), pltpu.VMEM((SPAN, SPAN), f32), pltpu.VMEM((LANE, SPAN), f32),
                        pltpu.VMEM((SPAN, INNER), f32), pltpu.VMEM((SPAN, 2 * NS), f32)],
        compiler_params=params(56),
        cost_estimate=COST,
        name="mamba_bwd",
    )(mix, dt, cum, cumt, ec, fw, g, segc, segr, dy, states, u, taps, meta, skip, heads, spread2, gather2, *carries)


NB = 8
LOW = (0, 2, 4, 6)
ORDERS = ((2, 4), (4, 2))
SETS = ((0, 1), (2, 3))
SET_MASKS = ((0, 2, 4, 6), (0, 4, 2, 6))


class Ring:
    def __init__(self, mesh):
        self.nd = mesh.shape["dp"]
        self.nt = mesh.shape["tensor"]
        self.unit = self.nd // NB
        base = range(0, self.nd, self.unit)
        self.groups = [[b + i for i in range(self.unit)] for b in base]

    def dp(self, value, mask):
        step = mask * self.unit
        return lax.ppermute(value, "dp", [(i, i ^ step) for i in range(self.nd)])

    def shift(self, value, s):
        n = self.nt
        return lax.ppermute(value, "tensor", [(i, (i + s) % n) for i in range(n)])

    def line(self, value, s):
        n = self.nt
        return lax.ppermute(value, "tensor", [(i, i + s) for i in range(n) if 0 <= i + s < n])

    def block(self, value):
        if self.unit == 1:
            return value
        return lax.all_gather(value, "dp", axis=0, tiled=True, axis_index_groups=self.groups)

    def unblock(self, value):
        if self.unit == 1:
            return value
        return lax.psum_scatter(value, "dp", scatter_dimension=0, tiled=True, axis_index_groups=self.groups)

    def gather(self, pack, hold=lambda stage, values: values):
        own = self.block(pack)
        (own,) = hold(0, [own])
        parts = [own] + [self.shift(own, s) for s in range(1, self.nt)]
        pairs = hold(1, [join([parts[s] for s in members]) for members in SETS])
        nears = [self.dp(pair, one) for pair, (one, _) in zip(pairs, ORDERS)]
        firsts = [
            join([parts[s] for s in members] + [near]) for members, near in zip(SETS, nears)
        ]
        firsts = hold(2, firsts)
        sides = [[first, self.dp(first, two)] for first, (_, two) in zip(firsts, ORDERS)]
        sides = [hold(3, side) for side in sides]
        return [[lows, [self.dp(low, 1) for low in lows]] for lows in sides]

    def scatter_sibling(self, sent, kept):
        came = self.dp(sent, 1)
        halves = []
        for n in range(2):
            here = slice(2 * n, 2 * n + 2)
            halves.append((add(kept[here, 2:], came[here, 2:]), add(kept[here, :2], came[here, :2])))
        return halves

    def scatter_first(self, halves):
        quarters = []
        for (out, mine), (_, axis) in zip(halves, ORDERS):
            got = self.dp(out, axis)
            quarters.append((add(mine[:, 1:], got[:, 1:]), add(mine[:, :1], got[:, :1])))
        return quarters

    def scatter_second(self, quarters):
        parts = []
        for (out, mine), (axis, _) in zip(quarters, ORDERS):
            got = self.dp(out, axis)
            parts += [add(mine[i, 0], got[i, 0]) for i in range(2)]
        return parts

    def total(self, parts):
        total = parts[0].astype(f32)
        for s in range(1, self.nt):
            total = total + self.shift(parts[s], self.nt - s).astype(f32)
        return total

    def collect(self, parts):
        return self.unblock(self.total(parts))

    def all_sum(self, value):
        bit = 1
        while bit < self.nd:
            value = value + lax.ppermute(value, "dp", [(i, i ^ bit) for i in range(self.nd)])
            bit *= 2
        return value + sum(self.shift(value, s) for s in range(1, self.nt))


def after(values, *others):
    return lax.optimization_barrier((tuple(values), others))[0]


def add(a, b):
    return (a.astype(f32) + b.astype(f32)).astype(bf16)


def join_kernel(*refs):
    out = refs[-1]
    if len(out.shape) == 3:
        for i, ref in enumerate(refs[:-1]):
            out[i] = ref[...]
    else:
        for i, ref in enumerate(refs[:2]):
            out[0, i] = ref[...]
        out[1] = refs[2][...]


def join(pieces):
    rows, cols = pieces[0].shape
    shape = (2, rows, cols) if len(pieces) == 2 else (2, 2, rows, cols)
    return pl.pallas_call(
        join_kernel,
        grid=(1,),
        out_shape=sds(shape, bf16),
        in_specs=wholes(pieces),
        out_specs=whole(shape),
        compiler_params=params(40),
        cost_estimate=COST,
        name="join",
    )(*pieces)


def block_rows(index_ref, at, rows):
    return pl.ds(pl.multiple_of(index_ref[at] * rows, rows), rows)


def part_columns(index_ref, s, width):
    return pl.ds(pl.multiple_of(index_ref[8 + s] * width, width), width)


def assemble_kernel(widths, index_ref, *refs):
    buffers, outs = refs[:8], refs[8:]
    rows = buffers[0].shape[2]
    for n in range(2):
        for half in range(2):
            for k in range(4):
                buffer = buffers[4 * n + 2 * half + k // 2]
                m = LOW.index(SET_MASKS[n][k])
                here = block_rows(index_ref, 4 * half + m, rows)
                for i in range(2):
                    at = 0
                    for width, out in zip(widths, outs):
                        piece = buffer[k % 2, i, :, at : at + width]
                        at += width
                        if out.shape[1] == width:
                            out[here, :] = piece if n + i == 0 else out[here, :] + piece
                        else:
                            out[here, part_columns(index_ref, 2 * n + i, width)] = piece


def assemble(index, sides, widths, totals):
    buffers = [buffer for side in sides for lows in side for buffer in lows]
    model = NB * buffers[0].shape[2]
    outs = tuple(sds((model, total), bf16) for total in totals)
    return pl.pallas_call(
        functools.partial(assemble_kernel, widths),
        grid=(1,),
        out_shape=outs,
        in_specs=[SMEM] + wholes(buffers),
        out_specs=tuple(wholes(outs)),
        compiler_params=params(48),
        cost_estimate=COST,
        name="assemble",
    )(index, *buffers)


def project_kernel(widths, index_ref, *refs):
    buffers, (normed_ref, halo_ref, cos_ref, sin_ref) = refs[:8], refs[8:12]
    weights, (u_ref, q_ref, kv_ref, dt_ref) = refs[12:16], refs[16:]
    assemble_kernel(widths, index_ref, *buffers, *weights)
    w_q, w_step, w_x, w_shared = weights
    kv_width = KVH * HD
    half = normed_ref.shape[0] // 2
    for r in range(2):
        here = slice(r * half, (r + 1) * half)
        normed = normed_ref[here, :]
        cosine, sine = cos_ref[here, :], sin_ref[here, :]
        kv = dot(normed, w_shared[:, : 2 * kv_width])
        kv_ref[here, :kv_width] = turn(kv[:, :kv_width], cosine, sine).astype(bf16)
        kv_ref[here, kv_width:] = kv[:, kv_width:].astype(bf16)
        q = dot(normed, w_q[...])
        for c in range(0, q.shape[1], LANE):
            tile = turn(q[:, c : c + LANE], cosine, sine).astype(bf16)
            q_ref[here, c : c + LANE] = tile * jnp.asarray(HD ** -0.5, bf16)
        dt_ref[here, :] = dot(normed, w_step[...])
        below = slice(HALO + r * half, HALO + (r + 1) * half)
        u_ref[below, INNER:] = dot(normed, w_shared[:, 2 * kv_width :])
        for c in range(0, INNER, 512):
            u_ref[below, c : c + 512] = dot(normed, w_x[:, c : c + 512])
    u_ref[:HALO, INNER:] = dot(halo_ref[...], w_shared[:, 2 * kv_width :])
    for c in range(0, INNER, 512):
        u_ref[:HALO, c : c + 512] = dot(halo_ref[...], w_x[:, c : c + 512])


def project(index, sides, widths, totals, normed, halo, cosine, sine):
    buffers = [buffer for side in sides for lows in side for buffer in lows]
    rows, model = normed.shape
    arrays = (*buffers, normed, halo, cosine, sine)
    outs = tuple(sds((model, total), bf16) for total in totals)
    outs += (sds((HALO + rows, INNER + 2 * NS), f32), sds((rows, QH * HD), bf16), sds((rows, 2 * KVH * HD), bf16),
             sds((rows, LANE), f32))
    return pl.pallas_call(
        functools.partial(project_kernel, widths),
        grid=(1,),
        out_shape=outs,
        in_specs=[SMEM] + wholes(arrays),
        out_specs=tuple(wholes(outs)),
        compiler_params=params(56),
        cost_estimate=COST,
        name="project",
    )(index, *arrays)


def transpose_into(out_ref, values):
    for c in range(0, values.shape[1], LANE):
        out_ref[c : c + LANE, :] = values[:, c : c + LANE].astype(f32).T.astype(bf16)


def norm_kernel(h_ref, c_ref, gain_ref, n_ref, nt_ref, ct_ref, scale_ref):
    values = h_ref[...].astype(f32)
    scale = lax.rsqrt(jnp.mean(values * values, axis=-1, keepdims=True) + epsilon)
    scale_ref[...] = scale
    n_ref[...] = (values * scale * gain_ref[...]).astype(bf16)
    transpose_into(nt_ref, n_ref[...])
    transpose_into(ct_ref, c_ref[...])


def pack_kernel(flips, *refs):
    out, at = refs[-1], 0
    for flip, ref in zip(flips, refs[:-1]):
        if flip:
            count = ref.shape[0]
            for r in range(0, count, LANE):
                out[:, at + r : at + r + LANE] = ref[r : r + LANE, :].astype(f32).T.astype(bf16)
        else:
            count = ref.shape[1]
            out[:, at : at + count] = ref[...]
        at += count


def pack(arrays, flips):
    rows = arrays[0].shape[0]
    columns = sum(a.shape[0] if flip else a.shape[1] for a, flip in zip(arrays, flips))
    return simple_call(functools.partial(pack_kernel, flips), "pack", tuple(arrays), sds((rows, columns), bf16))


def middle_kernel(att_ref, gated_ref, wa_ref, wm_ref, h_ref, gain_ref, res_ref, n_ref, nt_ref, scale_ref):
    model = h_ref.shape[1]
    for c in range(0, model, 256):
        cols = slice(c, c + 256)
        mixer = dot(att_ref[...], wa_ref[cols, :], NT) + dot(gated_ref[...], wm_ref[cols, :], NT)
        res_ref[:, cols] = h_ref[:, cols].astype(f32) + mixer
    values = res_ref[...]
    scale = lax.rsqrt(jnp.mean(values * values, axis=-1, keepdims=True) + epsilon)
    scale_ref[...] = scale
    n_ref[...] = (values * scale * gain_ref[...]).astype(bf16)
    transpose_into(nt_ref, n_ref[...])


def after_ffn_kernel(dn_ref, res_ref, scale_ref, gain_ref, c_ref, wa_ref, wm_ref,
                     dres_ref, dmt_ref, dg_ref, da_ref, gain_grad_ref):
    dn, values, scale = dn_ref[...], res_ref[...], scale_ref[...]
    weighted = dn * gain_ref[...]
    inner = jnp.mean(weighted * values, axis=-1, keepdims=True)
    gain_grad_ref[...] = jnp.broadcast_to(jnp.sum(dn * values * scale, axis=0, keepdims=True), gain_grad_ref.shape)
    dres = c_ref[...].astype(f32) + scale * weighted - values * (scale * scale * scale * inner)
    dres_ref[...] = dres
    low = dres.astype(bf16)
    transpose_into(dmt_ref, low)
    da_ref[...] = dot(low, wa_ref[...]).astype(bf16)
    for c in range(0, wm_ref.shape[1], 512):
        dg_ref[:, c : c + 512] = dot(low, wm_ref[:, c : c + 512]).astype(bf16)


def conv_back_kernel(dpre_ref, after_ref, tap_ref, keep_ref, dkv_ref, dx_ref, dshared_ref):
    rows = dpre_ref.shape[0]
    kv = dkv_ref.shape[1]
    dshared_ref[:, :kv] = dkv_ref[...]
    for c in range(0, rows, SPAN):
        keep = keep_ref[c : c + SPAN, :]
        for col in range(COLS):
            lanes = slice(col * LANE, (col + 1) * LANE)
            if c + SPAN < rows:
                window = dpre_ref[c : c + SPAN + 8, lanes]
            else:
                window = jnp.concatenate([dpre_ref[c : c + SPAN, lanes], after_ref[:, lanes]], axis=0)
            total = tap_ref[KCONV - 1 : KCONV, lanes] * window[:SPAN, :]
            for j in range(1, KCONV):
                total = total + tap_ref[KCONV - 1 - j : KCONV - j, lanes] * window[j : j + SPAN, :] * keep[:, j : j + 1]
            if col * LANE < INNER:
                dx_ref[c : c + SPAN, lanes] = total.astype(bf16)
            else:
                at = kv + col * LANE - INNER
                dshared_ref[c : c + SPAN, at : at + LANE] = total.astype(bf16)


def kv_back_kernel(cos_ref, sin_ref, own_ref, *refs):
    out_ref = refs[-1]
    total = own_ref[...]
    for ref in refs[:-1]:
        total = total + ref[...].astype(f32)
    kv_width = KVH * HD
    out_ref[:, :kv_width] = turn(total[:, :kv_width], cos_ref[...], -sin_ref[...]).astype(bf16)
    out_ref[:, kv_width:] = total[:, kv_width:].astype(bf16)


def simple_call(kernel, name, arrays, outs, flops=0):
    single = not isinstance(outs, tuple)
    shapes = (outs,) if single else outs
    size = sum(a.size * a.dtype.itemsize for a in arrays) + sum(a.size * a.dtype.itemsize for a in shapes)
    return pl.pallas_call(
        kernel,
        grid=(1,),
        out_shape=outs,
        in_specs=wholes(arrays),
        out_specs=whole(outs.shape) if single else tuple(wholes(outs)),
        compiler_params=params(56),
        cost_estimate=COST,
        name=name,
    )(*arrays)


def left_rows(index_ref, left_ref, half, side):
    rows = left_ref.shape[0] // NB
    order = [LOW.index(m) for m in SET_MASKS[side]]
    return jnp.concatenate([left_ref[block_rows(index_ref, 4 * half + m, rows), :] for m in order], axis=0)


def grad_kernel(plan, n_left, n_right, index_ref, *refs):
    lefts = refs[:n_left]
    rights = refs[n_left : n_left + n_right]
    sent_ref, kept_ref = refs[n_left + n_right :]
    for s in range(4):
        for half, out in ((1, sent_ref), (0, kept_ref)):
            cache = {}
            at = 0
            for left, right, width, kind in plan:
                if kind == "fixed":
                    value = rights[right][:, s * width : (s + 1) * width]
                elif kind == "all":
                    value = rights[right][...]
                else:
                    value = rights[right][:, part_columns(index_ref, s, width)]
                if left not in cache:
                    cache[left] = left_rows(index_ref, lefts[left], half, s // 2)
                result = dot(cache[left], value)
                out[s, :, :, at : at + width] = result.reshape(4, -1, width).astype(bf16)
                at += width


def weight_grads(index, lefts, rights, plan):
    rows = lefts[0].shape[0] // NB
    columns = sum(width for _, _, width, _ in plan)
    outs = (sds((4, 4, rows, columns), bf16),) * 2
    return pl.pallas_call(
        functools.partial(grad_kernel, plan, len(lefts), len(rights)),
        grid=(1,),
        out_shape=outs,
        in_specs=[SMEM] + wholes(lefts) + wholes(rights),
        out_specs=tuple(wholes(outs)),
        compiler_params=params(56),
        cost_estimate=COST,
        name="weight_grads",
    )(index, *lefts, *rights)


def ffn_kernel(index_ref, w_ref, n_ref, nt_ref, c_ref, ct_ref, res_ref, grad_ref, out_ref, dn_ref, acc_ref):
    s = pl.program_id(0)
    model = n_ref.shape[1]
    units = w_ref.shape[3] // 3

    def weight(k):
        return w_ref[:, 0, :, k * units : (k + 1) * units].reshape(model, units)

    @pl.when(s == 0)
    def _():
        acc_ref[...] = res_ref[...]
        dn_ref[...] = jnp.zeros_like(dn_ref)

    gate = dot(n_ref[...], weight(0))
    up = dot(n_ref[...], weight(1))
    dact = dot(c_ref[...], weight(2)).astype(bf16).astype(f32)
    sig = jax.nn.sigmoid(gate)
    silu = gate * sig
    act = (silu * up).astype(bf16)
    dgate = (dact * up * (sig * (1.0 + gate * (1.0 - sig)))).astype(bf16)
    dup = (dact * silu).astype(bf16)
    acc_ref[...] += dot(act, weight(2), NT)
    dn_ref[...] += dot(dgate, weight(0), NT) + dot(dup, weight(1), NT)
    grad_ref[:, :units] = dot(nt_ref[...], dgate).astype(bf16)
    grad_ref[:, units : 2 * units] = dot(nt_ref[...], dup).astype(bf16)
    grad_ref[:, 2 * units :] = dot(ct_ref[...], act).astype(bf16)

    @pl.when(s == pl.num_programs(0) - 1)
    def _():
        out_ref[...] = acc_ref[...].astype(bf16)


def ffn(index, weights, normed, normed_t, cot, cot_t, residual):
    nd, nt, rows, columns = weights.shape
    tokens, model = normed.shape
    arrays = (normed, normed_t, cot, cot_t, residual)
    return pl.pallas_call(
        ffn_kernel,
        grid_spec=pltpu.PrefetchScalarGridSpec(
            num_scalar_prefetch=1,
            grid=(nt,),
            in_specs=[pl.BlockSpec((nd, 1, rows, columns), lambda s, index: (0, index[8 + s], 0, 0))] + wholes(arrays),
            out_specs=(
                pl.BlockSpec((model, columns), lambda s, index: (0, index[8 + s])),
                whole((tokens, model)),
                whole((tokens, model)),
            ),
            scratch_shapes=[pltpu.VMEM((tokens, model), f32)],
        ),
        out_shape=(sds((model, nt * columns), bf16), sds((tokens, model), bf16), sds((tokens, model), f32)),
        compiler_params=params(60),
        cost_estimate=COST,
        name="ffn",
    )(index, weights, *arrays)


def rms_back(d_normed, values, scale, gain):
    weighted = d_normed * gain
    inner = jnp.mean(weighted * values, axis=-1, keepdims=True)
    gain_grad = jnp.sum(d_normed * values * scale, axis=0)
    return scale * weighted - values * (scale * scale * scale * inner), gain_grad


def rope_tables(rows, start):
    half = HD // 2
    frequency = rope_base ** (-2.0 * jnp.arange(half, dtype=f32) / HD)
    angles = (start + jnp.arange(rows)).astype(f32)[:, None] * frequency[None, :]
    cosine, sine = jnp.cos(angles), jnp.sin(angles)
    return jnp.concatenate([cosine] * 4, axis=1), jnp.concatenate([-sine, sine] * 2, axis=1)


def per_device(
    mesh,
    hidden,
    segments,
    cotangent,
    norm_gain,
    ffn_gain,
    query_proj,
    key_proj,
    value_proj,
    attn_out_proj,
    gate_inner,
    input_inner,
    state_proj,
    step_proj,
    mamba_out,
    conv_weight,
    conv_bias,
    decay_log,
    skip_gain,
    step_bias,
    ffn_gate,
    ffn_up,
    ffn_down,
):
    ring = Ring(mesh)
    nt = ring.nt
    di, ti = lax.axis_index("dp"), lax.axis_index("tensor")
    rows, width = hidden.shape
    seq = segments.shape[1]
    hops = -(-(seq // 2 - 1) // rows)
    back = hops * rows
    segment = segments[0]
    kv_width = KVH * HD
    step_cols = step_proj.shape[1]

    block = di // ring.unit
    index = jnp.stack(
        [block ^ m for m in LOW] + [block ^ m ^ 1 for m in LOW] + [lax.rem(ti + nt - s, nt) for s in range(nt)]
    ).astype(jnp.int32)

    start = ti * rows
    normed, normed_t, cot_t, scale1 = simple_call(
        norm_kernel,
        "norm_in",
        (hidden, cotangent, norm_gain[None, :]),
        (sds((rows, width), bf16), sds((width, rows), bf16), sds((width, rows), bf16), sds((rows, 1), f32)),
    )
    halo = ring.line(normed[rows - HALO :], 1)
    cosine, sine = rope_tables(rows, start)

    step_wide = jnp.zeros((step_proj.shape[0], LANE), bf16)
    step_wide = lax.dynamic_update_slice(step_wide, step_proj, (0, ti * step_cols))
    shared = jnp.concatenate([key_proj, value_proj, state_proj], axis=1)
    quarter = shared.shape[1] // nt
    shared_part = lax.dynamic_slice_in_dim(shared, ti * quarter, quarter, 1)
    widths1 = (query_proj.shape[1], LANE, input_inner.shape[1], quarter)
    widths2 = (gate_inner.shape[1], attn_out_proj.shape[0], mamba_out.shape[0])
    stages = {}

    def note(stage, values):
        if stage == 1:
            values = after(values, normed)
        if stage == 3:
            values = after(values, halo)
        stages[stage] = stages.get(stage, []) + list(values)
        return values

    pack1 = pack((query_proj, step_wide, input_inner, shared_part), (False,) * 4)
    sides1 = ring.gather(pack1, note)
    pack2 = pack((gate_inner, attn_out_proj, mamba_out), (False, True, True))
    ffn_pack = pack((ffn_gate, ffn_up, ffn_down), (False, False, True))
    (ffn_pack,) = after([ffn_pack], *stages[FFN_AFTER]) if FFN_AFTER else [ffn_pack]
    w_ffn = lax.all_gather(ffn_pack, ("dp", "tensor"), axis=0, tiled=True)
    w_ffn = w_ffn.reshape(ring.nd, nt, *ffn_pack.shape)
    w_q, w_step, w_x, w_shared, u, query8, kv_own, dt_raw = project(
        index, sides1, widths1, (widths1[0] * nt, LANE, widths1[2] * nt, quarter * nt), normed, halo, cosine, sine
    )
    padded = jnp.concatenate([jnp.full((back,), -1, jnp.int32), segment])
    seg_keys = lax.dynamic_slice_in_dim(padded, start, back + rows)
    seg_own = seg_keys[back:]
    seg_col, seg_row = seg_own[:, None], seg_own[None, :]
    chunks = rows // SPAN
    grouped = seg_own.reshape(chunks, SPAN)
    before = jnp.concatenate([seg_keys[back - 1 : back], grouped[:-1, -1]])
    carry_in = (grouped == before[:, None]).astype(f32).reshape(rows)
    in_last = (grouped == grouped[:, -1:]).astype(f32).reshape(rows)
    keeps = [(seg_keys[back - j : back - j + rows] == seg_own).astype(f32) for j in range(KCONV)]
    zero = jnp.zeros((rows,), f32)
    meta = jnp.stack(keeps + [carry_in, in_last, zero, zero], axis=1)
    first_tokens = seg_own.reshape(rows // QB, QB)[:, 0]
    doc_start = jnp.sum((segment[None, :] < first_tokens[:, None]).astype(jnp.int32), axis=1)
    first_block = (jnp.maximum(doc_start - (start - back), 0) // KB).astype(jnp.int32)

    seg_after = jnp.concatenate([segment, jnp.full((KCONV,), -2, jnp.int32)])
    keeps_after = [(lax.dynamic_slice_in_dim(seg_after, start + j, rows) == seg_own).astype(f32) for j in range(KCONV)]
    keeps_after = jnp.stack(keeps_after + [zero] * 4, axis=1)
    kvs = [ring.line(kv_own, s) for s in range(hops, 0, -1)] + [kv_own]

    waits = {0: (stages[1],), 1: (kv_own,)}

    def hold(stage, values):
        return after(values, *waits[stage])

    (own2,) = hold(0, [ring.block(pack2)])
    parts2 = [own2] + [ring.shift(own2, s) for s in range(1, nt)]
    pairs2 = hold(1, [join([parts2[s] for s in members]) for members in SETS])
    nears2 = [ring.dp(pair, one) for pair, (one, _) in zip(pairs2, ORDERS)]
    (u,) = after([u], pairs2)
    taps = jnp.concatenate([conv_weight, conv_bias[None, :], jnp.zeros((3, INNER + 2 * NS), f32)], axis=0)
    rate = -jnp.exp(decay_log)
    heads = jnp.pad(jnp.stack([step_bias, rate]), ((0, 6), (0, LANE - MH)))
    skip = jnp.broadcast_to(jnp.repeat(skip_gain, MP)[None, :], (8, INNER))
    spread = np.arange(LANE)[:, None] == np.arange(INNER)[None, :] // MP
    spread2 = jnp.asarray(np.concatenate([spread, spread], axis=0), bf16)
    gather2 = jnp.asarray(np.concatenate([spread.T, spread.T], axis=0), bf16)

    mix, dt, cum, cumt, ec, fw, g, final = mamba_pre(u, taps, meta, dt_raw, heads, spread2)
    firsts2 = after([join([parts2[s] for s in members] + [near]) for members, near in zip(SETS, nears2)], mix, kvs)
    sides2 = [[first, ring.dp(first, two)] for first, (_, two) in zip(firsts2, ORDERS)]
    (query8,) = after([query8], *firsts2)
    carries = [ring.line(final, s) for s in range(1, hops + 1)]
    attended, lse = attn_fwd(first_block, query8, seg_row, seg_keys[:, None], kvs)
    waits[3] = (attended, carries)
    sides2 = [[lows, [ring.dp(low, 1) for low in lows]] for lows in [hold(3, side) for side in sides2]]
    w_z, w_ao, w_mo = assemble(index, sides2, widths2, tuple(w * nt for w in widths2))
    z_gate = dot(normed, w_z)
    gated, full, states = mamba_fwd(
        mix, dt, cum, cumt, ec, fw, g, seg_col, seg_row, z_gate, skip, spread2, carries
    )
    residual, normed2, normed2_t, scale2 = simple_call(
        middle_kernel,
        "middle",
        (attended, gated, w_ao, w_mo, hidden, ffn_gain[None, :]),
        (sds((rows, width), f32), sds((rows, width), bf16), sds((width, rows), bf16), sds((rows, 1), f32)),
        2 * rows * width * (INNER + QH * HD),
    )

    ffn_grads, output, d_normed2 = ffn(index, w_ffn, normed2, normed2_t, cotangent, cot_t, residual)
    ffn_grads = lax.psum_scatter(ffn_grads, "dp", scatter_dimension=0, tiled=True)
    units = ffn_gate.shape[1]
    g_ffn = lax.psum_scatter(ffn_grads, "tensor", scatter_dimension=1, tiled=True).astype(f32)
    d_residual, d_mixer_t, d_gated, d_attended, ffn_gain_grad = simple_call(
        after_ffn_kernel,
        "after_ffn",
        (d_normed2, residual, scale2, ffn_gain[None, :], cotangent, w_ao, w_mo),
        (sds((rows, width), f32), sds((width, rows), bf16), sds((rows, INNER), bf16), sds((rows, QH * HD), bf16),
         sds((8, width), f32)),
        2 * rows * width * (INNER + QH * HD),
    )
    ffn_gain_grad = ffn_gain_grad[0]

    dy, d_z, back_state = mamba_bpre(d_gated, z_gate, full, mix, ec, g, spread2)
    d_carries = [ring.line(back_state, -s) for s in range(1, hops + 1)]
    d_q, *d_kvs = attn_bwd(
        first_block, query8, d_attended, attended, lse, seg_row, seg_keys[:, None], cosine, sine, kvs
    )
    came = [ring.line(d_kvs[hops - s], -s) for s in range(1, hops + 1)]
    def kv_back(own):
        return simple_call(kv_back_kernel, "kv_back", (cosine, sine, own, *came), sds(kv_own.shape, bf16))


    plan2 = (
        (0, 0, widths2[1], "part"),
        (0, 1, widths2[2], "part"),
        (1, 2, widths2[0], "part"),
        (1, 3, widths1[0], "part"),
    )
    (d_q2,) = after([d_q], *d_carries)
    sent2, kept2 = weight_grads(index, (d_mixer_t, normed_t), (attended, gated, d_z, d_q2), plan2)
    (dy,) = after([dy], sent2)

    d_pre, d_step, conv_grads, small = mamba_bwd(
        mix, dt, cum, cumt, ec, fw, g, seg_col, seg_row, dy, states, u, taps, meta, skip, heads, spread2, gather2, d_carries
    )
    kept2, own_kv = after([kept2, d_kvs[-1]], d_pre)
    d_kv = kv_back(own_kv)
    halves2 = ring.scatter_sibling(sent2, kept2)
    d_after = ring.line(d_pre[:8], -1)
    d_x, d_shared = simple_call(
        conv_back_kernel,
        "conv_back",
        (d_pre, d_after, *after([taps], halves2, ffn_grads), keeps_after, d_kv),
        (sds((rows, INNER), bf16), sds((rows, quarter * nt), bf16)),
    )

    plan1 = ((0, 0, widths1[2], "part"), (0, 1, LANE, "all"), (0, 2, quarter, "fixed"))
    sent1, kept1 = weight_grads(index, (normed_t,), (d_x, d_step, d_shared), plan1)
    quarters2 = ring.scatter_first([(out, after([mine], sent1)[0]) for out, mine in halves2])
    halves1 = ring.scatter_sibling(sent1, after([kept1], quarters2)[0])
    parts2 = ring.scatter_second([(out, after([mine], halves1)[0]) for out, mine in quarters2])
    quarters1 = ring.scatter_first([(out, after([mine], parts2)[0]) for out, mine in halves1])
    grads2 = ring.collect(after(parts2[:1], quarters1) + tuple(parts2[1:]))
    parts = ring.scatter_second(quarters1)
    common = widths1[2] + LANE
    shared_sum = jnp.concatenate([part[:, common:] for part in parts], axis=1)
    shared_sum = ring.unblock(shared_sum)
    piece = shared_sum.shape[0] // nt
    parts = [part[:, :common] for part in parts]
    rows_of = []
    for s in range(nt):
        mine = lax.dynamic_slice_in_dim(shared_sum, lax.rem(ti + nt - s, nt) * piece, piece, 0)
        rows_of.append(jnp.concatenate([mine[:, i * quarter : (i + 1) * quarter] for i in range(nt)], axis=0))
    if ring.unit == 1:
        total = ring.total([jnp.concatenate(both, axis=1) for both in zip(parts, rows_of)])
        grads1, g_shared = total[:, :common], total[:, common:]
    else:
        grads1, g_shared = ring.collect(parts), ring.total(rows_of)
    g_shared = jnp.concatenate([g_shared[i * piece : (i + 1) * piece] for i in range(nt)], axis=1)

    d_q, d_x, d_z = after([d_q, d_x, d_z], halves1)
    d_normed = (
        dot(d_q, w_q, NT) + dot(d_z, w_z, NT) + dot(d_x, w_x, NT) + dot(d_shared, w_shared, NT) + dot(d_step, w_step, NT)
    )
    d_hid_norm, norm_gain_grad = rms_back(d_normed, hidden.astype(f32), scale1, norm_gain[None, :])
    hidden_grad = d_residual + d_hid_norm

    pieces = [norm_gain_grad, ffn_gain_grad, conv_grads[: KCONV + 1].reshape(-1), small[:3, :MH].reshape(-1)]
    vector = jnp.concatenate(pieces)
    size = vector.shape[0]
    vector = jnp.pad(vector, (0, -size % 1024)).reshape(-1, LANE)
    vector = ring.all_sum(vector).reshape(-1)
    at = 2 * width
    conv_sum = vector[at : at + (KCONV + 1) * (INNER + 2 * NS)].reshape(KCONV + 1, INNER + 2 * NS)
    small_sum = vector[size - 3 * MH : size].reshape(3, MH)

    def cut(value, *sizes):
        outs, at = [], 0
        for size in sizes:
            outs.append(value[:, at : at + size])
            at += size
        return outs

    g_fg, g_fu, g_fd = cut(g_ffn, units, units, units)
    g_ao, g_mo, g_z, g_q = cut(grads2, widths2[1], widths2[2], widths2[0], widths1[0])
    g_x, g_step_wide = cut(grads1, widths1[2], LANE)
    g_step = lax.dynamic_slice_in_dim(g_step_wide, ti * step_cols, step_cols, 1)
    return (
        output,
        hidden_grad,
        vector[:width],
        vector[width : 2 * width],
        g_q,
        g_shared[:, :kv_width],
        g_shared[:, kv_width : 2 * kv_width],
        g_ao.T,
        g_z,
        g_x,
        g_shared[:, 2 * kv_width :],
        g_step,
        g_mo.T,
        conv_sum[:KCONV],
        conv_sum[KCONV],
        small_sum[0],
        small_sum[1],
        small_sum[2],
        g_fg,
        g_fu,
        g_fd.T,
    )


def solution(mesh):
    in_specs = (
        P(("dp", "tensor"), None),
        P("dp", None),
        P(("dp", "tensor"), None),
        P(),
        P(),
        P("dp", "tensor"),
        P("dp", None),
        P("dp", None),
        P("tensor", "dp"),
        P("dp", "tensor"),
        P("dp", "tensor"),
        P("dp", None),
        P("dp", "tensor"),
        P("tensor", "dp"),
        P(),
        P(),
        P(),
        P(),
        P(),
        P("dp", "tensor"),
        P("dp", "tensor"),
        P("tensor", "dp"),
    )
    out_specs = (
        P(("dp", "tensor"), None),
        P(("dp", "tensor"), None),
        P(),
        P(),
        P("dp", "tensor"),
        P(("dp", "tensor"), None),
        P(("dp", "tensor"), None),
        P("tensor", "dp"),
        P("dp", "tensor"),
        P("dp", "tensor"),
        P(("dp", "tensor"), None),
        P("dp", "tensor"),
        P("tensor", "dp"),
        P(),
        P(),
        P(),
        P(),
        P(),
        P("dp", "tensor"),
        P("dp", "tensor"),
        P("tensor", "dp"),
    )
    return jax.shard_map(
        functools.partial(per_device, mesh), mesh=mesh, in_specs=in_specs, out_specs=out_specs, check_vma=False
    )
```

```python
import functools

import jax
import jax.numpy as jnp
import numpy as np
from jax import lax
from jax.experimental import pallas as pl
from jax.experimental.pallas import tpu as pltpu
from jax.sharding import PartitionSpec as P

QH = 8
KVH = 2
HD = 64
MH = 24
MP = 64
NS = 128
KCONV = 4
GROUP = QH // KVH
INNER = MH * MP
SPAN = 128
HALO = 16
LANE = 128
QB = 128
KB = 256
NEG = -1e30
FFN_AFTER = 1
COST = pl.CostEstimate(flops=2_000_000_000, bytes_accessed=4_000_000, transcendentals=0)

epsilon = 1e-05
rope_base = 100000000000.0
f32 = jnp.float32
bf16 = jnp.bfloat16

NN = (((1,), (0,)), ((), ()))
NT = (((1,), (1,)), ((), ()))
TN = (((0,), (0,)), ((), ()))


def dot(a, b, dims=NN):
    return lax.dot_general(a, b, dims, preferred_element_type=f32)


def split2(v, axis=1):
    hi = v.astype(bf16)
    lo = (v - hi.astype(f32)).astype(bf16)
    return jnp.concatenate([hi, lo], axis=axis)


def params(mb):
    return pltpu.CompilerParams(vmem_limit_bytes=mb * 1024 * 1024)


def sds(shape, dtype):
    return jax.ShapeDtypeStruct(shape, dtype)


def whole(shape):
    return pl.BlockSpec(shape, lambda *_: (0,) * len(shape), pipeline_mode=pl.Buffered(1))


def wholes(arrays):
    return [whole(a.shape) for a in arrays]


def attn_keep(segk_ref, segq_ref, off, i, back):
    pos_k = lax.broadcasted_iota(jnp.int32, (KB, QB), 0) + off
    pos_q = lax.broadcasted_iota(jnp.int32, (KB, QB), 1) + (back + i * QB)
    same = segk_ref[pl.ds(off, KB), :] == segq_ref[:, i * QB : (i + 1) * QB]
    return same & (pos_k <= pos_q)


def head_columns(g):
    return [slice(c * HD, (c + 2) * HD) for c in range(g * GROUP, (g + 1) * GROUP, 2)]


def stack_heads(ref, i, columns):
    rows = slice(i * QB, (i + 1) * QB)
    heads = []
    for at in columns:
        pair = ref[rows, at]
        heads += [pair[:, :HD], pair[:, HD:]]
    return jnp.concatenate(heads, axis=0)


def turn(v, cosine, sine):
    lane = lax.broadcasted_iota(jnp.int32, v.shape, 1)
    swapped = jnp.where(lane % HD < HD // 2, pltpu.roll(v, LANE - HD // 2, 1), pltpu.roll(v, HD // 2, 1))
    return v * cosine + swapped * sine


def load_pairs(pair_ref, kv_refs, at):
    rows = kv_refs[0].shape[0]
    for n, ref in enumerate(kv_refs):
        both = ref[:, at : at + KVH * HD]
        for g in range(KVH):
            pair_ref[g, n * rows : (n + 1) * rows, :] = both[:, g * HD : (g + 1) * HD]


def attn_fwd_kernel(first_ref, q_ref, segq_ref, segk_ref, *refs):
    kv_refs, (o_ref, lse_ref, k_ref, vt_ref) = refs[:-4], refs[-4:]
    rows = q_ref.shape[0]
    back = k_ref.shape[1] - rows
    wide = GROUP * QB
    load_pairs(k_ref, kv_refs, 0)
    for n, ref in enumerate(kv_refs):
        vt_ref[:, n * rows : (n + 1) * rows] = ref[:, KVH * HD :].astype(f32).T.astype(bf16)
    for i in range(rows // QB):
        last = (back + (i + 1) * QB + KB - 1) // KB
        for g in range(KVH):
            columns = head_columns(g)
            queries = stack_heads(q_ref, i, columns)

            def body(j, carry):
                top, total, acc = carry
                off = pl.multiple_of(j * KB, KB)
                scores = dot(k_ref[g, pl.ds(off, KB), :], queries, NT)
                keep = attn_keep(segk_ref, segq_ref, off, i, back)
                keep = jnp.concatenate([keep] * GROUP, axis=1)
                scores = jnp.where(keep, scores, NEG)
                new_top = jnp.maximum(top, jnp.max(scores, axis=0, keepdims=True))
                scale = jnp.exp(top - new_top)
                probs = jnp.exp(scores - new_top)
                total = total * scale + jnp.sum(probs, axis=0, keepdims=True)
                vt = vt_ref[g * HD : (g + 1) * HD, pl.ds(off, KB)]
                acc = acc * scale + dot(vt, probs.astype(bf16))
                return new_top, total, acc

            start = (jnp.full((1, wide), NEG, f32), jnp.zeros((1, wide), f32), jnp.zeros((HD, wide), f32))
            top, total, acc = lax.fori_loop(first_ref[i], last, body, start)
            lse_ref[i * KVH + g : i * KVH + g + 1, :] = top + jnp.log(total)
            acc = acc / total
            for h in range(0, GROUP, 2):
                pair = jnp.concatenate(
                    [acc[:, h * QB : (h + 1) * QB], acc[:, (h + 1) * QB : (h + 2) * QB]], axis=0
                ).T
                o_ref[i * QB : (i + 1) * QB, columns[h // 2]] = pair.astype(bf16)


def attn_bwd_kernel(first_ref, q_ref, do_ref, o_ref, lse_ref, segq_ref, segk_ref, cos_ref, sin_ref, *refs):
    n_kv = (len(refs) - 5) // 2
    kv_refs, dq_ref, dkv_refs = refs[:n_kv], refs[n_kv], refs[n_kv + 1 : 2 * n_kv + 1]
    k_ref, v_ref, dk_ref, dv_ref = refs[2 * n_kv + 1 :]
    rows = q_ref.shape[0]
    back = k_ref.shape[1] - rows
    wide = GROUP * QB
    load_pairs(k_ref, kv_refs, 0)
    load_pairs(v_ref, kv_refs, KVH * HD)
    dk_ref[...] = jnp.zeros_like(dk_ref)
    dv_ref[...] = jnp.zeros_like(dv_ref)
    for i in range(rows // QB):
        last = (back + (i + 1) * QB + KB - 1) // KB
        here = slice(i * QB, (i + 1) * QB)
        for g in range(KVH):
            columns = head_columns(g)
            queries = stack_heads(q_ref, i, columns)
            grads = stack_heads(do_ref, i, columns)
            outs = stack_heads(o_ref, i, columns)
            prod = grads.astype(f32) * outs.astype(f32)
            ones = jnp.ones((8, 2 * HD), bf16)
            delta = dot(ones, split2(prod), NT)[0:1, :]
            lse = lse_ref[i * KVH + g : i * KVH + g + 1, :]

            def body(j, acc):
                off = pl.multiple_of(j * KB, KB)
                keys = k_ref[g, pl.ds(off, KB), :]
                vals = v_ref[g, pl.ds(off, KB), :]
                keep = attn_keep(segk_ref, segq_ref, off, i, back)
                keep = jnp.concatenate([keep] * GROUP, axis=1)
                scores = jnp.where(keep, dot(keys, queries, NT), NEG)
                probs = jnp.exp(scores - lse)
                dprobs = dot(vals, grads, NT)
                dscores = (probs * (dprobs - delta)).astype(bf16)
                dv_ref[g, pl.ds(off, KB), :] += dot(probs.astype(bf16), grads)
                dk_ref[g, pl.ds(off, KB), :] += dot(dscores, queries)
                return acc + dot(keys, dscores, TN)

            acc = lax.fori_loop(first_ref[i], last, body, jnp.zeros((HD, wide), f32))
            acc = acc * (HD ** -0.5)
            for h in range(0, GROUP, 2):
                pair = jnp.concatenate(
                    [acc[:, h * QB : (h + 1) * QB], acc[:, (h + 1) * QB : (h + 2) * QB]], axis=0
                ).T
                pair = turn(pair.astype(bf16).astype(f32), cos_ref[here, :], -sin_ref[here, :])
                dq_ref[here, columns[h // 2]] = pair.astype(bf16)
    for n, out in enumerate(dkv_refs):
        span = slice(n * rows, (n + 1) * rows)
        for at, ref in ((0, dk_ref), (KVH * HD, dv_ref)):
            both = jnp.concatenate([ref[g, span, :] for g in range(KVH)], axis=1)
            out[:, at : at + KVH * HD] = both.astype(out.dtype)


SMEM = pl.BlockSpec(memory_space=pltpu.SMEM)


def attn_fwd(first, q, segq, segk, kvs):
    rows = q.shape[0]
    total = rows * len(kvs)
    arrays = (q, segq, segk, *kvs)
    outs = (sds(q.shape, bf16), sds((rows // QB * KVH, GROUP * QB), f32))
    return pl.pallas_call(
        attn_fwd_kernel,
        grid=(1,),
        out_shape=outs,
        in_specs=[SMEM] + wholes(arrays),
        out_specs=tuple(wholes(outs)),
        scratch_shapes=[pltpu.VMEM((KVH, total, HD), bf16), pltpu.VMEM((KVH * HD, total), bf16)],
        compiler_params=params(40),
        cost_estimate=COST,
        name="attn_fwd",
    )(first, *arrays)


def attn_bwd(first, q, do, o, lse, segq, segk, cosine, sine, kvs):
    total = q.shape[0] * len(kvs)
    arrays = (q, do, o, lse, segq, segk, cosine, sine, *kvs)
    outs = (sds(q.shape, bf16), *[sds(a.shape, bf16) for a in kvs[:-1]], sds(kvs[-1].shape, f32))
    return pl.pallas_call(
        attn_bwd_kernel,
        grid=(1,),
        out_shape=outs,
        in_specs=[SMEM] + wholes(arrays),
        out_specs=tuple(wholes(outs)),
        scratch_shapes=[pltpu.VMEM((KVH, total, HD), bf16)] * 2 + [pltpu.VMEM((KVH, total, HD), f32)] * 2,
        compiler_params=params(40),
        cost_estimate=COST,
        name="attn_bwd",
    )(first, *arrays)


COLS = (INNER + 2 * NS) // LANE


def tri_masks():
    t = lax.broadcasted_iota(jnp.int32, (SPAN, SPAN), 0)
    s = lax.broadcasted_iota(jnp.int32, (SPAN, SPAN), 1)
    return t, s


def widen(v, spread2):
    return dot(split2(v), spread2)


def store_carry(step, carry_ref, state_ref, keep_ref):
    @pl.when(step == pl.num_programs(0) - 1)
    def _():
        carry_ref[:NS, :] = state_ref[...].astype(bf16)
        keep = keep_ref[...]
        high = keep.astype(bf16)
        carry_ref[NS:, :] = jnp.concatenate([high, (keep - high.astype(f32)).astype(bf16)], axis=0)


def load_carry(near_ref, far_refs):
    state = near_ref[:NS, :].astype(f32)
    for far_ref in far_refs:
        kept = near_ref[NS : NS + 1, :].astype(f32) + near_ref[NS + 8 : NS + 9, :].astype(f32)
        state = state + far_ref[:NS, :].astype(f32) * kept
    return state


def conv_block(u_ref, tap_ref, meta, base, col):
    lanes = slice(col * LANE, (col + 1) * LANE)
    window = u_ref[pl.ds(base + HALO - 8, SPAN + 8), lanes]
    taps = [window[8:, :]]
    for j in range(1, KCONV):
        taps.append(window[8 - j : 8 - j + SPAN, :] * meta[:, j : j + 1])
    total = tap_ref[KCONV : KCONV + 1, lanes] + tap_ref[KCONV - 1 : KCONV, lanes] * taps[0]
    for j in range(1, KCONV):
        total = total + tap_ref[KCONV - 1 - j : KCONV - j, lanes] * taps[j]
    return taps, total


def mamba_pre_kernel(u_ref, tap_ref, meta_ref, dtr_ref, head_ref, spread_ref,
                     mix_ref, dt_ref, cum_ref, cumt_ref, ec_ref, fw_ref, g_ref, carry_ref, fin_ref, keep_ref):
    c = pl.program_id(0)
    base = pl.multiple_of(c * SPAN, SPAN)

    @pl.when(c == 0)
    def _():
        fin_ref[...] = jnp.zeros_like(fin_ref)
        keep_ref[...] = jnp.ones_like(keep_ref)

    meta = meta_ref[...]
    for col in range(COLS):
        total = conv_block(u_ref, tap_ref, meta, base, col)[1]
        mix_ref[:, col * LANE : (col + 1) * LANE] = (total * jax.nn.sigmoid(total)).astype(bf16)
    raw = dtr_ref[...] + head_ref[0:1, :]
    dt = jnp.maximum(raw, 0.0) + jnp.log1p(jnp.exp(-jnp.abs(raw)))
    decay = dt * head_ref[1:2, :]
    t, s = tri_masks()
    lower = (t >= s).astype(f32)
    cum = lax.dot_general(lower, decay, NN, precision=lax.Precision.HIGHEST, preferred_element_type=f32)
    end = cum[SPAN - 1 : SPAN, :]
    ec = meta[:, 4:5] * jnp.exp(cum)
    fw = meta[:, 5:6] * jnp.exp(end - cum)
    gain = ec[SPAN - 1 : SPAN, :]
    dt_ref[...] = dt
    cum_ref[...] = cum
    cumt_ref[...] = cum.T[: cumt_ref.shape[0], :]
    ec_ref[...] = ec
    fw_ref[...] = fw
    gain8 = jnp.broadcast_to(gain, (8, LANE))
    g_ref[...] = gain8
    spread2 = spread_ref[...]
    weight = widen(fw * dt, spread2)
    x = mix_ref[:, :INNER].astype(f32)
    b = mix_ref[:, INNER : INNER + NS]
    gain_wide = widen(gain8, spread2)
    fin_ref[...] = fin_ref[...] * gain_wide[0:1, :] + dot(b, (x * weight).astype(bf16), TN)
    keep_ref[...] = keep_ref[...] * gain_wide
    store_carry(c, carry_ref, fin_ref, keep_ref)


def chunk_spec(width):
    return pl.BlockSpec((SPAN, width), lambda c: (c, 0))


def mamba_pre(u, taps, meta, dt_raw, heads, spread2):
    rows = meta.shape[0]
    n = rows // SPAN
    width = INNER + 2 * NS
    hl = 32
    return pl.pallas_call(
        mamba_pre_kernel,
        grid=(n,),
        in_specs=[whole(u.shape), whole(taps.shape), chunk_spec(8), chunk_spec(LANE), whole(heads.shape),
                  whole(spread2.shape)],
        out_specs=(chunk_spec(width), chunk_spec(LANE), chunk_spec(LANE), pl.BlockSpec((hl, SPAN), lambda c: (0, c)),
                   chunk_spec(LANE), chunk_spec(LANE), pl.BlockSpec((8, LANE), lambda c: (c, 0)), whole((NS + 16, INNER))),
        out_shape=(sds((rows, width), bf16), sds((rows, LANE), f32), sds((rows, LANE), f32), sds((hl, rows), f32),
                   sds((rows, LANE), f32), sds((rows, LANE), f32), sds((8 * n, LANE), f32),
                   sds((NS + 16, INNER), bf16)),
        scratch_shapes=[pltpu.VMEM((NS, INNER), f32), pltpu.VMEM((8, INNER), f32)],
        compiler_params=params(40),
        cost_estimate=COST,
        name="mamba_pre",
    )(u, taps, meta, dt_raw, heads, spread2)


def pair_halves(v):
    lane = lax.broadcasted_iota(jnp.int32, v.shape, 1)
    zero = jnp.zeros_like(v)
    return jnp.concatenate([jnp.where(lane < MP, v, zero), jnp.where(lane < MP, zero, v)], axis=0)


def mamba_fwd_kernel(mix_ref, dt_ref, cum_ref, cumt_ref, ec_ref, fw_ref, g_ref, segc_ref, segr_ref,
                     z_ref, skip_ref, spread_ref, *refs):
    carries, (gated_ref, full_ref, states_ref, state_ref) = refs[:-4], refs[-4:]
    c = pl.program_id(0)

    @pl.when(c == 0)
    def _():
        state_ref[...] = load_carry(carries[0], carries[1:])

    state = state_ref[...].astype(bf16)
    states_ref[0] = state
    spread2 = spread_ref[...]
    b = mix_ref[:, INNER : INNER + NS]
    cm = mix_ref[:, INNER + NS :]
    t, s = tri_masks()
    allowed = (segc_ref[...] == segr_ref[...]) & (t >= s)
    off = jnp.where(allowed, 0.0, NEG)
    affinity = dot(cm, b, NT)
    cum = cum_ref[...]
    dt = dt_ref[...]
    wide = widen(jnp.concatenate([dt, ec_ref[...], fw_ref[...] * dt, g_ref[...]], axis=0), spread2)
    dt_wide, ec_wide, weight = wide[:SPAN], wide[SPAN : 2 * SPAN], wide[2 * SPAN : 3 * SPAN]
    gain = wide[3 * SPAN : 3 * SPAN + 1]
    carried = dot(cm, state) * ec_wide
    for p in range(MH // 2):
        lanes = slice(p * LANE, (p + 1) * LANE)
        x = mix_ref[:, lanes].astype(f32)
        pieces = []
        for h in (2 * p, 2 * p + 1):
            gap = cum[:, h : h + 1] - cumt_ref[h : h + 1, :] + off
            pieces.append((affinity * jnp.exp(gap)).astype(bf16))
        scaled = (x * dt_wide[:, lanes]).astype(bf16)
        y = dot(jnp.concatenate(pieces, axis=1), pair_halves(scaled)) + carried[:, lanes]
        y = y + skip_ref[0:1, lanes] * x
        z = z_ref[:, lanes]
        full_ref[:, lanes] = y.astype(bf16)
        gated_ref[:, lanes] = (y * (z * jax.nn.sigmoid(z))).astype(bf16)
    x = mix_ref[:, :INNER].astype(f32)
    state_ref[...] = state_ref[...] * gain + dot(b, (x * weight).astype(bf16), TN)


def mamba_fwd(mix, dt, cum, cumt, ec, fw, g, segc, segr, z, skip, spread2, carries):
    rows = mix.shape[0]
    n = rows // SPAN
    return pl.pallas_call(
        mamba_fwd_kernel,
        grid=(n,),
        in_specs=[chunk_spec(mix.shape[1]), chunk_spec(LANE), chunk_spec(LANE),
                  pl.BlockSpec((cumt.shape[0], SPAN), lambda c: (0, c)), chunk_spec(LANE), chunk_spec(LANE),
                  pl.BlockSpec((8, LANE), lambda c: (c, 0)), chunk_spec(1), pl.BlockSpec((1, SPAN), lambda c: (0, c)),
                  chunk_spec(INNER), whole(skip.shape), whole(spread2.shape), *wholes(carries)],
        out_specs=(chunk_spec(INNER), chunk_spec(INNER), pl.BlockSpec((1, NS, INNER), lambda c: (c, 0, 0))),
        out_shape=(sds((rows, INNER), bf16), sds((rows, INNER), bf16), sds((n, NS, INNER), bf16)),
        scratch_shapes=[pltpu.VMEM((NS, INNER), f32)],
        compiler_params=params(40),
        cost_estimate=COST,
        name="mamba_fwd",
    )(mix, dt, cum, cumt, ec, fw, g, segc, segr, z, skip, spread2, *carries)


def mamba_bpre_kernel(dg_ref, z_ref, full_ref, cm_ref, ec_ref, g_ref, spread_ref, dy_ref, dz_ref, carry_ref, back_ref, keep_ref):
    c = pl.program_id(0)

    @pl.when(c == 0)
    def _():
        back_ref[...] = jnp.zeros_like(back_ref)
        keep_ref[...] = jnp.ones_like(keep_ref)

    spread2 = spread_ref[...]
    z = z_ref[...]
    sig = jax.nn.sigmoid(z)
    dg = dg_ref[...].astype(f32)
    dy = dg * (z * sig)
    dy_ref[...] = dy.astype(bf16)
    dz_ref[...] = (dg * full_ref[...].astype(f32) * (sig * (1.0 + z * (1.0 - sig)))).astype(bf16)
    weighted = (dy * widen(ec_ref[...], spread2)).astype(bf16)
    gain_wide = widen(g_ref[...], spread2)
    back_ref[...] = back_ref[...] * gain_wide[0:1, :] + dot(cm_ref[...], weighted, TN)
    keep_ref[...] = keep_ref[...] * gain_wide
    store_carry(c, carry_ref, back_ref, keep_ref)


def mamba_bpre(dg, z, full, mix, ec, g, spread2):
    rows = dg.shape[0]
    n = rows // SPAN
    rev = lambda width, col=0: pl.BlockSpec((SPAN, width), lambda c: (n - 1 - c, col))
    return pl.pallas_call(
        mamba_bpre_kernel,
        grid=(n,),
        in_specs=[rev(INNER), rev(INNER), rev(INNER), rev(NS, (INNER + NS) // NS), rev(LANE),
                  pl.BlockSpec((8, LANE), lambda c: (n - 1 - c, 0)), whole(spread2.shape)],
        out_specs=(rev(INNER), rev(INNER), whole((NS + 16, INNER))),
        out_shape=(sds((rows, INNER), bf16), sds((rows, INNER), bf16), sds((NS + 16, INNER), bf16)),
        scratch_shapes=[pltpu.VMEM((NS, INNER), f32), pltpu.VMEM((8, INNER), f32)],
        compiler_params=params(40),
        cost_estimate=COST,
        name="mamba_bpre",
    )(dg, z, full, mix, ec, g, spread2)


def mamba_bwd_kernel(mix_ref, dt_ref, cum_ref, cumt_ref, ec_ref, fw_ref, g_ref, segc_ref, segr_ref,
                     dy_ref, states_ref, u_ref, tap_ref, meta_ref, skip_ref, head_ref, spread_ref, gather_ref, *refs):
    carries = refs[:-9]
    dpre_ref, ddt_ref, conv_ref, small_ref, dstate_ref, acc_ref, rows_ref, dx_ref, dbc_ref = refs[-9:]
    step = pl.program_id(0)
    c = pl.num_programs(0) - 1 - step
    base = pl.multiple_of(c * SPAN, SPAN)

    @pl.when(step == 0)
    def _():
        dstate_ref[...] = load_carry(carries[0], carries[1:])
        conv_ref[...] = jnp.zeros_like(conv_ref)
        small_ref[...] = jnp.zeros_like(small_ref)
        rows_ref[...] = jnp.zeros_like(rows_ref)

    spread2 = spread_ref[...]
    gather2 = gather_ref[...]
    b = mix_ref[:, INNER : INNER + NS]
    cm = mix_ref[:, INNER + NS :]
    cum = cum_ref[...]
    dt = dt_ref[...]
    wide = widen(jnp.concatenate([dt, ec_ref[...], fw_ref[...], g_ref[...]], axis=0), spread2)
    dt_wide, ec_wide, fw_wide = wide[:SPAN], wide[SPAN : 2 * SPAN], wide[2 * SPAN : 3 * SPAN]
    gain = wide[3 * SPAN : 3 * SPAN + 1]
    s, t = tri_masks()
    allowed = (segc_ref[...] == segr_ref[...]) & (t >= s)
    off = jnp.where(allowed, 0.0, NEG)
    affinity = dot(b, cm, NT)
    acc_ref[...] = jnp.zeros_like(acc_ref)
    for p in range(MH // 2):
        lanes = slice(p * LANE, (p + 1) * LANE)
        x = mix_ref[:, lanes].astype(f32)
        scaled = (x * dt_wide[:, lanes]).astype(bf16)
        dy = dy_ref[:, lanes]
        dmix = dot(pair_halves(scaled), dy, NT)
        pieces = []
        total = None
        for q, h in enumerate((2 * p, 2 * p + 1)):
            gap = cumt_ref[h : h + 1, :] - cum[:, h : h + 1] + off
            decays = jnp.exp(gap)
            mixing = (affinity * decays).astype(bf16)
            pieces.append(mixing)
            dm = dmix[q * SPAN : (q + 1) * SPAN, :]
            rows_ref[h : h + 1, :] = jnp.sum(dm * mixing.astype(f32), axis=0, keepdims=True)
            part = dm * decays
            total = part if total is None else total + part
        acc_ref[...] += total
        dx_ref[:, lanes] = dot(jnp.concatenate(pieces, axis=1), pair_halves(dy))
    dscaled = dx_ref[...]
    x = mix_ref[:, :INNER].astype(f32)
    scaled = (x * dt_wide).astype(bf16).astype(f32)
    dy = dy_ref[...].astype(f32)
    dstate = dstate_ref[...]
    dstate_low = dstate.astype(bf16)
    state = states_ref[0]
    from_state = fw_wide * dot(b, dstate_low)
    carried = ec_wide * dot(cm, state)
    weighted_dy = (dy * ec_wide).astype(bf16)
    dxd = dscaled + from_state
    state_dot = jnp.sum(dstate * state.astype(f32), axis=0, keepdims=True) * gain
    sums = [split2(scaled * dscaled, axis=0)]
    sums += [v.astype(bf16) for v in (dy * carried, scaled * from_state, x * dxd, dy * x)]
    sums.append(split2(jnp.broadcast_to(state_dot, (16, INNER)), axis=0))
    sums = dot(jnp.concatenate(sums, axis=0), gather2[:INNER, :])
    cols_sum = sums[:SPAN] + sums[SPAN : 2 * SPAN]
    carr_sum, fdf_sum, ddt_direct, skip_part = [sums[n * SPAN : (n + 1) * SPAN] for n in range(2, 6)]
    state_dot = sums[6 * SPAN : 6 * SPAN + 1] + sums[6 * SPAN + 16 : 6 * SPAN + 17]
    tt, ss = tri_masks()
    suffix = (ss >= tt).astype(bf16)
    prefix = (ss < tt).astype(bf16)
    suffix2 = jnp.concatenate([suffix, suffix], axis=1)
    dlog = dot(suffix2, split2(carr_sum - cols_sum, axis=0))
    dlog = dlog + dot(suffix2, split2(rows_ref[...]), NT)
    dlog = dlog + dot(jnp.concatenate([prefix, prefix], axis=1), split2(fdf_sum, axis=0)) + state_dot
    decay_rate = head_ref[1:2, :]
    ddt = (ddt_direct + dlog * decay_rate) * (1.0 - jnp.exp(-dt))
    ddt_ref[...] = ddt.astype(bf16)
    small_ref[0:1, :] += jnp.sum(dlog * dt, axis=0, keepdims=True) * decay_rate
    small_ref[1:2, :] += jnp.sum(skip_part, axis=0, keepdims=True)
    small_ref[2:3, :] += jnp.sum(ddt, axis=0, keepdims=True)
    dx_ref[...] = dxd * dt_wide + skip_ref[0:1, :] * dy
    daff = acc_ref[...]
    daff_low = daff.astype(bf16)
    fx = (scaled * fw_wide).astype(bf16)
    dbc_ref[:, :NS] = dot(daff_low, cm) + dot(fx, dstate_low, NT)
    dbc_ref[:, NS:] = dot(daff_low, b, TN) + dot(weighted_dy, state, NT)
    dstate_ref[...] = dstate * gain + dot(cm, weighted_dy, TN)
    meta = meta_ref[...]
    for col in range(COLS):
        lanes = slice(col * LANE, (col + 1) * LANE)
        taps, total = conv_block(u_ref, tap_ref, meta, base, col)
        sig = jax.nn.sigmoid(total)
        if col * LANE < INNER:
            dmixed = dx_ref[:, lanes]
        else:
            dmixed = dbc_ref[:, col * LANE - INNER : (col + 1) * LANE - INNER]
        dpre = dmixed * (sig * (1.0 + total * (1.0 - sig)))
        dpre_ref[:, lanes] = dpre
        for j in range(KCONV):
            conv_ref[KCONV - 1 - j : KCONV - j, lanes] += jnp.sum(dpre * taps[j], axis=0, keepdims=True)
        conv_ref[KCONV : KCONV + 1, lanes] += jnp.sum(dpre, axis=0, keepdims=True)


def mamba_bwd(mix, dt, cum, cumt, ec, fw, g, segc, segr, dy, states, u, taps, meta, skip, heads, spread2, gather2,
              carries):
    rows = mix.shape[0]
    n = rows // SPAN
    width = mix.shape[1]
    rev = lambda w: pl.BlockSpec((SPAN, w), lambda c: (n - 1 - c, 0))
    return pl.pallas_call(
        mamba_bwd_kernel,
        grid=(n,),
        in_specs=[rev(width), rev(LANE), rev(LANE),
                  pl.BlockSpec((cumt.shape[0], SPAN), lambda c: (0, n - 1 - c)), rev(LANE), rev(LANE),
                  pl.BlockSpec((8, LANE), lambda c: (n - 1 - c, 0)), rev(1),
                  pl.BlockSpec((1, SPAN), lambda c: (0, n - 1 - c)), rev(INNER),
                  pl.BlockSpec((1, NS, INNER), lambda c: (n - 1 - c, 0, 0)), whole(u.shape), whole(taps.shape),
                  rev(8), whole(skip.shape), whole(heads.shape), whole(spread2.shape), whole(gather2.shape),
                  *wholes(carries)],
        out_specs=(rev(width), rev(LANE), whole((8, width)), whole((8, LANE))),
        out_shape=(sds((rows, width), f32), sds((rows, LANE), bf16), sds((8, width), f32), sds((8, LANE), f32)),
        scratch_shapes=[pltpu.VMEM((NS, INNER), f32), pltpu.VMEM((SPAN, SPAN), f32), pltpu.VMEM((LANE, SPAN), f32),
                        pltpu.VMEM((SPAN, INNER), f32), pltpu.VMEM((SPAN, 2 * NS), f32)],
        compiler_params=params(56),
        cost_estimate=COST,
        name="mamba_bwd",
    )(mix, dt, cum, cumt, ec, fw, g, segc, segr, dy, states, u, taps, meta, skip, heads, spread2, gather2, *carries)


NB = 8
LOW = (0, 2, 4, 6)
ORDERS = ((2, 4), (4, 2))
SETS = ((0, 1), (2, 3))
SET_MASKS = ((0, 2, 4, 6), (0, 4, 2, 6))


class Ring:
    def __init__(self, mesh):
        self.nd = mesh.shape["dp"]
        self.nt = mesh.shape["tensor"]
        self.unit = self.nd // NB
        base = range(0, self.nd, self.unit)
        self.groups = [[b + i for i in range(self.unit)] for b in base]

    def dp(self, value, mask):
        step = mask * self.unit
        return lax.ppermute(value, "dp", [(i, i ^ step) for i in range(self.nd)])

    def shift(self, value, s):
        n = self.nt
        return lax.ppermute(value, "tensor", [(i, (i + s) % n) for i in range(n)])

    def line(self, value, s):
        n = self.nt
        return lax.ppermute(value, "tensor", [(i, i + s) for i in range(n) if 0 <= i + s < n])

    def block(self, value):
        if self.unit == 1:
            return value
        return lax.all_gather(value, "dp", axis=0, tiled=True, axis_index_groups=self.groups)

    def unblock(self, value):
        if self.unit == 1:
            return value
        return lax.psum_scatter(value, "dp", scatter_dimension=0, tiled=True, axis_index_groups=self.groups)

    def gather(self, pack, hold=lambda stage, values: values):
        own = self.block(pack)
        (own,) = hold(0, [own])
        parts = [own] + [self.shift(own, s) for s in range(1, self.nt)]
        pairs = hold(1, [join([parts[s] for s in members]) for members in SETS])
        nears = [self.dp(pair, one) for pair, (one, _) in zip(pairs, ORDERS)]
        firsts = [
            join([parts[s] for s in members] + [near]) for members, near in zip(SETS, nears)
        ]
        firsts = hold(2, firsts)
        sides = [[first, self.dp(first, two)] for first, (_, two) in zip(firsts, ORDERS)]
        sides = [hold(3, side) for side in sides]
        return [[lows, [self.dp(low, 1) for low in lows]] for lows in sides]

    def scatter_sibling(self, sent, kept):
        came = self.dp(sent, 1)
        halves = []
        for n in range(2):
            here = slice(2 * n, 2 * n + 2)
            halves.append((add(kept[here, 2:], came[here, 2:]), add(kept[here, :2], came[here, :2])))
        return halves

    def scatter_first(self, halves):
        quarters = []
        for (out, mine), (_, axis) in zip(halves, ORDERS):
            got = self.dp(out, axis)
            quarters.append((add(mine[:, 1:], got[:, 1:]), add(mine[:, :1], got[:, :1])))
        return quarters

    def scatter_second(self, quarters):
        parts = []
        for (out, mine), (axis, _) in zip(quarters, ORDERS):
            got = self.dp(out, axis)
            parts += [add(mine[i, 0], got[i, 0]) for i in range(2)]
        return parts

    def total(self, parts):
        total = parts[0].astype(f32)
        for s in range(1, self.nt):
            total = total + self.shift(parts[s], self.nt - s).astype(f32)
        return total

    def collect(self, parts):
        return self.unblock(self.total(parts))

    def all_sum(self, value):
        bit = 1
        while bit < self.nd:
            value = value + lax.ppermute(value, "dp", [(i, i ^ bit) for i in range(self.nd)])
            bit *= 2
        return value + sum(self.shift(value, s) for s in range(1, self.nt))


def after(values, *others):
    return lax.optimization_barrier((tuple(values), others))[0]


def add(a, b):
    return (a.astype(f32) + b.astype(f32)).astype(bf16)


def join_kernel(*refs):
    out = refs[-1]
    if len(out.shape) == 3:
        for i, ref in enumerate(refs[:-1]):
            out[i] = ref[...]
    else:
        for i, ref in enumerate(refs[:2]):
            out[0, i] = ref[...]
        out[1] = refs[2][...]


def join(pieces):
    rows, cols = pieces[0].shape
    shape = (2, rows, cols) if len(pieces) == 2 else (2, 2, rows, cols)
    return pl.pallas_call(
        join_kernel,
        grid=(1,),
        out_shape=sds(shape, bf16),
        in_specs=wholes(pieces),
        out_specs=whole(shape),
        compiler_params=params(40),
        cost_estimate=COST,
        name="join",
    )(*pieces)


def block_rows(index_ref, at, rows):
    return pl.ds(pl.multiple_of(index_ref[at] * rows, rows), rows)


def part_columns(index_ref, s, width):
    return pl.ds(pl.multiple_of(index_ref[8 + s] * width, width), width)


def assemble_kernel(widths, index_ref, *refs):
    buffers, outs = refs[:8], refs[8:]
    rows = buffers[0].shape[2]
    for n in range(2):
        for half in range(2):
            for k in range(4):
                buffer = buffers[4 * n + 2 * half + k // 2]
                m = LOW.index(SET_MASKS[n][k])
                here = block_rows(index_ref, 4 * half + m, rows)
                for i in range(2):
                    at = 0
                    for width, out in zip(widths, outs):
                        piece = buffer[k % 2, i, :, at : at + width]
                        at += width
                        if out.shape[1] == width:
                            out[here, :] = piece if n + i == 0 else out[here, :] + piece
                        else:
                            out[here, part_columns(index_ref, 2 * n + i, width)] = piece


def assemble(index, sides, widths, totals):
    buffers = [buffer for side in sides for lows in side for buffer in lows]
    model = NB * buffers[0].shape[2]
    outs = tuple(sds((model, total), bf16) for total in totals)
    return pl.pallas_call(
        functools.partial(assemble_kernel, widths),
        grid=(1,),
        out_shape=outs,
        in_specs=[SMEM] + wholes(buffers),
        out_specs=tuple(wholes(outs)),
        compiler_params=params(48),
        cost_estimate=COST,
        name="assemble",
    )(index, *buffers)


def project_kernel(widths, index_ref, *refs):
    buffers, (normed_ref, halo_ref, cos_ref, sin_ref) = refs[:8], refs[8:12]
    weights, (u_ref, q_ref, kv_ref, dt_ref) = refs[12:16], refs[16:]
    assemble_kernel(widths, index_ref, *buffers, *weights)
    w_q, w_step, w_x, w_shared = weights
    kv_width = KVH * HD
    half = normed_ref.shape[0] // 2
    for r in range(2):
        here = slice(r * half, (r + 1) * half)
        normed = normed_ref[here, :]
        cosine, sine = cos_ref[here, :], sin_ref[here, :]
        kv = dot(normed, w_shared[:, : 2 * kv_width])
        kv_ref[here, :kv_width] = turn(kv[:, :kv_width], cosine, sine).astype(bf16)
        kv_ref[here, kv_width:] = kv[:, kv_width:].astype(bf16)
        q = dot(normed, w_q[...])
        for c in range(0, q.shape[1], LANE):
            tile = turn(q[:, c : c + LANE], cosine, sine).astype(bf16)
            q_ref[here, c : c + LANE] = tile * jnp.asarray(HD ** -0.5, bf16)
        dt_ref[here, :] = dot(normed, w_step[...])
        below = slice(HALO + r * half, HALO + (r + 1) * half)
        u_ref[below, INNER:] = dot(normed, w_shared[:, 2 * kv_width :])
        for c in range(0, INNER, 512):
            u_ref[below, c : c + 512] = dot(normed, w_x[:, c : c + 512])
    u_ref[:HALO, INNER:] = dot(halo_ref[...], w_shared[:, 2 * kv_width :])
    for c in range(0, INNER, 512):
        u_ref[:HALO, c : c + 512] = dot(halo_ref[...], w_x[:, c : c + 512])


def project(index, sides, widths, totals, normed, halo, cosine, sine):
    buffers = [buffer for side in sides for lows in side for buffer in lows]
    rows, model = normed.shape
    arrays = (*buffers, normed, halo, cosine, sine)
    outs = tuple(sds((model, total), bf16) for total in totals)
    outs += (sds((HALO + rows, INNER + 2 * NS), f32), sds((rows, QH * HD), bf16), sds((rows, 2 * KVH * HD), bf16),
             sds((rows, LANE), f32))
    return pl.pallas_call(
        functools.partial(project_kernel, widths),
        grid=(1,),
        out_shape=outs,
        in_specs=[SMEM] + wholes(arrays),
        out_specs=tuple(wholes(outs)),
        compiler_params=params(56),
        cost_estimate=COST,
        name="project",
    )(index, *arrays)


def transpose_into(out_ref, values):
    for c in range(0, values.shape[1], LANE):
        out_ref[c : c + LANE, :] = values[:, c : c + LANE].astype(f32).T.astype(bf16)


def norm_kernel(h_ref, c_ref, gain_ref, n_ref, nt_ref, ct_ref, scale_ref):
    values = h_ref[...].astype(f32)
    scale = lax.rsqrt(jnp.mean(values * values, axis=-1, keepdims=True) + epsilon)
    scale_ref[...] = scale
    n_ref[...] = (values * scale * gain_ref[...]).astype(bf16)
    transpose_into(nt_ref, n_ref[...])
    transpose_into(ct_ref, c_ref[...])


def pack_kernel(flips, *refs):
    out, at = refs[-1], 0
    for flip, ref in zip(flips, refs[:-1]):
        if flip:
            count = ref.shape[0]
            for r in range(0, count, LANE):
                out[:, at + r : at + r + LANE] = ref[r : r + LANE, :].astype(f32).T.astype(bf16)
        else:
            count = ref.shape[1]
            out[:, at : at + count] = ref[...]
        at += count


def pack(arrays, flips):
    rows = arrays[0].shape[0]
    columns = sum(a.shape[0] if flip else a.shape[1] for a, flip in zip(arrays, flips))
    return simple_call(functools.partial(pack_kernel, flips), "pack", tuple(arrays), sds((rows, columns), bf16))


def middle_kernel(att_ref, gated_ref, wa_ref, wm_ref, h_ref, gain_ref, res_ref, n_ref, nt_ref, scale_ref):
    model = h_ref.shape[1]
    for c in range(0, model, 256):
        cols = slice(c, c + 256)
        mixer = dot(att_ref[...], wa_ref[cols, :], NT) + dot(gated_ref[...], wm_ref[cols, :], NT)
        res_ref[:, cols] = h_ref[:, cols].astype(f32) + mixer
    values = res_ref[...]
    scale = lax.rsqrt(jnp.mean(values * values, axis=-1, keepdims=True) + epsilon)
    scale_ref[...] = scale
    n_ref[...] = (values * scale * gain_ref[...]).astype(bf16)
    transpose_into(nt_ref, n_ref[...])


def after_ffn_kernel(dn_ref, res_ref, scale_ref, gain_ref, c_ref, wa_ref, wm_ref,
                     dres_ref, dmt_ref, dg_ref, da_ref, gain_grad_ref):
    dn, values, scale = dn_ref[...], res_ref[...], scale_ref[...]
    weighted = dn * gain_ref[...]
    inner = jnp.mean(weighted * values, axis=-1, keepdims=True)
    gain_grad_ref[...] = jnp.broadcast_to(jnp.sum(dn * values * scale, axis=0, keepdims=True), gain_grad_ref.shape)
    dres = c_ref[...].astype(f32) + scale * weighted - values * (scale * scale * scale * inner)
    dres_ref[...] = dres
    low = dres.astype(bf16)
    transpose_into(dmt_ref, low)
    da_ref[...] = dot(low, wa_ref[...]).astype(bf16)
    for c in range(0, wm_ref.shape[1], 512):
        dg_ref[:, c : c + 512] = dot(low, wm_ref[:, c : c + 512]).astype(bf16)


def conv_back_kernel(dpre_ref, after_ref, tap_ref, keep_ref, dkv_ref, dx_ref, dshared_ref):
    rows = dpre_ref.shape[0]
    kv = dkv_ref.shape[1]
    dshared_ref[:, :kv] = dkv_ref[...]
    for c in range(0, rows, SPAN):
        keep = keep_ref[c : c + SPAN, :]
        for col in range(COLS):
            lanes = slice(col * LANE, (col + 1) * LANE)
            if c + SPAN < rows:
                window = dpre_ref[c : c + SPAN + 8, lanes]
            else:
                window = jnp.concatenate([dpre_ref[c : c + SPAN, lanes], after_ref[:, lanes]], axis=0)
            total = tap_ref[KCONV - 1 : KCONV, lanes] * window[:SPAN, :]
            for j in range(1, KCONV):
                total = total + tap_ref[KCONV - 1 - j : KCONV - j, lanes] * window[j : j + SPAN, :] * keep[:, j : j + 1]
            if col * LANE < INNER:
                dx_ref[c : c + SPAN, lanes] = total.astype(bf16)
            else:
                at = kv + col * LANE - INNER
                dshared_ref[c : c + SPAN, at : at + LANE] = total.astype(bf16)


def kv_back_kernel(cos_ref, sin_ref, own_ref, *refs):
    out_ref = refs[-1]
    total = own_ref[...]
    for ref in refs[:-1]:
        total = total + ref[...].astype(f32)
    kv_width = KVH * HD
    out_ref[:, :kv_width] = turn(total[:, :kv_width], cos_ref[...], -sin_ref[...]).astype(bf16)
    out_ref[:, kv_width:] = total[:, kv_width:].astype(bf16)


def simple_call(kernel, name, arrays, outs, flops=0):
    single = not isinstance(outs, tuple)
    shapes = (outs,) if single else outs
    size = sum(a.size * a.dtype.itemsize for a in arrays) + sum(a.size * a.dtype.itemsize for a in shapes)
    return pl.pallas_call(
        kernel,
        grid=(1,),
        out_shape=outs,
        in_specs=wholes(arrays),
        out_specs=whole(outs.shape) if single else tuple(wholes(outs)),
        compiler_params=params(56),
        cost_estimate=COST,
        name=name,
    )(*arrays)


def left_rows(index_ref, left_ref, half, side):
    rows = left_ref.shape[0] // NB
    order = [0, 1 + side, 2 - side, 3]
    return jnp.concatenate([left_ref[block_rows(index_ref, 4 * half + m, rows), :] for m in order], axis=0)


def grad_kernel(plan, n_left, n_right, index_ref, *refs):
    lefts = refs[:n_left]
    rights = refs[n_left : n_left + n_right]
    sent_ref, kept_ref = refs[n_left + n_right :]
    s = pl.program_id(0)
    for half, out in ((1, sent_ref), (0, kept_ref)):
        cache = {}
        at = 0
        for left, right, width, kind in plan:
            if kind == "fixed":
                value = rights[right][:, pl.ds(pl.multiple_of(s * width, width), width)]
            elif kind == "all":
                value = rights[right][...]
            else:
                value = rights[right][:, part_columns(index_ref, s, width)]
            if left not in cache:
                cache[left] = left_rows(index_ref, lefts[left], half, s // 2)
            result = dot(cache[left], value)
            out[0, :, :, at : at + width] = result.reshape(4, -1, width).astype(bf16)
            at += width


def weight_grads(index, lefts, rights, plan):
    rows = lefts[0].shape[0] // NB
    columns = sum(width for _, _, width, _ in plan)
    outs = (sds((4, 4, rows, columns), bf16),) * 2
    return pl.pallas_call(
        functools.partial(grad_kernel, plan, len(lefts), len(rights)),
        grid=(4,),
        out_shape=outs,
        in_specs=[SMEM] + wholes(lefts) + wholes(rights),
        out_specs=(pl.BlockSpec((1, 4, rows, columns), lambda s: (s, 0, 0, 0)),) * 2,
        compiler_params=params(56),
        cost_estimate=COST,
        name="weight_grads",
    )(index, *lefts, *rights)


def ffn_kernel(index_ref, w_ref, n_ref, nt_ref, c_ref, ct_ref, res_ref, grad_ref, out_ref, dn_ref, acc_ref):
    s = pl.program_id(0)
    model = n_ref.shape[1]
    units = w_ref.shape[3] // 3

    def weight(k):
        return w_ref[:, 0, :, k * units : (k + 1) * units].reshape(model, units)

    @pl.when(s == 0)
    def _():
        acc_ref[...] = res_ref[...]
        dn_ref[...] = jnp.zeros_like(dn_ref)

    gate = dot(n_ref[...], weight(0))
    up = dot(n_ref[...], weight(1))
    dact = dot(c_ref[...], weight(2)).astype(bf16).astype(f32)
    sig = jax.nn.sigmoid(gate)
    silu = gate * sig
    act = (silu * up).astype(bf16)
    dgate = (dact * up * (sig * (1.0 + gate * (1.0 - sig)))).astype(bf16)
    dup = (dact * silu).astype(bf16)
    acc_ref[...] += dot(act, weight(2), NT)
    dn_ref[...] += dot(dgate, weight(0), NT) + dot(dup, weight(1), NT)
    grad_ref[:, :units] = dot(nt_ref[...], dgate).astype(bf16)
    grad_ref[:, units : 2 * units] = dot(nt_ref[...], dup).astype(bf16)
    grad_ref[:, 2 * units :] = dot(ct_ref[...], act).astype(bf16)

    @pl.when(s == pl.num_programs(0) - 1)
    def _():
        out_ref[...] = acc_ref[...].astype(bf16)


def ffn(index, weights, normed, normed_t, cot, cot_t, residual):
    nd, nt, rows, columns = weights.shape
    tokens, model = normed.shape
    arrays = (normed, normed_t, cot, cot_t, residual)
    return pl.pallas_call(
        ffn_kernel,
        grid_spec=pltpu.PrefetchScalarGridSpec(
            num_scalar_prefetch=1,
            grid=(nt,),
            in_specs=[pl.BlockSpec((nd, 1, rows, columns), lambda s, index: (0, index[8 + s], 0, 0))] + wholes(arrays),
            out_specs=(
                pl.BlockSpec((model, columns), lambda s, index: (0, index[8 + s])),
                whole((tokens, model)),
                whole((tokens, model)),
            ),
            scratch_shapes=[pltpu.VMEM((tokens, model), f32)],
        ),
        out_shape=(sds((model, nt * columns), bf16), sds((tokens, model), bf16), sds((tokens, model), f32)),
        compiler_params=params(60),
        cost_estimate=COST,
        name="ffn",
    )(index, weights, *arrays)


def rms_back(d_normed, values, scale, gain):
    weighted = d_normed * gain
    inner = jnp.mean(weighted * values, axis=-1, keepdims=True)
    gain_grad = jnp.sum(d_normed * values * scale, axis=0)
    return scale * weighted - values * (scale * scale * scale * inner), gain_grad


def rope_tables(rows, start):
    half = HD // 2
    frequency = rope_base ** (-2.0 * jnp.arange(half, dtype=f32) / HD)
    angles = (start + jnp.arange(rows)).astype(f32)[:, None] * frequency[None, :]
    cosine, sine = jnp.cos(angles), jnp.sin(angles)
    return jnp.concatenate([cosine] * 4, axis=1), jnp.concatenate([-sine, sine] * 2, axis=1)


def per_device(
    mesh,
    hidden,
    segments,
    cotangent,
    norm_gain,
    ffn_gain,
    query_proj,
    key_proj,
    value_proj,
    attn_out_proj,
    gate_inner,
    input_inner,
    state_proj,
    step_proj,
    mamba_out,
    conv_weight,
    conv_bias,
    decay_log,
    skip_gain,
    step_bias,
    ffn_gate,
    ffn_up,
    ffn_down,
):
    ring = Ring(mesh)
    nt = ring.nt
    di, ti = lax.axis_index("dp"), lax.axis_index("tensor")
    rows, width = hidden.shape
    seq = segments.shape[1]
    hops = -(-(seq // 2 - 1) // rows)
    back = hops * rows
    segment = segments[0]
    kv_width = KVH * HD
    step_cols = step_proj.shape[1]

    block = di // ring.unit
    index = jnp.stack(
        [block ^ m for m in LOW] + [block ^ m ^ 1 for m in LOW] + [lax.rem(ti + nt - s, nt) for s in range(nt)]
    ).astype(jnp.int32)

    start = ti * rows
    normed, normed_t, cot_t, scale1 = simple_call(
        norm_kernel,
        "norm_in",
        (hidden, cotangent, norm_gain[None, :]),
        (sds((rows, width), bf16), sds((width, rows), bf16), sds((width, rows), bf16), sds((rows, 1), f32)),
    )
    halo = ring.line(normed[rows - HALO :], 1)
    cosine, sine = rope_tables(rows, start)

    step_wide = jnp.zeros((step_proj.shape[0], LANE), bf16)
    step_wide = lax.dynamic_update_slice(step_wide, step_proj, (0, ti * step_cols))
    shared = jnp.concatenate([key_proj, value_proj, state_proj], axis=1)
    quarter = shared.shape[1] // nt
    shared_part = lax.dynamic_slice_in_dim(shared, ti * quarter, quarter, 1)
    widths1 = (query_proj.shape[1], LANE, input_inner.shape[1], quarter)
    widths2 = (gate_inner.shape[1], attn_out_proj.shape[0], mamba_out.shape[0])
    stages = {}

    def note(stage, values):
        if stage == 1:
            values = after(values, normed)
        if stage == 3:
            values = after(values, halo)
        stages[stage] = stages.get(stage, []) + list(values)
        return values

    pack1 = pack((query_proj, step_wide, input_inner, shared_part), (False,) * 4)
    sides1 = ring.gather(pack1, note)
    pack2 = pack((gate_inner, attn_out_proj, mamba_out), (False, True, True))
    ffn_pack = pack((ffn_gate, ffn_up, ffn_down), (False, False, True))
    (ffn_pack,) = after([ffn_pack], *stages[FFN_AFTER]) if FFN_AFTER else [ffn_pack]
    w_ffn = lax.all_gather(ffn_pack, ("dp", "tensor"), axis=0, tiled=True)
    w_ffn = w_ffn.reshape(ring.nd, nt, *ffn_pack.shape)
    w_q, w_step, w_x, w_shared, u, query8, kv_own, dt_raw = project(
        index, sides1, widths1, (widths1[0] * nt, LANE, widths1[2] * nt, quarter * nt), normed, halo, cosine, sine
    )
    padded = jnp.concatenate([jnp.full((back,), -1, jnp.int32), segment])
    seg_keys = lax.dynamic_slice_in_dim(padded, start, back + rows)
    seg_own = seg_keys[back:]
    seg_col, seg_row = seg_own[:, None], seg_own[None, :]
    chunks = rows // SPAN
    grouped = seg_own.reshape(chunks, SPAN)
    before = jnp.concatenate([seg_keys[back - 1 : back], grouped[:-1, -1]])
    carry_in = (grouped == before[:, None]).astype(f32).reshape(rows)
    in_last = (grouped == grouped[:, -1:]).astype(f32).reshape(rows)
    keeps = [(seg_keys[back - j : back - j + rows] == seg_own).astype(f32) for j in range(KCONV)]
    zero = jnp.zeros((rows,), f32)
    meta = jnp.stack(keeps + [carry_in, in_last, zero, zero], axis=1)
    first_tokens = seg_own.reshape(rows // QB, QB)[:, 0]
    doc_start = jnp.sum((segment[None, :] < first_tokens[:, None]).astype(jnp.int32), axis=1)
    first_block = (jnp.maximum(doc_start - (start - back), 0) // KB).astype(jnp.int32)

    seg_after = jnp.concatenate([segment, jnp.full((KCONV,), -2, jnp.int32)])
    keeps_after = [(lax.dynamic_slice_in_dim(seg_after, start + j, rows) == seg_own).astype(f32) for j in range(KCONV)]
    keeps_after = jnp.stack(keeps_after + [zero] * 4, axis=1)
    kvs = [ring.line(kv_own, s) for s in range(hops, 0, -1)] + [kv_own]

    waits = {0: (stages[1],), 1: (kv_own,)}

    def hold(stage, values):
        return after(values, *waits[stage])

    (own2,) = hold(0, [ring.block(pack2)])
    parts2 = [own2] + [ring.shift(own2, s) for s in range(1, nt)]
    pairs2 = hold(1, [join([parts2[s] for s in members]) for members in SETS])
    nears2 = [ring.dp(pair, one) for pair, (one, _) in zip(pairs2, ORDERS)]
    (u,) = after([u], pairs2)
    taps = jnp.concatenate([conv_weight, conv_bias[None, :], jnp.zeros((3, INNER + 2 * NS), f32)], axis=0)
    rate = -jnp.exp(decay_log)
    heads = jnp.pad(jnp.stack([step_bias, rate]), ((0, 6), (0, LANE - MH)))
    skip = jnp.broadcast_to(jnp.repeat(skip_gain, MP)[None, :], (8, INNER))
    spread = np.arange(LANE)[:, None] == np.arange(INNER)[None, :] // MP
    spread2 = jnp.asarray(np.concatenate([spread, spread], axis=0), bf16)
    gather2 = jnp.asarray(np.concatenate([spread.T, spread.T], axis=0), bf16)

    mix, dt, cum, cumt, ec, fw, g, final = mamba_pre(u, taps, meta, dt_raw, heads, spread2)
    firsts2 = after([join([parts2[s] for s in members] + [near]) for members, near in zip(SETS, nears2)], mix, kvs)
    sides2 = [[first, ring.dp(first, two)] for first, (_, two) in zip(firsts2, ORDERS)]
    (query8,) = after([query8], *firsts2)
    carries = [ring.line(final, s) for s in range(1, hops + 1)]
    attended, lse = attn_fwd(first_block, query8, seg_row, seg_keys[:, None], kvs)
    waits[3] = (attended, carries)
    sides2 = [[lows, [ring.dp(low, 1) for low in lows]] for lows in [hold(3, side) for side in sides2]]
    w_z, w_ao, w_mo = assemble(index, sides2, widths2, tuple(w * nt for w in widths2))
    z_gate = dot(normed, w_z)
    gated, full, states = mamba_fwd(
        mix, dt, cum, cumt, ec, fw, g, seg_col, seg_row, z_gate, skip, spread2, carries
    )
    residual, normed2, normed2_t, scale2 = simple_call(
        middle_kernel,
        "middle",
        (attended, gated, w_ao, w_mo, hidden, ffn_gain[None, :]),
        (sds((rows, width), f32), sds((rows, width), bf16), sds((width, rows), bf16), sds((rows, 1), f32)),
        2 * rows * width * (INNER + QH * HD),
    )

    ffn_grads, output, d_normed2 = ffn(index, w_ffn, normed2, normed2_t, cotangent, cot_t, residual)
    ffn_grads = lax.psum_scatter(ffn_grads, "dp", scatter_dimension=0, tiled=True)
    units = ffn_gate.shape[1]
    g_ffn = lax.psum_scatter(ffn_grads, "tensor", scatter_dimension=1, tiled=True).astype(f32)
    d_residual, d_mixer_t, d_gated, d_attended, ffn_gain_grad = simple_call(
        after_ffn_kernel,
        "after_ffn",
        (d_normed2, residual, scale2, ffn_gain[None, :], cotangent, w_ao, w_mo),
        (sds((rows, width), f32), sds((width, rows), bf16), sds((rows, INNER), bf16), sds((rows, QH * HD), bf16),
         sds((8, width), f32)),
        2 * rows * width * (INNER + QH * HD),
    )
    ffn_gain_grad = ffn_gain_grad[0]

    dy, d_z, back_state = mamba_bpre(d_gated, z_gate, full, mix, ec, g, spread2)
    d_carries = [ring.line(back_state, -s) for s in range(1, hops + 1)]
    d_q, *d_kvs = attn_bwd(
        first_block, query8, d_attended, attended, lse, seg_row, seg_keys[:, None], cosine, sine, kvs
    )
    came = [ring.line(d_kvs[hops - s], -s) for s in range(1, hops + 1)]
    def kv_back(own):
        return simple_call(kv_back_kernel, "kv_back", (cosine, sine, own, *came), sds(kv_own.shape, bf16))


    plan2 = (
        (0, 0, widths2[1], "part"),
        (0, 1, widths2[2], "part"),
        (1, 2, widths2[0], "part"),
        (1, 3, widths1[0], "part"),
    )
    (d_q2,) = after([d_q], *d_carries)
    sent2, kept2 = weight_grads(index, (d_mixer_t, normed_t), (attended, gated, d_z, d_q2), plan2)
    (dy,) = after([dy], sent2)

    d_pre, d_step, conv_grads, small = mamba_bwd(
        mix, dt, cum, cumt, ec, fw, g, seg_col, seg_row, dy, states, u, taps, meta, skip, heads, spread2, gather2, d_carries
    )
    kept2, own_kv = after([kept2, d_kvs[-1]], d_pre)
    d_kv = kv_back(own_kv)
    halves2 = ring.scatter_sibling(sent2, kept2)
    d_after = ring.line(d_pre[:8], -1)
    d_x, d_shared = simple_call(
        conv_back_kernel,
        "conv_back",
        (d_pre, d_after, *after([taps], halves2, ffn_grads), keeps_after, d_kv),
        (sds((rows, INNER), bf16), sds((rows, quarter * nt), bf16)),
    )

    plan1 = ((0, 0, widths1[2], "part"), (0, 1, LANE, "all"), (0, 2, quarter, "fixed"))
    quarters2 = ring.scatter_first([(out, after([mine], d_x)[0]) for out, mine in halves2])
    (d_shared,) = after([d_shared], quarters2)
    sent1, kept1 = weight_grads(index, (normed_t,), (d_x, d_step, d_shared), plan1)
    halves1 = ring.scatter_sibling(sent1, kept1)
    parts2 = ring.scatter_second([(out, after([mine], halves1)[0]) for out, mine in quarters2])
    quarters1 = ring.scatter_first([(out, after([mine], parts2)[0]) for out, mine in halves1])
    grads2 = ring.collect(after(parts2[:1], quarters1) + tuple(parts2[1:]))
    parts = ring.scatter_second(quarters1)
    common = widths1[2] + LANE
    shared_sum = jnp.concatenate([part[:, common:] for part in parts], axis=1)
    shared_sum = ring.unblock(shared_sum)
    piece = shared_sum.shape[0] // nt
    parts = [part[:, :common] for part in parts]
    rows_of = []
    for s in range(nt):
        mine = lax.dynamic_slice_in_dim(shared_sum, lax.rem(ti + nt - s, nt) * piece, piece, 0)
        rows_of.append(jnp.concatenate([mine[:, i * quarter : (i + 1) * quarter] for i in range(nt)], axis=0))
    if ring.unit == 1:
        total = ring.total([jnp.concatenate(both, axis=1) for both in zip(parts, rows_of)])
        grads1, g_shared = total[:, :common], total[:, common:]
    else:
        grads1, g_shared = ring.collect(parts), ring.total(rows_of)
    g_shared = jnp.concatenate([g_shared[i * piece : (i + 1) * piece] for i in range(nt)], axis=1)

    d_q, d_x, d_z = after([d_q, d_x, d_z], halves1)
    d_normed = (
        dot(d_q, w_q, NT) + dot(d_z, w_z, NT) + dot(d_x, w_x, NT) + dot(d_shared, w_shared, NT) + dot(d_step, w_step, NT)
    )
    d_hid_norm, norm_gain_grad = rms_back(d_normed, hidden.astype(f32), scale1, norm_gain[None, :])
    hidden_grad = d_residual + d_hid_norm

    pieces = [norm_gain_grad, ffn_gain_grad, conv_grads[: KCONV + 1].reshape(-1), small[:3, :MH].reshape(-1)]
    vector = jnp.concatenate(pieces)
    size = vector.shape[0]
    vector = jnp.pad(vector, (0, -size % 1024)).reshape(-1, LANE)
    vector = ring.all_sum(vector).reshape(-1)
    at = 2 * width
    conv_sum = vector[at : at + (KCONV + 1) * (INNER + 2 * NS)].reshape(KCONV + 1, INNER + 2 * NS)
    small_sum = vector[size - 3 * MH : size].reshape(3, MH)

    def cut(value, *sizes):
        outs, at = [], 0
        for size in sizes:
            outs.append(value[:, at : at + size])
            at += size
        return outs

    g_fg, g_fu, g_fd = cut(g_ffn, units, units, units)
    g_ao, g_mo, g_z, g_q = cut(grads2, widths2[1], widths2[2], widths2[0], widths1[0])
    g_x, g_step_wide = cut(grads1, widths1[2], LANE)
    g_step = lax.dynamic_slice_in_dim(g_step_wide, ti * step_cols, step_cols, 1)
    return (
        output,
        hidden_grad,
        vector[:width],
        vector[width : 2 * width],
        g_q,
        g_shared[:, :kv_width],
        g_shared[:, kv_width : 2 * kv_width],
        g_ao.T,
        g_z,
        g_x,
        g_shared[:, 2 * kv_width :],
        g_step,
        g_mo.T,
        conv_sum[:KCONV],
        conv_sum[KCONV],
        small_sum[0],
        small_sum[1],
        small_sum[2],
        g_fg,
        g_fu,
        g_fd.T,
    )


def solution(mesh):
    in_specs = (
        P(("dp", "tensor"), None),
        P("dp", None),
        P(("dp", "tensor"), None),
        P(),
        P(),
        P("dp", "tensor"),
        P("dp", None),
        P("dp", None),
        P("tensor", "dp"),
        P("dp", "tensor"),
        P("dp", "tensor"),
        P("dp", None),
        P("dp", "tensor"),
        P("tensor", "dp"),
        P(),
        P(),
        P(),
        P(),
        P(),
        P("dp", "tensor"),
        P("dp", "tensor"),
        P("tensor", "dp"),
    )
    out_specs = (
        P(("dp", "tensor"), None),
        P(("dp", "tensor"), None),
        P(),
        P(),
        P("dp", "tensor"),
        P(("dp", "tensor"), None),
        P(("dp", "tensor"), None),
        P("tensor", "dp"),
        P("dp", "tensor"),
        P("dp", "tensor"),
        P(("dp", "tensor"), None),
        P("dp", "tensor"),
        P("tensor", "dp"),
        P(),
        P(),
        P(),
        P(),
        P(),
        P("dp", "tensor"),
        P("dp", "tensor"),
        P("tensor", "dp"),
    )
    return jax.shard_map(
        functools.partial(per_device, mesh), mesh=mesh, in_specs=in_specs, out_specs=out_specs, check_vma=False
    )
```
